32 devices in a mesh: scene: 16 (over z, y, core), tile: 2 (over x).
Axes of the slice: x: 2, y: 2, z: 4, core: 2. Of those that a mesh axis runs over, the one named last changes fastest.
Arguments:
- features_in: bfloat16 [16, 4, 64, 4096], P('scene', 'tile'), may hold values from -6 to 6
- strided_weights: bfloat16 [2, 64, 1024], replicated, may hold values from -0.1875 to 0.1875
- dilated_weights: bfloat16 [2, 64, 576], replicated, may hold values from -0.25 to 0.25
- tile_bias: float32 [32, 64], replicated, may hold values from -3 to 3
- cost_cotangent: bfloat16 [16, 4, 1024], P('scene', 'tile'), may hold values from -6 to 6
- footprint_pairing: int32 [8, 4], replicated, may hold values from 0 to 3, each once within a row
- valid_counts: int32 [8], replicated, may hold values from 1 to 4, as said below
- tile_owner: int32 [16], replicated, may hold values from 0 to 31, as said below
Outputs:
- grad_features: bfloat16 [16, 4, 64, 4096], P('scene', 'tile')
- grad_weights: float32 [128, 1600], P('scene')
- grad_bias: float32 [32, 64], P(('scene', 'tile'))
The draws below stay inside these ranges and needn't reach their ends.
Inputs may be any that keep to these rules, and one draw needn't show every extreme that they name: `footprint_pairing`: row k maps each patch of scene 2k to the patch of scene 2k + 1 that covers its footprint; each row is a permutation. `valid_counts`: patches 0 to count - 1 of both scenes of a pair are live; some pair has all 4 live. `tile_owner`: several scenes may share a tile, and many tiles have no scene.
All inputs are finite; a program needn't handle non-finite values.
Results may differ from the reference program's by a relative error of at most 0.007.
Values may be sent and summed in bfloat16 or wider, within the bound.
No kernel may reach another device: no remote copies, remote signals or barrier semaphores. Data moves between devices by JAX's collectives and lax.ppermute only.
A program may use at most 64 MiB of HBM per device.

```python
import math
import jax
import jax.numpy as jnp
from jax import lax

CH = 64
GRID = 64
CELLS_IN = 4096
CELLS = 1024
PATCH_SCENE = 4
SCENES = 16
PAIRS = 8
TILES = 32


def draw_valid_counts(key, part):
    first_key, second_key = jax.random.split(key)
    counts = jax.random.randint(first_key, (PAIRS,), 1, PATCH_SCENE + 1, dtype=jnp.int32)
    full_pair = jax.random.randint(second_key, (), 0, PAIRS, dtype=jnp.int32)
    return jnp.where(jnp.arange(PAIRS, dtype=jnp.int32) == full_pair, PATCH_SCENE, counts).astype(jnp.int32)


def draw_tile_owner(key, part):
    owner_key = jax.random.fold_in(key, 7)
    offset_key, bit_key, free_key = jax.random.split(owner_key, 3)
    group = TILES // SCENES
    scene_ids = jnp.arange(SCENES, dtype=jnp.int32)
    offset = jax.random.randint(offset_key, (), 0, 4, dtype=jnp.int32)
    category = (scene_ids + offset) % 4
    own_tile = scene_ids * group
    before_tile = (scene_ids - 1 + SCENES) % SCENES * group + group - 1
    far_bits = jax.random.randint(bit_key, (SCENES,), 0, group, dtype=jnp.int32)
    far_tile = (scene_ids + SCENES // 2) % SCENES * group + far_bits
    free_tile = jax.random.randint(free_key, (SCENES,), 0, TILES, dtype=jnp.int32)
    chosen = jnp.where(category == 0, own_tile, jnp.where(category == 1, before_tile, jnp.where(category == 2, far_tile, free_tile)))
    return chosen.astype(jnp.int32)


def shard_levels(stream_key, extent, cuts, smallest, high):
    def one(dim, blocks):
        draws = jax.random.uniform(jax.random.fold_in(jax.random.fold_in(stream_key, 6), dim), (blocks,), jnp.float32, smallest / len(cuts), high / len(cuts))
        return jnp.repeat(jnp.exp(draws), extent[dim] // blocks).reshape((-1,) + (1,) * (len(extent) - dim - 1))

    loudness = one(*cuts[0])
    for cut in cuts[1:]:
        loudness = loudness * one(*cut)
    return loudness


def centred(stream_key, dims, scale, limit, pieces=(), kind=jnp.bfloat16):
    values = jax.random.normal(stream_key, dims, jnp.float32) * scale
    if len(pieces) > 0:
        values = shard_levels(stream_key, dims, pieces, -0.22, 0.18) * values
    return jnp.clip(values, min=-limit, max=limit).astype(kind)


def setup_inputs(seed: int = 0) -> dict:
    key_of = jax.random.split(jax.random.key(seed), 9)
    return {
        "features_in": centred(key_of[0], (SCENES, PATCH_SCENE, CH, CELLS_IN), 1.0, 6.0, ((0, 16), (1, 2))),
        "strided_weights": centred(key_of[1], (2, CH, 16 * CH), (16 * CH) ** -0.5, 0.1875),
        "dilated_weights": centred(key_of[2], (2, CH, 9 * CH), (9 * CH) ** -0.5, 0.25),
        "tile_bias": centred(key_of[3], (TILES, CH), 0.5, 3.0, (), jnp.float32),
        "cost_cotangent": centred(key_of[4], (SCENES, PATCH_SCENE, CELLS), 1.0, 6.0, ((0, 16), (1, 2))),
        "footprint_pairing": jax.vmap(lambda own: jax.random.permutation(own, PATCH_SCENE))(jax.random.split(key_of[5], PAIRS)).reshape((PAIRS, PATCH_SCENE)).astype(jnp.int32),
        "valid_counts": draw_valid_counts(jax.random.fold_in(key_of[8], 71), 0),
        "tile_owner": draw_tile_owner(jax.random.fold_in(key_of[8], 71), 0),
    }


def strided_taps(feature_grid):
    patches, channels, grid_side = (feature_grid.shape[0], feature_grid.shape[1], feature_grid.shape[2])
    half_side = grid_side // 2
    padded = jnp.pad(feature_grid, ((0, 0), (0, 0), (1, 1), (1, 1)))
    folded = padded.reshape(patches, channels, half_side + 1, 2, half_side + 1, 2)
    tap_list = []
    for row_tap in range(4):
        for col_tap in range(4):
            row_shift, col_shift = (row_tap // 2, col_tap // 2)
            tap_piece = folded[:, :, row_shift:row_shift + half_side, row_tap % 2, col_shift:col_shift + half_side, col_tap % 2]
            tap_list.append(tap_piece.reshape(patches, channels, half_side * half_side))
    return tap_list

def strided_untaps(tap_parts, grid_side):
    patches, channels = (tap_parts[0].shape[0], tap_parts[0].shape[1])
    half_side = grid_side // 2
    tap_sums = [[jnp.zeros((patches, channels, half_side + 1, half_side + 1), jnp.float32) for col_phase in range(2)] for row_phase in range(2)]
    for row_tap in range(4):
        for col_tap in range(4):
            tap_piece = tap_parts[row_tap * 4 + col_tap].reshape(patches, channels, half_side, half_side)
            row_shift, col_shift = (row_tap // 2, col_tap // 2)
            placed = jnp.pad(tap_piece, ((0, 0), (0, 0), (row_shift, 1 - row_shift), (col_shift, 1 - col_shift)))
            tap_sums[row_tap % 2][col_tap % 2] = tap_sums[row_tap % 2][col_tap % 2] + placed
    row_stack = [jnp.stack([tap_sums[row_phase][0], tap_sums[row_phase][1]], axis=-1) for row_phase in range(2)]
    folded = jnp.stack(row_stack, axis=3)
    padded = folded.reshape(patches, channels, grid_side + 2, grid_side + 2)
    return padded[:, :, 1:grid_side + 1, 1:grid_side + 1]

def dilated_taps(feature_grid):
    patches, channels, grid_side = (feature_grid.shape[0], feature_grid.shape[1], feature_grid.shape[2])
    padded = jnp.pad(feature_grid, ((0, 0), (0, 0), (2, 2), (2, 2)))
    tap_list = []
    for row_tap in range(3):
        for col_tap in range(3):
            tap_piece = padded[:, :, 2 * row_tap:2 * row_tap + grid_side, 2 * col_tap:2 * col_tap + grid_side]
            tap_list.append(tap_piece.reshape(patches, channels, grid_side * grid_side))
    return tap_list

def dilated_untaps(tap_parts, grid_side):
    patches, channels = (tap_parts[0].shape[0], tap_parts[0].shape[1])
    running_sum = jnp.zeros((patches, channels, grid_side + 4, grid_side + 4), jnp.float32)
    for row_tap in range(3):
        for col_tap in range(3):
            tap_piece = tap_parts[row_tap * 3 + col_tap].reshape(patches, channels, grid_side, grid_side)
            running_sum = running_sum + jnp.pad(tap_piece, ((0, 0), (0, 0), (2 * row_tap, 4 - 2 * row_tap), (2 * col_tap, 4 - 2 * col_tap)))
    return running_sum[:, :, 2:grid_side + 2, 2:grid_side + 2]

def project(kernel, tap_list):
    running_sum = None
    for tap_index in range(len(tap_list)):
        tap_term = jnp.einsum('oi,pic->poc', kernel[:, :, tap_index].astype(jnp.float32), tap_list[tap_index].astype(jnp.float32))
        running_sum = tap_term if running_sum is None else running_sum + tap_term
    return running_sum

def silu_slope(pre_act):
    sigmoid_gate = jax.nn.sigmoid(pre_act)
    return sigmoid_gate * (1.0 + pre_act * (1.0 - sigmoid_gate))

def forward_block(features, strided_kernel, dilated_kernel, bias_row, grid_side):
    patches, channels = (features.shape[0], features.shape[1])
    half_side = grid_side // 2
    feature_grid = features.reshape(patches, channels, grid_side, grid_side)
    pre_act = project(strided_kernel, strided_taps(feature_grid)) + bias_row[None, :, None]
    activation = jax.nn.silu(pre_act).astype(jnp.bfloat16)
    act_grid = activation.reshape(patches, channels, half_side, half_side)
    branch_out = project(dilated_kernel, dilated_taps(act_grid)).astype(jnp.bfloat16)
    return (pre_act, activation, branch_out)

def backward_block(features, pre_act, activation, out_grad, strided_kernel, dilated_kernel, grid_side):
    patches, channels = (features.shape[0], features.shape[1])
    half_side = grid_side // 2
    out_wide = out_grad.astype(jnp.float32)
    act_list = dilated_taps(activation.reshape(patches, channels, half_side, half_side))
    grad_dilated = jnp.stack([jnp.einsum('poc,pic->oi', out_wide, tap_piece.astype(jnp.float32)) for tap_piece in act_list], axis=-1)
    act_parts = [jnp.einsum('oi,poc->pic', dilated_kernel[:, :, tap_index].astype(jnp.float32), out_wide) for tap_index in range(9)]
    act_grad = dilated_untaps(act_parts, half_side).reshape(patches, channels, half_side * half_side)
    pre_grad = act_grad * silu_slope(pre_act)
    bias_grad = lax.optimization_barrier(jnp.sum(pre_grad, axis=(0, 2)))
    pre_wide = pre_grad.astype(jnp.bfloat16).astype(jnp.float32)
    feature_list = strided_taps(features.reshape(patches, channels, grid_side, grid_side))
    grad_strided = jnp.stack([jnp.einsum('poc,pic->oi', pre_wide, tap_piece.astype(jnp.float32)) for tap_piece in feature_list], axis=-1)
    feature_parts = [jnp.einsum('oi,poc->pic', strided_kernel[:, :, tap_index].astype(jnp.float32), pre_wide) for tap_index in range(16)]
    feature_grad = strided_untaps(feature_parts, grid_side).reshape(patches, channels, grid_side * grid_side).astype(jnp.bfloat16)
    grad_row = jnp.concatenate([grad_strided.reshape(channels, channels * 16), grad_dilated.reshape(channels, channels * 9)], axis=1)
    return (grad_row, bias_grad, feature_grad)

def match_rows(pairing_row, branch, first_patch, patch_count):
    total_patches = pairing_row.shape[0]
    all_patches = jnp.arange(total_patches, dtype=jnp.int32)
    inverse = lax.optimization_barrier(jnp.sum(jnp.where(pairing_row[:, None] == all_patches[None, :], all_patches[:, None], 0), axis=0)).astype(jnp.int32)
    positions = (first_patch + jnp.arange(patch_count, dtype=jnp.int32)).astype(jnp.int32)
    return jnp.where(branch == 0, jnp.take(pairing_row, positions), jnp.take(inverse, positions)).astype(jnp.int32)

def reference(features_in, strided_weights, dilated_weights, tile_bias, cost_cotangent, footprint_pairing, valid_counts, tile_owner):
    scene_ids = jnp.arange(SCENES, dtype=jnp.int32)

    def kernels_of(scene_id):
        branch = scene_id % 2
        strided_kernel = strided_weights[branch].reshape(CH, CH, 16)
        dilated_kernel = dilated_weights[branch].reshape(CH, CH, 9)
        return (branch, strided_kernel, dilated_kernel)

    def forward_scene(scene_item):
        features, scene_id = scene_item
        branch, strided_kernel, dilated_kernel = kernels_of(scene_id)
        bias_row = tile_bias[tile_owner[scene_id]]
        return forward_block(features, strided_kernel, dilated_kernel, bias_row, GRID)
    pre_all, activation_all, branch_outs = lax.map(forward_scene, (features_in, scene_ids))

    def backward_scene(loop_state, scene_item):
        grad_rows, bias_grads = loop_state
        features, pre_act, activation, own_cotangent, scene_id = scene_item
        branch, strided_kernel, dilated_kernel = kernels_of(scene_id)
        partner = jnp.bitwise_xor(scene_id, 1).astype(jnp.int32)
        pair_index = (scene_id // 2).astype(jnp.int32)
        matched = match_rows(footprint_pairing[pair_index], branch, jnp.int32(0), PATCH_SCENE)
        partner_out = jnp.take(branch_outs[partner], matched, axis=0)
        partner_cot = jnp.take(cost_cotangent[partner], matched, axis=0)
        live_mask = (jnp.arange(PATCH_SCENE, dtype=jnp.int32) < valid_counts[pair_index]).astype(jnp.float32)
        signal = (own_cotangent.astype(jnp.float32) + partner_cot.astype(jnp.float32)) * live_mask[:, None]
        out_grad = (signal[:, None, :] * partner_out.astype(jnp.float32)).astype(jnp.bfloat16)
        grad_row, bias_grad, feature_grad = backward_block(features, pre_act, activation, out_grad, strided_kernel, dilated_kernel, GRID)
        branch_hit = jnp.arange(2, dtype=jnp.int32)[:, None, None] == branch
        grad_rows = grad_rows + jnp.where(branch_hit, grad_row[None], jnp.float32(0.0))
        tile_hit = jnp.arange(TILES, dtype=jnp.int32)[:, None] == tile_owner[scene_id]
        bias_grads = bias_grads + jnp.where(tile_hit, bias_grad[None, :], jnp.float32(0.0))
        return ((grad_rows, bias_grads), feature_grad)
    initial = (jnp.zeros((2, CH, 25 * CH), jnp.float32), jnp.zeros((TILES, CH), jnp.float32))
    (grad_rows, bias_grads), grad_features = lax.scan(backward_scene, initial, (features_in, pre_all, activation_all, cost_cotangent, scene_ids))
    weight_scale = 1.0 / math.sqrt(SCENES * PATCH_SCENE * CELLS)
    bias_scale = 1.0 / math.sqrt(PATCH_SCENE * CELLS)
    grad_weights = grad_rows.reshape(2 * CH, 25 * CH) * weight_scale
    grad_bias = bias_grads * bias_scale
    return (grad_features, grad_weights, grad_bias)
```

```python
import functools
import math

import jax
import jax.numpy as jnp
from jax import lax
from jax.experimental import pallas as pl
from jax.experimental.pallas import tpu as pltpu
from jax.sharding import PartitionSpec as P

CH = 64
ROW_TAPS = 4
DIL_TAPS = 9
BLOCKS = 14
SHIFTS = [(dr, dc) for dr in (-1, 0, 1) for dc in (-1, 0, 1)]
F32 = jnp.float32
BF16 = jnp.bfloat16
VMEM_LIMIT = 40 * 1024 * 1024


def shift_index(dr, dc):
    return (dr + 1) * 3 + dc + 1


def dot(a, b):
    return lax.dot_general(a, b, (((1,), (0,)), ((), ())), preferred_element_type=F32)


def dot_nt(a, b):
    return lax.dot_general(a, b, (((1,), (1,)), ((), ())), preferred_element_type=F32)


def shifted_masks(side, reach):
    cell = lax.broadcasted_iota(jnp.int32, (1, side * side), 1)
    row, col = cell // side, cell % side
    masks = {}
    for dr, dc in SHIFTS:
        ok = (
            (row + dr * reach >= 0)
            & (row + dr * reach < side)
            & (col + dc * reach >= 0)
            & (col + dc * reach < side)
        )
        masks[dr, dc] = ok.astype(F32).astype(BF16)
    return masks


def shifted(x, dr, dc, side, reach, masks):
    if dr == 0 and dc == 0:
        return x
    cells = side * side
    return pltpu.roll(x, (-(dr * side + dc) * reach) % cells, 1) * masks[dr, dc]


def phase_matrix(side, transposed):
    size = 16 * side
    dims = (size, size)
    source = lax.broadcasted_iota(jnp.int32, dims, 1 if transposed else 0)
    target = lax.broadcasted_iota(jnp.int32, dims, 0 if transposed else 1)
    phase, cell = target // (4 * side), target % (4 * side)
    row, col = cell // side, cell % side
    wanted = (2 * row + phase // 2) * (2 * side) + 2 * col + phase % 2
    return jnp.where(source == wanted, 1.0, 0.0).astype(BF16)


TAP_LINES = {0: (1, -1), 1: (0, 0), 2: (1, 0), 3: (0, 1)}


def tap_matrices(weight, taps, scratch):
    wide = weight.astype(F32)
    scratch[0 : CH * taps, 0:CH] = wide.T
    return [scratch[pl.ds(tap, CH, stride=taps), 0:CH] for tap in range(taps)]


def forward_kernel(
    owner_ref, x_ref, ws_ref, wd_ref, bias_ref, cot_ref, ph_ref, pre_ref, act_ref, send_ref, wscr, im_scr
):
    patches, side = x_ref.shape[0], math.isqrt(x_ref.shape[2]) // 2
    cells = side * side
    scene = lax.axis_index("scene")
    branch = scene % 2
    split = phase_matrix(side, False)
    run = 16 * side
    runs = x_ref.shape[2] // run
    mats = tap_matrices(ws_ref[branch], 16, wscr)
    w_strided = jnp.concatenate(mats, axis=0).T.astype(BF16)
    mats = tap_matrices(wd_ref[branch], 9, wscr)
    w_dilated = jnp.concatenate(mats, axis=0).T.astype(BF16)
    bias_row = bias_ref[pl.ds(owner_ref[scene], 1), :]
    bias_col = jnp.broadcast_to(bias_row, (8, CH)).T[:, 0:1]
    near = shifted_masks(side, 1)
    far = shifted_masks(side, 2)
    for p in range(patches):
        for q in range(runs):
            part = dot(x_ref[p, :, q * run : (q + 1) * run], split).astype(BF16)
            for phase in range(4):
                ph_ref[p, phase * CH : (phase + 1) * CH, q * 4 * side : (q + 1) * 4 * side] = part[
                    :, phase * 4 * side : (phase + 1) * 4 * side
                ]
        for rt in range(4):
            for ct in range(4):
                (pr, dr), (pc, dc) = TAP_LINES[rt], TAP_LINES[ct]
                phase, tap = pr * 2 + pc, rt * 4 + ct
                im_scr[tap * CH : (tap + 1) * CH, :] = shifted(
                    ph_ref[p, phase * CH : (phase + 1) * CH, :], dr, dc, side, 1, near
                )
        pre = dot(w_strided, im_scr[...]) + bias_col
        pre_ref[p] = pre
        act = (pre * (1.0 / (1.0 + jnp.exp(-pre)))).astype(BF16)
        act_ref[p] = act
        for tap, (dr, dc) in enumerate(SHIFTS):
            im_scr[tap * CH : (tap + 1) * CH, :] = shifted(act, dr, dc, side, 2, far)
        out = dot(w_dilated, im_scr[0 : DIL_TAPS * CH, :])
        send_ref[p * CH : (p + 1) * CH, :] = out.astype(BF16)
    cot = cot_ref[...].astype(F32)
    cot = jnp.concatenate([cot, jnp.zeros((16 - patches, cells), F32)], axis=0)
    send_ref[patches * CH :, :] = cot.astype(BF16)


def prepare_kernel(pre_ref, ws_ref, wd_ref, slope_ref, wf_ref, wt_ref, wscr):
    branch = lax.axis_index("scene") % 2
    for p in range(pre_ref.shape[0]):
        pre = pre_ref[p]
        gate = 1.0 / (1.0 + jnp.exp(-pre))
        slope_ref[p] = gate * (1.0 + pre * (1.0 - gate))
    mats = tap_matrices(ws_ref[branch], 16, wscr)
    blocks = {}
    for rt in range(4):
        for ct in range(4):
            (pr, dr), (pc, dc) = TAP_LINES[rt], TAP_LINES[ct]
            blocks[pr * 2 + pc, shift_index(-dr, -dc)] = mats[rt * 4 + ct]
    zero = jnp.zeros((CH, CH), F32)
    for phase in range(4):
        row = [blocks.get((phase, s), zero) for s in range(9)]
        wf_ref[phase * CH : (phase + 1) * CH, :] = jnp.concatenate(row, axis=1).astype(BF16)
    mats = tap_matrices(wd_ref[branch], 9, wscr)
    wt_ref[...] = jnp.concatenate(mats[::-1], axis=1).astype(BF16)


def backward_kernel(
    pairing_ref, valid_ref, near_ref, far_ref, cot_ref, act_ref, slope_ref, ph_ref, wt_ref,
    pre_b_ref, *refs, chunked, weight_scale, bias_scale,
):
    if chunked:
        keep_ref, give_ref, shift_scr, dil_scr, grad_acc, grad_scr = refs
    else:
        grad_scr, shift_scr, dil_scr, grad_acc = refs
    patches, side = act_ref.shape[0], math.isqrt(act_ref.shape[2])
    total = pairing_ref.shape[1]
    scene, tile = lax.axis_index("scene"), lax.axis_index("tile")
    branch, pair = scene % 2, scene // 2
    first = tile * patches
    near, far = shifted_masks(side, 1), shifted_masks(side, 2)
    bias = jnp.zeros((CH, 1), F32)
    for p in range(patches):
        position = first + p
        direct = pairing_ref[pair, position]
        inverse = jnp.int32(0)
        for i in range(total):
            inverse = inverse + jnp.where(pairing_ref[pair, i] == position, i, 0)
        match = jnp.where(branch == 0, direct, inverse)
        local, here = match % patches, match // patches == tile
        start = pl.multiple_of(local * CH, CH)
        partner = jnp.where(here, near_ref[pl.ds(start, CH), :], far_ref[pl.ds(start, CH), :])
        cots_near = near_ref[patches * CH :, :].astype(F32)
        cots_far = far_ref[patches * CH :, :].astype(F32)
        cots = jnp.where(here, cots_near, cots_far)
        pick = lax.broadcasted_iota(jnp.int32, cots.shape, 0) == local
        partner_cot = jnp.sum(jnp.where(pick, cots, 0.0), axis=0, keepdims=True)
        live = jnp.where(position < valid_ref[pair], 1.0, 0.0)
        signal = (cot_ref[p : p + 1, :].astype(F32) + partner_cot) * live
        out_grad = (signal * partner.astype(F32)).astype(BF16)
        for tap, (dr, dc) in enumerate(SHIFTS):
            shift_scr[tap * CH : (tap + 1) * CH, :] = shifted(out_grad, dr, dc, side, 2, far)
        act_grad = dot(wt_ref[...], shift_scr[...])
        act = act_ref[p]
        dil = dot_nt(shift_scr[...], jnp.concatenate([act, act], axis=0))
        pre_grad = act_grad * slope_ref[p]
        bias = bias + jnp.sum(pre_grad, axis=1, keepdims=True)
        pre_b = pre_grad.astype(BF16)
        pre_b_ref[p] = pre_b
        for s, (dr, dc) in enumerate(SHIFTS):
            shift_scr[s * CH : (s + 1) * CH, :] = shifted(pre_b, dr, dc, side, 1, near)
        strided = dot_nt(shift_scr[...], ph_ref[p])
        if p == 0:
            dil_scr[...] = dil
            grad_acc[...] = strided
        else:
            dil_scr[...] += dil
            grad_acc[...] += strided
    lower = lax.broadcasted_iota(jnp.int32, (CH, 2 * CH), 1) < CH

    def strided_piece(pr, shift, low):
        return grad_acc[shift * CH : (shift + 1) * CH, pr * 2 * CH : (pr + 1) * 2 * CH]

    for rt in range(4):
        pr, dr = TAP_LINES[rt]
        for k in range(2):
            low_dc, high_dc = (0, 0) if k == 0 else (1, -1)
            low = strided_piece(pr, shift_index(-dr, -low_dc), True)
            high = strided_piece(pr, shift_index(-dr, -high_dc), False)
            grad_scr[rt * 2 + k] = jnp.where(lower, low, high) * weight_scale
    for j in range(5):
        low = dil_scr[(8 - 2 * j) * CH : (9 - 2 * j) * CH, :]
        high = dil_scr[(7 - 2 * j) * CH : (8 - 2 * j) * CH, :] if j < 4 else jnp.zeros_like(low)
        grad_scr[8 + j] = jnp.where(lower, low, high) * weight_scale
    bias_wide = jnp.concatenate([jnp.broadcast_to(bias, (CH, 8)).T, jnp.zeros((8, CH), F32)], axis=1)
    top = lax.broadcasted_iota(jnp.int32, (8, 2 * CH), 0) == 0
    bias_rows = jnp.where(top, bias_wide * bias_scale, 0.0)
    if not chunked:
        grad_scr[BLOCKS - 1] = jnp.concatenate([bias_rows] * 8, axis=0)
        return
    for ref, core in ((keep_ref, branch), (give_ref, 1 - branch)):
        for half in range(2):
            pieces = []
            for block in range(BLOCKS - 1):
                for y in range(2):
                    row = pl.multiple_of((half * 4 + y * 2 + core) * 8, 8)
                    pieces.append(grad_scr[block, pl.ds(row, 8), :])
            pieces += [bias_rows, jnp.zeros((8, 2 * CH), F32)]
            ref[half] = jnp.concatenate(pieces, axis=0).astype(BF16)


def spread_kernel(owner_ref, keep_ref, got_ref, own_ref, one_ref, two_ref, three_ref, *, bias_rows):
    scene = lax.axis_index("scene")
    core, z = scene % 2, scene // 4
    rows = keep_ref.shape[1]
    bias_at = rows - 16
    mine = keep_ref[0, bias_at:, :].astype(F32)[0:1, :]
    theirs = got_ref[0, bias_at:, :].astype(F32)[0:1, :]
    index = lax.broadcasted_iota(jnp.int32, (16, 2 * CH), 0)
    for distance, ref in ((0, own_ref), (1, one_ref), (2, two_ref), (3, three_ref)):
        target = z ^ distance
        kept = target // 2 == core
        ref[...] = jnp.where(kept, keep_ref[target % 2], got_ref[target % 2])
        bias = jnp.zeros((16, 2 * CH), F32)
        for source, vector in ((scene, mine), (scene ^ 1, theirs)):
            owner = owner_ref[source]
            place = owner // (2 * bias_rows)
            row = (place // 2 % 2) * 8 + owner % (2 * bias_rows)
            hit = (place % 2 == core) & (place // 4 == target)
            bias = bias + jnp.where(index == jnp.where(hit, row, -1), vector, 0.0)
        ref[bias_at:, :] = bias.astype(BF16)


def join_kernel(own_ref, a_ref, b_ref, c_ref, keep_ref, stay_ref, cross_ref, scr):
    y = lax.axis_index("scene") // 2 % 2
    scr[...] = (own_ref[...].astype(F32) + a_ref[...].astype(F32)) + (
        b_ref[...].astype(F32) + c_ref[...].astype(F32)
    )

    def chunk(which):
        return jnp.concatenate(
            [scr[pl.ds(pl.multiple_of(block * 16 + which * 8, 8), 8), :] for block in range(BLOCKS)], axis=0
        )

    kept = chunk(y)
    keep_ref[...] = kept
    stay_ref[...] = kept.astype(BF16)
    cross_ref[...] = chunk(1 - y).astype(BF16)


def finish_kernel(own_ref, a_ref, b_ref, c_ref, weights_ref, bias_ref, strided_scr, dilated_scr):
    tile = lax.axis_index("tile")
    total = (own_ref[...] + a_ref[...].astype(F32)) + (b_ref[...].astype(F32) + c_ref[...].astype(F32))
    bias = total[(BLOCKS - 1) * 8 :, :]
    index = lax.broadcasted_iota(jnp.int32, bias.shape, 0)
    bias_ref[...] = jnp.sum(jnp.where(index == tile, bias, 0.0), axis=0, keepdims=True)[:, 0:CH]
    width = 2 * CH
    turned = jnp.concatenate([total, jnp.zeros((width - BLOCKS * 8, width), F32)], axis=0).T
    for block in range(BLOCKS - 1):
        lined = turned if block == 0 else pltpu.roll(turned, width - block * 8, 1)
        for half in range(2):
            piece = lined[half * CH : (half + 1) * CH, :]
            if block < 8:
                tap = block // 2 * 4 + ((1, 2), (3, 0))[block % 2][half]
                strided_scr[pl.ds(tap, CH, stride=16), :] = piece
            elif (block - 8) * 2 + half < DIL_TAPS:
                dilated_scr[pl.ds((block - 8) * 2 + half, CH, stride=DIL_TAPS), :] = piece
    weights_ref[:, 0 : 16 * CH] = strided_scr[...].T[0:8, :]
    weights_ref[:, 16 * CH :] = dilated_scr[...].T[0:8, :]


def feature_kernel(pre_b_ref, wf_ref, out_ref, shift_scr):
    patches, side = pre_b_ref.shape[0], math.isqrt(pre_b_ref.shape[2])
    near = shifted_masks(side, 1)
    merge = phase_matrix(side, True)
    run = 16 * side
    for p in range(patches):
        pre_b = pre_b_ref[p]
        for s, (dr, dc) in enumerate(SHIFTS):
            shift_scr[s * CH : (s + 1) * CH, :] = shifted(pre_b, dr, dc, side, 1, near)
        phases = dot(wf_ref[...], shift_scr[...]).astype(BF16)
        for q in range(out_ref.shape[2] // run):
            part = jnp.concatenate(
                [
                    phases[phase * CH : (phase + 1) * CH, q * 4 * side : (q + 1) * 4 * side]
                    for phase in range(4)
                ],
                axis=1,
            )
            out_ref[p, :, q * run : (q + 1) * run] = dot(part, merge).astype(BF16)


def call(kernel, outs, ins, scratch, *args, flops=0):
    vmem, smem = pl.BlockSpec(memory_space=pltpu.VMEM), pl.BlockSpec(memory_space=pltpu.SMEM)
    return pl.pallas_call(
        kernel,
        out_shape=[jax.ShapeDtypeStruct(shape, kind) for shape, kind in outs],
        in_specs=[smem if space == "s" else vmem for space in ins],
        out_specs=[vmem] * len(outs),
        scratch_shapes=[pltpu.VMEM(shape, kind) for shape, kind in scratch],
        compiler_params=pltpu.CompilerParams(vmem_limit_bytes=VMEM_LIMIT),
        cost_estimate=pl.CostEstimate(flops=flops, bytes_accessed=1 << 20, transcendentals=0),
    )(*args)


def scene_xor(x, distance):
    return lax.ppermute(x, "scene", [(i, i ^ distance) for i in range(lax.axis_size("scene"))])


def device_xor(x, scene_distance, tile_distance):
    tiles, scenes = lax.axis_size("tile"), lax.axis_size("scene")
    pairs = [
        (s * tiles + t, (s ^ scene_distance) * tiles + (t ^ tile_distance))
        for s in range(scenes)
        for t in range(tiles)
    ]
    return lax.ppermute(x, ("scene", "tile"), pairs)


def reduce_anywhere(blocks, tile_owner, bias_rows):
    channels = blocks.shape[1]
    scene = lax.axis_index("scene")
    scenes, tiles = lax.axis_size("scene"), lax.axis_size("tile")
    halves = blocks.reshape(BLOCKS, channels, 2, channels)
    strided, dilated = [None] * 16, []
    for block in range(8):
        for half in range(2):
            strided[block // 2 * 4 + ((1, 2), (3, 0))[block % 2][half]] = halves[block, :, half]
    for tap in range(DIL_TAPS):
        dilated.append(halves[8 + tap // 2, :, tap % 2])
    row = jnp.concatenate(
        [
            jnp.stack(strided, axis=-1).reshape(channels, 16 * channels),
            jnp.stack(dilated, axis=-1).reshape(channels, DIL_TAPS * channels),
        ],
        axis=1,
    )
    hit = jnp.arange(2, dtype=jnp.int32)[:, None, None] == scene % 2
    term = jnp.where(hit, row[None], 0.0).reshape(2 * channels, 25 * channels)
    weights = lax.psum(lax.psum_scatter(term, "scene", scatter_dimension=0, tiled=True), "tile")
    tile_id = lax.dynamic_index_in_dim(tile_owner, scene, 0, keepdims=False)
    owned = jnp.arange(scenes * tiles * bias_rows, dtype=jnp.int32) == tile_id
    bias = jnp.where(owned[:, None], halves[BLOCKS - 1, 0, 0][None, :], 0.0)
    return weights, lax.psum_scatter(bias, ("scene", "tile"), scatter_dimension=0, tiled=True)


def local(
    features_in,
    strided_weights,
    dilated_weights,
    tile_bias,
    cost_cotangent,
    footprint_pairing,
    valid_counts,
    tile_owner,
):
    features, own_cot = features_in[0], cost_cotangent[0]
    patches, channels, cells_in = features.shape
    cells = own_cot.shape[1]
    scenes, tiles = lax.axis_size("scene"), lax.axis_size("tile")
    weight_scale = 1.0 / math.sqrt(scenes * patches * tiles * cells)
    bias_scale = 1.0 / math.sqrt(patches * tiles * cells)
    bias_rows = tile_bias.shape[0] // (scenes * tiles)
    grid = (patches, channels, cells)
    wscr = ((16 * channels, 2 * channels), F32)
    phases, pre, act, send = call(
        forward_kernel,
        [((patches, 4 * channels, cells), BF16), (grid, F32), (grid, BF16), ((patches * channels + 16, cells), BF16)],
        "svvvvv",
        [wscr, ((16 * channels, cells), BF16)],
        tile_owner, features, strided_weights, dilated_weights, tile_bias, own_cot,
        flops=10**9,
    )
    far = device_xor(send, 1, 1)
    near = scene_xor(send, 1)
    slope, w_feature, w_act = call(
        prepare_kernel,
        [(grid, F32), ((4 * channels, 9 * channels), BF16), ((channels, 9 * channels), BF16)],
        "vvv",
        [wscr],
        pre, strided_weights, dilated_weights,
        flops=10**9,
    )
    chunked = scenes == 16 and tiles == 2 and bias_rows == 1
    block_shape = ((BLOCKS, channels, 128), F32)
    half_shape = ((2, BLOCKS * 16, 128), BF16)
    scratch = [
        ((9 * channels, cells), BF16),
        ((9 * channels, 128), F32),
        ((9 * channels, 4 * channels), F32),
    ]
    pre_b, *grads = call(
        functools.partial(
            backward_kernel, chunked=chunked, weight_scale=weight_scale, bias_scale=bias_scale
        ),
        [(grid, BF16)] + ([half_shape] * 2 if chunked else [block_shape]),
        "ssvvvvvvv",
        scratch + ([block_shape] if chunked else []),
        footprint_pairing, valid_counts, near, far, own_cot, act, slope, phases, w_act,
        flops=10**9,
    )
    if not chunked:
        (feature_grads,) = call(
            feature_kernel,
            [(features.shape, BF16)],
            "vv",
            [((9 * channels, cells), BF16)],
            pre_b, w_feature,
            flops=10**9,
        )
        return (feature_grads[None],) + reduce_anywhere(grads[0], tile_owner, bias_rows)
    keep, give = grads
    got = scene_xor(give, 1)
    own, one, two, three = call(
        functools.partial(spread_kernel, bias_rows=bias_rows),
        [((BLOCKS * 16, 128), BF16)] * 4,
        "svv",
        [],
        tile_owner, keep, got,
    )
    two, three, one = scene_xor(two, 8), scene_xor(three, 12), scene_xor(one, 4)
    (feature_grads,) = call(
        feature_kernel,
        [(features.shape, BF16)],
        "vv",
        [((9 * channels, cells), BF16)],
        pre_b, w_feature,
        flops=10**9,
    )
    kept, stay, cross = call(
        join_kernel,
        [((BLOCKS * 8, 128), F32), ((BLOCKS * 8, 128), BF16), ((BLOCKS * 8, 128), BF16)],
        "vvvv",
        [((BLOCKS * 16, 128), F32)],
        own, one, two, three,
    )
    by_y, by_xy, by_x = device_xor(cross, 2, 0), device_xor(cross, 2, 1), device_xor(stay, 0, 1)
    grad_weights, grad_bias = call(
        finish_kernel,
        [((8, 25 * channels), F32), ((1, channels), F32)],
        "vvvv",
        [((16 * channels, 128), F32), ((9 * channels, 128), F32)],
        kept, by_y, by_xy, by_x,
    )
    return (feature_grads[None], grad_weights, grad_bias)


def solution(mesh):
    return jax.shard_map(
        local,
        mesh=mesh,
        in_specs=(
            P("scene", "tile", None, None),
            P(),
            P(),
            P(),
            P("scene", "tile", None),
            P(),
            P(),
            P(),
        ),
        out_specs=(P("scene", "tile", None, None), P("scene", None), P(("scene", "tile"), None)),
        check_vma=False,
    )
```

```python
import functools
import math

import jax
import jax.numpy as jnp
from jax import lax
from jax.experimental import pallas as pl
from jax.experimental.pallas import tpu as pltpu
from jax.sharding import PartitionSpec as P

CH = 64
ROW_TAPS = 4
DIL_TAPS = 9
BLOCKS = 14
SHIFTS = [(dr, dc) for dr in (-1, 0, 1) for dc in (-1, 0, 1)]
F32 = jnp.float32
BF16 = jnp.bfloat16
VMEM_LIMIT = 24 * 1024 * 1024


def shift_index(dr, dc):
    return (dr + 1) * 3 + dc + 1


def dot(a, b):
    return lax.dot_general(a, b, (((1,), (0,)), ((), ())), preferred_element_type=F32)


def dot_nt(a, b):
    return lax.dot_general(a, b, (((1,), (1,)), ((), ())), preferred_element_type=F32)


def shifted_masks(side, reach):
    cell = lax.broadcasted_iota(jnp.int32, (1, side * side), 1)
    row, col = cell // side, cell % side
    masks = {}
    for dr, dc in SHIFTS:
        ok = (
            (row + dr * reach >= 0)
            & (row + dr * reach < side)
            & (col + dc * reach >= 0)
            & (col + dc * reach < side)
        )
        masks[dr, dc] = ok.astype(F32).astype(BF16)
    return masks


def shifted(x, dr, dc, side, reach, masks):
    if dr == 0 and dc == 0:
        return x
    cells = side * side
    return pltpu.roll(x, (-(dr * side + dc) * reach) % cells, 1) * masks[dr, dc]


def phase_matrix(side, transposed):
    size = 16 * side
    dims = (size, size)
    source = lax.broadcasted_iota(jnp.int32, dims, 1 if transposed else 0)
    target = lax.broadcasted_iota(jnp.int32, dims, 0 if transposed else 1)
    phase, cell = target // (4 * side), target % (4 * side)
    row, col = cell // side, cell % side
    wanted = (2 * row + phase // 2) * (2 * side) + 2 * col + phase % 2
    return jnp.where(source == wanted, 1.0, 0.0).astype(BF16)


TAP_LINES = {0: (1, -1), 1: (0, 0), 2: (1, 0), 3: (0, 1)}


def tap_matrices(weight, taps, scratch):
    wide = weight.astype(F32)
    scratch[0 : CH * taps, 0:CH] = wide.T
    return [scratch[pl.ds(tap, CH, stride=taps), 0:CH] for tap in range(taps)]


def forward_patch(x_ref, cot, w_strided, w_dilated, bias_col, ph_ref, pre_ref, act_ref, send_ref, im_scr):
    side = math.isqrt(x_ref.shape[1]) // 2
    run, lanes = 16 * side, side * side // 128
    split = phase_matrix(side, False)
    near, far = shifted_masks(side, 1), shifted_masks(side, 2)
    runs = x_ref.shape[1] // run
    stacked = jnp.concatenate([x_ref[:, q * run : (q + 1) * run] for q in range(runs)], axis=0)
    parts = dot(stacked, split).astype(BF16)
    for q in range(runs):
        for phase in range(4):
            ph_ref[phase * CH : (phase + 1) * CH, q * 4 * side : (q + 1) * 4 * side] = parts[
                q * CH : (q + 1) * CH, phase * 4 * side : (phase + 1) * 4 * side
            ]
    for rt in range(4):
        for ct in range(4):
            (pr, dr), (pc, dc) = TAP_LINES[rt], TAP_LINES[ct]
            phase, tap = pr * 2 + pc, rt * 4 + ct
            im_scr[tap * CH : (tap + 1) * CH, :] = shifted(
                ph_ref[phase * CH : (phase + 1) * CH, :], dr, dc, side, 1, near
            )
    pre = dot(w_strided, im_scr[...]) + bias_col
    pre_ref[...] = pre
    act = (pre * (1.0 / (1.0 + jnp.exp(-pre)))).astype(BF16)
    act_ref[...] = act
    for tap, (dr, dc) in enumerate(SHIFTS):
        im_scr[tap * CH : (tap + 1) * CH, :] = shifted(act, dr, dc, side, 2, far)
    out = dot(w_dilated, im_scr[0 : DIL_TAPS * CH, :]).astype(BF16)
    for lane in range(lanes):
        send_ref[lane * CH : (lane + 1) * CH, :] = out[:, lane * 128 : (lane + 1) * 128]
    rows = [cot[:, lane * 128 : (lane + 1) * 128] for lane in range(lanes)]
    rows.append(jnp.zeros((16 - lanes, 128), F32))
    send_ref[lanes * CH :, :] = jnp.concatenate(rows, axis=0).astype(BF16)


def first_kernel(
    owner_hbm, x_hbm, ws_hbm, wd_hbm, bias_hbm, cot_hbm,
    ph_ref, pre_ref, act_ref, send_ref, strided_ref, dilated_ref, bias_ref,
    x_ref, ws_ref, wd_ref, cot_ref, table_ref, owner_ref, wscr, im_scr, sems,
):
    scene = lax.axis_index("scene")
    branch = scene % 2
    copies = [
        pltpu.make_async_copy(source, target, sems.at[i])
        for i, (source, target) in enumerate(
            [
                (ws_hbm.at[branch], ws_ref),
                (wd_hbm.at[branch], wd_ref),
                (x_hbm.at[0], x_ref),
                (owner_hbm, owner_ref),
                (bias_hbm, table_ref),
                (cot_hbm, cot_ref),
            ]
        )
    ]
    for copy in copies:
        copy.start()
    copies[0].wait()
    mats = tap_matrices(ws_ref[...], 16, wscr)
    strided_ref[...] = jnp.concatenate(mats, axis=0).T.astype(BF16)
    copies[1].wait()
    mats = tap_matrices(wd_ref[...], 9, wscr)
    dilated_ref[...] = jnp.concatenate(mats, axis=0).T.astype(BF16)
    for copy in copies[2:]:
        copy.wait()
    bias_row = table_ref[pl.ds(owner_ref[scene], 1), :]
    bias_ref[...] = jnp.broadcast_to(jnp.broadcast_to(bias_row, (8, CH)).T[:, 0:1], (CH, 128))
    forward_patch(
        x_ref, cot_ref[...].astype(F32)[0:1, :], strided_ref[...], dilated_ref[...], bias_ref[:, 0:1],
        ph_ref, pre_ref, act_ref, send_ref, im_scr,
    )


def later_kernel(
    x_ref, cot_ref, w_strided_ref, w_dilated_ref, bias_ref, *refs, patch
):
    ph_ref, pre_ref, act_ref, send_ref, im_scr = refs[-5:]
    forward_patch(
        x_ref.at[patch], cot_ref[...].astype(F32)[patch : patch + 1, :], w_strided_ref[...], w_dilated_ref[...],
        bias_ref[:, 0:1], ph_ref, pre_ref, act_ref, send_ref, im_scr,
    )


def prepare_kernel(pairing_ref, valid_ref, owner_ref, ws_ref, wd_ref, *refs, bias_rows):
    patches = (len(refs) - 5) // 2
    pre_refs, slope_refs = refs[:patches], refs[patches : 2 * patches]
    wf_ref, wt_ref, select_ref, place_ref, wscr = refs[2 * patches :]
    scene, tile = lax.axis_index("scene"), lax.axis_index("tile")
    branch, pair = scene % 2, scene // 2
    for pre_ref, slope_ref in zip(pre_refs, slope_refs):
        pre = pre_ref[...]
        gate = 1.0 / (1.0 + jnp.exp(-pre))
        slope_ref[...] = gate * (1.0 + pre * (1.0 - gate))
    mats = tap_matrices(ws_ref[branch], 16, wscr)
    blocks = {}
    for rt in range(4):
        for ct in range(4):
            (pr, dr), (pc, dc) = TAP_LINES[rt], TAP_LINES[ct]
            blocks[pr * 2 + pc, shift_index(-dr, -dc)] = mats[rt * 4 + ct]
    zero = jnp.zeros((CH, CH), F32)
    for phase in range(4):
        row = [blocks.get((phase, s), zero) for s in range(9)]
        wf_ref[phase * CH : (phase + 1) * CH, :] = jnp.concatenate(row, axis=1).astype(BF16)
    mats = tap_matrices(wd_ref[branch], 9, wscr)
    wt_ref[...] = jnp.concatenate(mats[::-1], axis=1).astype(BF16)
    total = pairing_ref.shape[1]
    row = lax.broadcasted_iota(jnp.int32, select_ref.shape, 0)
    select = jnp.zeros(select_ref.shape, F32)
    for p in range(patches):
        position = tile * patches + p
        matched, inverse = pairing_ref[pair, position], jnp.int32(0)
        for i in range(total):
            inverse = inverse + jnp.where(pairing_ref[pair, i] == position, i, 0)
        matched = jnp.where(branch == 0, matched, inverse)
        chosen = p * total + jnp.where(matched // patches == tile, 0, patches) + matched % patches
        live = jnp.where(position < valid_ref[pair], patches * total + p, -1)
        select = jnp.where((row == chosen) | (row == live), 1.0, select)
    select_ref[...] = select
    row = lax.broadcasted_iota(jnp.int32, place_ref.shape, 0)
    here = scene // 2 % 4
    place = jnp.zeros(place_ref.shape, F32)
    for k, source in enumerate((scene, scene ^ 1)):
        owner = owner_ref[source]
        target = owner // (2 * bias_rows)
        half = jnp.where(target // 8 == branch, 0, 1)
        wanted = k * 64 + ((target // 2 % 4) ^ here) * 16 + half * 8 + owner % (2 * bias_rows)
        place = jnp.where(row == jnp.where(target % 2 == branch, wanted, -1), 1.0, place)
    place_ref[...] = place


def backward_kernel(select_ref, wt_ref, *refs, patches, chunked, weight_scale, bias_scale):
    near_refs, far_refs, own_refs, act_refs, slope_refs, ph_refs = (
        refs[k * patches : (k + 1) * patches] for k in range(6)
    )
    pre_b_refs, refs = refs[6 * patches : 7 * patches], refs[7 * patches :]
    if chunked:
        keep_ref, give_ref, shift_scr, dil_scr, grad_acc, grad_scr = refs
    else:
        grad_scr, shift_scr, dil_scr, grad_acc = refs
    side = math.isqrt(act_refs[0].shape[1])
    lanes = side * side // 128
    scene = lax.axis_index("scene")
    branch = scene % 2
    near, far = shifted_masks(side, 1), shifted_masks(side, 2)
    bias = jnp.zeros((CH, 1), F32)
    candidates = list(near_refs) + list(far_refs)
    count = len(candidates)
    for p in range(patches):
        partner = None
        for k, ref in enumerate(candidates):
            term = ref[...] * select_ref[p * count + k : p * count + k + 1, :].astype(BF16)
            partner = term if partner is None else partner + term
        live = select_ref[patches * count + p : patches * count + p + 1, :]
        cots = own_refs[p][lanes * CH :, :].astype(F32) + partner[lanes * CH :, :].astype(F32)
        signal = cots * live
        out_grad = jnp.concatenate(
            [
                (signal[j : j + 1, :] * partner[j * CH : (j + 1) * CH, :].astype(F32)).astype(BF16)
                for j in range(lanes)
            ],
            axis=1,
        )
        for tap, (dr, dc) in enumerate(SHIFTS):
            shift_scr[tap * CH : (tap + 1) * CH, :] = shifted(out_grad, dr, dc, side, 2, far)
        act_grad = dot(wt_ref[...], shift_scr[...])
        act = act_refs[p][...]
        dil = dot_nt(shift_scr[...], jnp.concatenate([act, act], axis=0))
        pre_grad = act_grad * slope_refs[p][...]
        bias = bias + jnp.sum(pre_grad, axis=1, keepdims=True)
        pre_b = pre_grad.astype(BF16)
        pre_b_refs[p][...] = pre_b
        for s, (dr, dc) in enumerate(SHIFTS):
            shift_scr[s * CH : (s + 1) * CH, :] = shifted(pre_b, dr, dc, side, 1, near)
        strided = dot_nt(shift_scr[...], ph_refs[p][...])
        if p == 0:
            dil_scr[...] = dil
            grad_acc[...] = strided
        else:
            dil_scr[...] += dil
            grad_acc[...] += strided
    lower = lax.broadcasted_iota(jnp.int32, (CH, 2 * CH), 1) < CH

    def strided_piece(pr, shift):
        return grad_acc[shift * CH : (shift + 1) * CH, pr * 2 * CH : (pr + 1) * 2 * CH]

    for rt in range(4):
        pr, dr = TAP_LINES[rt]
        for k in range(2):
            low_dc, high_dc = (0, 0) if k == 0 else (1, -1)
            low = strided_piece(pr, shift_index(-dr, -low_dc))
            high = strided_piece(pr, shift_index(-dr, -high_dc))
            grad_scr[rt * 2 + k] = jnp.where(lower, low, high) * weight_scale
    for j in range(5):
        low = dil_scr[(8 - 2 * j) * CH : (9 - 2 * j) * CH, :]
        high = dil_scr[(7 - 2 * j) * CH : (8 - 2 * j) * CH, :] if j < 4 else jnp.zeros_like(low)
        grad_scr[8 + j] = jnp.where(lower, low, high) * weight_scale
    bias_wide = jnp.concatenate([jnp.broadcast_to(bias, (CH, 8)).T, jnp.zeros((8, CH), F32)], axis=1)
    bias_wide = bias_wide * bias_scale
    if not chunked:
        grad_scr[BLOCKS - 1] = jnp.concatenate([bias_wide] * 8, axis=0)
        return
    here = scene // 2 % 4
    for ref, core in ((keep_ref, branch), (give_ref, 1 - branch)):
        for d in range(4):
            row = pl.multiple_of(((here ^ d) * 2 + core) * 8, 8)
            pieces = [grad_scr[block, pl.ds(row, 8), :] for block in range(BLOCKS - 1)]
            ref[d] = jnp.concatenate(pieces + [bias_wide], axis=0).astype(BF16)


def spread_kernel(place_ref, keep_ref, got_ref, *out_refs):
    rows = keep_ref.shape[1]
    top = lax.broadcasted_iota(jnp.int32, (16, 128), 0) < 8
    mine = keep_ref[0, rows - 16 :, :].astype(F32)[8:9, :]
    theirs = got_ref[0, rows - 16 :, :].astype(F32)[8:9, :]
    for d, out_ref in enumerate(out_refs):
        for half, ref in enumerate((keep_ref, got_ref)):
            at = d * 16 + half * 8
            bias = place_ref[at : at + 8, :] * mine + place_ref[64 + at : 72 + at, :] * theirs
            last = ref[d, rows - 16 :, :].astype(F32)
            last = jnp.where(top, last, jnp.concatenate([bias, bias], axis=0))
            out_ref[half * rows : (half + 1) * rows - 16, :] = ref[d, : rows - 16, :]
            out_ref[(half + 1) * rows - 16 : (half + 1) * rows, :] = last.astype(BF16)


def join_kernel(own_ref, a_ref, b_ref, c_ref, keep_ref, stay_ref, cross_ref):
    scene = lax.axis_index("scene")
    rows = keep_ref.shape[0]
    total = (own_ref[...].astype(F32) + a_ref[...].astype(F32)) + (
        b_ref[...].astype(F32) + c_ref[...].astype(F32)
    )
    mine, theirs = total[:rows, :], total[rows:, :]
    first = scene // 8 == scene % 2
    kept = jnp.where(first, mine, theirs)
    keep_ref[...] = kept
    stay_ref[...] = kept.astype(BF16)
    cross_ref[...] = jnp.where(first, theirs, mine).astype(BF16)


def finish_kernel(own_ref, a_ref, b_ref, c_ref, weights_ref, bias_ref, strided_scr, dilated_scr):
    tile = lax.axis_index("tile")
    total = (own_ref[...] + a_ref[...].astype(F32)) + (b_ref[...].astype(F32) + c_ref[...].astype(F32))
    bias = total[(BLOCKS - 1) * 8 :, :]
    index = lax.broadcasted_iota(jnp.int32, bias.shape, 0)
    bias_ref[...] = jnp.sum(jnp.where(index == tile, bias, 0.0), axis=0, keepdims=True)[:, 0:CH]
    width = 2 * CH
    turned = jnp.concatenate([total, jnp.zeros((width - BLOCKS * 8, width), F32)], axis=0).T
    for block in range(BLOCKS - 1):
        lined = turned if block == 0 else pltpu.roll(turned, width - block * 8, 1)
        for half in range(2):
            piece = lined[half * CH : (half + 1) * CH, :]
            if block < 8:
                tap = block // 2 * 4 + ((1, 2), (3, 0))[block % 2][half]
                strided_scr[pl.ds(tap, CH, stride=16), :] = piece
            elif (block - 8) * 2 + half < DIL_TAPS:
                dilated_scr[pl.ds((block - 8) * 2 + half, CH, stride=DIL_TAPS), :] = piece
    weights_ref[:, 0 : 16 * CH] = strided_scr[...].T[0:8, :]
    weights_ref[:, 16 * CH :] = dilated_scr[...].T[0:8, :]


def feature_kernel(pre_b_ref, wf_ref, *refs, patch):
    out_hbm, shift_scr, out_scr, sem = refs[-4:]
    side = math.isqrt(pre_b_ref.shape[1])
    near = shifted_masks(side, 1)
    merge = phase_matrix(side, True)
    run, wide = 16 * side, 4 * side
    pre_b = pre_b_ref[...]
    for s, (dr, dc) in enumerate(SHIFTS):
        shift_scr[s * CH : (s + 1) * CH, :] = shifted(pre_b, dr, dc, side, 1, near)
    phases = dot(wf_ref[...], shift_scr[...]).astype(BF16)
    runs = out_scr.shape[1] // run
    stacked = jnp.concatenate(
        [
            jnp.concatenate(
                [phases[k * CH : (k + 1) * CH, q * wide : (q + 1) * wide] for k in range(4)], axis=1
            )
            for q in range(runs)
        ],
        axis=0,
    )
    merged = dot(stacked, merge).astype(BF16)
    for q in range(runs):
        out_scr[:, q * run : (q + 1) * run] = merged[q * CH : (q + 1) * CH, :]
    copy = pltpu.make_async_copy(out_scr, out_hbm.at[patch], sem)
    copy.start()
    copy.wait()


SPACES = {"s": pltpu.SMEM, "v": pltpu.VMEM, "h": pltpu.HBM, "a": pl.ANY}


def call(kernel, outs, ins, scratch, *args, flops=0, out_space="v", aliases=None):
    args = [
        pltpu.with_memory_space_constraint(arg, pltpu.HBM) if space == "h" else arg
        for space, arg in zip(ins, args)
    ]
    return pl.pallas_call(
        kernel,
        out_shape=[jax.ShapeDtypeStruct(shape, kind) for shape, kind in outs],
        in_specs=[pl.BlockSpec(memory_space=SPACES[space]) for space in ins],
        out_specs=[pl.BlockSpec(memory_space=SPACES[out_space])] * len(outs),
        scratch_shapes=[pltpu.VMEM(*item) if isinstance(item, tuple) else item for item in scratch],
        input_output_aliases=aliases or {},
        compiler_params=pltpu.CompilerParams(vmem_limit_bytes=VMEM_LIMIT),
        cost_estimate=pl.CostEstimate(flops=flops, bytes_accessed=1 << 20, transcendentals=0),
    )(*args)


def scene_xor(x, distance):
    return lax.ppermute(x, "scene", [(i, i ^ distance) for i in range(lax.axis_size("scene"))])


def device_xor(x, scene_distance, tile_distance):
    tiles, scenes = lax.axis_size("tile"), lax.axis_size("scene")
    pairs = [
        (s * tiles + t, (s ^ scene_distance) * tiles + (t ^ tile_distance))
        for s in range(scenes)
        for t in range(tiles)
    ]
    return lax.ppermute(x, ("scene", "tile"), pairs)


def reduce_anywhere(blocks, tile_owner, bias_rows):
    channels = blocks.shape[1]
    scene = lax.axis_index("scene")
    scenes, tiles = lax.axis_size("scene"), lax.axis_size("tile")
    halves = blocks.reshape(BLOCKS, channels, 2, channels)
    strided, dilated = [None] * 16, []
    for block in range(8):
        for half in range(2):
            strided[block // 2 * 4 + ((1, 2), (3, 0))[block % 2][half]] = halves[block, :, half]
    for tap in range(DIL_TAPS):
        dilated.append(halves[8 + tap // 2, :, tap % 2])
    row = jnp.concatenate(
        [
            jnp.stack(strided, axis=-1).reshape(channels, 16 * channels),
            jnp.stack(dilated, axis=-1).reshape(channels, DIL_TAPS * channels),
        ],
        axis=1,
    )
    hit = jnp.arange(2, dtype=jnp.int32)[:, None, None] == scene % 2
    term = jnp.where(hit, row[None], 0.0).reshape(2 * channels, 25 * channels)
    weights = lax.psum(lax.psum_scatter(term, "scene", scatter_dimension=0, tiled=True), "tile")
    tile_id = lax.dynamic_index_in_dim(tile_owner, scene, 0, keepdims=False)
    owned = jnp.arange(scenes * tiles * bias_rows, dtype=jnp.int32) == tile_id
    bias = jnp.where(owned[:, None], halves[BLOCKS - 1, 0, 0][None, :], 0.0)
    return weights, lax.psum_scatter(bias, ("scene", "tile"), scatter_dimension=0, tiled=True)


def local(
    features_in,
    strided_weights,
    dilated_weights,
    tile_bias,
    cost_cotangent,
    footprint_pairing,
    valid_counts,
    tile_owner,
):
    features, own_cot = features_in[0], cost_cotangent[0]
    patches, channels, cells_in = features.shape
    cells = own_cot.shape[1]
    scenes, tiles = lax.axis_size("scene"), lax.axis_size("tile")
    weight_scale = 1.0 / math.sqrt(scenes * patches * tiles * cells)
    bias_scale = 1.0 / math.sqrt(patches * tiles * cells)
    bias_rows = tile_bias.shape[0] // (scenes * tiles)
    grid = (channels, cells)
    payload = (cells * channels // 128 + 16, 128)
    chunked = scenes == 16 and tiles == 2 and patches == 2 and bias_rows == 1
    wscr = ((16 * channels, 2 * channels), F32)
    im_scr = ((16 * channels, cells), BF16)
    patch_outs = [((4 * channels, cells), BF16), (grid, F32), (grid, BF16), (payload, BF16)]
    first_outs = patch_outs + [
        ((channels, 16 * channels), BF16),
        ((channels, 9 * channels), BF16),
        ((channels, 128), F32),
    ]
    *part, w_strided, w_dilated, bias_col = call(
        first_kernel,
        first_outs,
        "hhhhhh",
        [
            ((channels, cells_in), BF16),
            (strided_weights.shape[1:], BF16),
            (dilated_weights.shape[1:], BF16),
            (own_cot.shape, BF16),
            (tile_bias.shape, F32),
            pltpu.SMEM(tile_owner.shape, jnp.int32),
            wscr,
            im_scr,
            pltpu.SemaphoreType.DMA((6,)),
        ],
        tile_owner, features, strided_weights, dilated_weights, tile_bias, own_cot,
        flops=10**9,
    )
    parts, far, near = [part], [device_xor(part[3], 1, 1)], [scene_xor(part[3], 1)]
    for p in range(1, patches):
        part = call(
            functools.partial(later_kernel, patch=p),
            patch_outs,
            "vvvvv" + "a" * len(near),
            [im_scr],
            features, own_cot, w_strided, w_dilated, bias_col, *near,
            flops=10**9,
        )
        parts.append(part)
        far.append(device_xor(part[3], 1, 1))
        near.append(scene_xor(part[3], 1))
    phases, pre, act, send = zip(*parts)
    *slope, w_feature, w_act, select, place = call(
        functools.partial(prepare_kernel, bias_rows=bias_rows),
        [(grid, F32)] * patches
        + [
            ((4 * channels, 9 * channels), BF16),
            ((channels, 9 * channels), BF16),
            ((16, 128), F32),
            ((128, 128), F32),
        ],
        "sssvv" + "v" * patches,
        [wscr],
        footprint_pairing, valid_counts, tile_owner, strided_weights, dilated_weights, *pre,
        flops=10**9,
    )
    block_shape = ((BLOCKS, channels, 128), F32)
    half_shape = ((4, BLOCKS * 8, 128), BF16)
    scratch = [
        ((9 * channels, cells), BF16),
        ((9 * channels, 128), F32),
        ((9 * channels, 4 * channels), F32),
    ]
    results = call(
        functools.partial(
            backward_kernel, patches=patches, chunked=chunked, weight_scale=weight_scale, bias_scale=bias_scale
        ),
        [(grid, BF16)] * patches + ([half_shape] * 2 if chunked else [block_shape]),
        "v" * (2 + 6 * patches),
        scratch + ([block_shape] if chunked else []),
        select, w_act, *near, *far, *send, *act, *slope, *phases,
        flops=10**9,
    )
    pre_b, grads = results[:patches], results[patches:]

    def features_of(p, base):
        return call(
            functools.partial(feature_kernel, patch=p),
            [(features.shape, BF16)],
            "vv" if base is None else "vvh",
            [
                ((9 * channels, cells), BF16),
                ((channels, cells_in), BF16),
                pltpu.SemaphoreType.DMA,
            ],
            *((pre_b[p], w_feature) if base is None else (pre_b[p], w_feature, base)),
            flops=10**9,
            out_space="h",
            aliases=None if base is None else {2: 0},
        )[0]

    if not chunked:
        feature_grads = None
        for p in range(patches):
            feature_grads = features_of(p, feature_grads)
        return (feature_grads[None],) + reduce_anywhere(grads[0], tile_owner, bias_rows)
    keep, give = grads
    got = scene_xor(give, 1)
    stage = ((2 * BLOCKS * 8, 128), BF16)
    own, by_y, by_z, by_zy = call(spread_kernel, [stage] * 4, "vvv", [], place, keep, got)
    by_zy, by_z, by_y = scene_xor(by_zy, 6), scene_xor(by_z, 4), scene_xor(by_y, 2)
    feature_grads = features_of(0, None)
    feature_grads, own = lax.optimization_barrier((feature_grads, own))
    chunk = (BLOCKS * 8, 128)
    kept, stay, cross = call(
        join_kernel,
        [(chunk, F32), (chunk, BF16), (chunk, BF16)],
        "vvvv",
        [],
        own, by_y, by_z, by_zy,
    )
    by_zx, by_z, by_x = device_xor(cross, 8, 1), device_xor(cross, 8, 0), device_xor(stay, 0, 1)
    feature_grads = features_of(1, feature_grads)
    grad_weights, grad_bias = call(
        finish_kernel,
        [((8, 25 * channels), F32), ((1, channels), F32)],
        "vvvv",
        [((16 * channels, 128), F32), ((9 * channels, 128), F32)],
        kept, by_zx, by_z, by_x,
    )
    return (feature_grads[None], grad_weights, grad_bias)


def solution(mesh):
    return jax.shard_map(
        local,
        mesh=mesh,
        in_specs=(
            P("scene", "tile", None, None),
            P(),
            P(),
            P(),
            P("scene", "tile", None),
            P(),
            P(),
            P(),
        ),
        out_specs=(P("scene", "tile", None, None), P("scene", None), P(("scene", "tile"), None)),
        check_vma=False,
    )
```

```python
import functools
import math

import jax
import jax.numpy as jnp
from jax import lax
from jax.experimental import pallas as pl
from jax.experimental.pallas import tpu as pltpu
from jax.sharding import PartitionSpec as P

CH = 64
ROW_TAPS = 4
DIL_TAPS = 9
BLOCKS = 14
SHIFTS = [(dr, dc) for dr in (-1, 0, 1) for dc in (-1, 0, 1)]
F32 = jnp.float32
BF16 = jnp.bfloat16
VMEM_LIMIT = 24 * 1024 * 1024


def shift_index(dr, dc):
    return (dr + 1) * 3 + dc + 1


def dot(a, b):
    return lax.dot_general(a, b, (((1,), (0,)), ((), ())), preferred_element_type=F32)


def dot_nt(a, b):
    return lax.dot_general(a, b, (((1,), (1,)), ((), ())), preferred_element_type=F32)


def shifted_masks(side, reach):
    cell = lax.broadcasted_iota(jnp.int32, (1, side * side), 1)
    row, col = cell // side, cell % side
    masks = {}
    for dr, dc in SHIFTS:
        ok = (
            (row + dr * reach >= 0)
            & (row + dr * reach < side)
            & (col + dc * reach >= 0)
            & (col + dc * reach < side)
        )
        masks[dr, dc] = ok.astype(F32).astype(BF16)
    return masks


def shifted(x, dr, dc, side, reach, masks):
    if dr == 0 and dc == 0:
        return x
    cells = side * side
    return pltpu.roll(x, (-(dr * side + dc) * reach) % cells, 1) * masks[dr, dc]


def phase_matrix(side, transposed):
    size = 16 * side
    dims = (size, size)
    source = lax.broadcasted_iota(jnp.int32, dims, 1 if transposed else 0)
    target = lax.broadcasted_iota(jnp.int32, dims, 0 if transposed else 1)
    phase, cell = target // (4 * side), target % (4 * side)
    row, col = cell // side, cell % side
    wanted = (2 * row + phase // 2) * (2 * side) + 2 * col + phase % 2
    return jnp.where(source == wanted, 1.0, 0.0).astype(BF16)


TAP_LINES = {0: (1, -1), 1: (0, 0), 2: (1, 0), 3: (0, 1)}


def tap_matrices(weight, taps, scratch):
    wide = weight.astype(F32)
    scratch[0 : CH * taps, 0:CH] = wide.T
    return [scratch[pl.ds(tap, CH, stride=taps), 0:CH] for tap in range(taps)]


def forward_patch(x_ref, cot, w_strided, w_dilated, bias_col, ph_ref, pre_ref, act_ref, send_ref, im_scr):
    side = math.isqrt(x_ref.shape[1]) // 2
    run, lanes = 16 * side, side * side // 128
    split = phase_matrix(side, False)
    near, far = shifted_masks(side, 1), shifted_masks(side, 2)
    runs = x_ref.shape[1] // run
    stacked = jnp.concatenate([x_ref[:, q * run : (q + 1) * run] for q in range(runs)], axis=0)
    parts = dot(stacked, split).astype(BF16)
    for q in range(runs):
        for phase in range(4):
            ph_ref[phase * CH : (phase + 1) * CH, q * 4 * side : (q + 1) * 4 * side] = parts[
                q * CH : (q + 1) * CH, phase * 4 * side : (phase + 1) * 4 * side
            ]
    for rt in range(4):
        for ct in range(4):
            (pr, dr), (pc, dc) = TAP_LINES[rt], TAP_LINES[ct]
            phase, tap = pr * 2 + pc, rt * 4 + ct
            im_scr[tap * CH : (tap + 1) * CH, :] = shifted(
                ph_ref[phase * CH : (phase + 1) * CH, :], dr, dc, side, 1, near
            )
    pre = dot(w_strided, im_scr[...]) + bias_col
    pre_ref[...] = pre
    act = (pre * (1.0 / (1.0 + jnp.exp(-pre)))).astype(BF16)
    act_ref[...] = act
    for tap, (dr, dc) in enumerate(SHIFTS):
        im_scr[tap * CH : (tap + 1) * CH, :] = shifted(act, dr, dc, side, 2, far)
    out = dot(w_dilated, im_scr[0 : DIL_TAPS * CH, :]).astype(BF16)
    for lane in range(lanes):
        send_ref[lane * CH : (lane + 1) * CH, :] = out[:, lane * 128 : (lane + 1) * 128]
    rows = [cot[:, lane * 128 : (lane + 1) * 128] for lane in range(lanes)]
    rows.append(jnp.zeros((16 - lanes, 128), F32))
    send_ref[lanes * CH :, :] = jnp.concatenate(rows, axis=0).astype(BF16)


def first_kernel(
    owner_hbm, x_hbm, ws_hbm, wd_hbm, bias_hbm, cot_hbm,
    ph_ref, pre_ref, act_ref, send_ref, strided_ref, dilated_ref, bias_ref,
    x_ref, ws_ref, wd_ref, cot_ref, table_ref, owner_ref, wscr, im_scr, sems,
):
    scene = lax.axis_index("scene")
    branch = scene % 2
    copies = [
        pltpu.make_async_copy(source, target, sems.at[i])
        for i, (source, target) in enumerate(
            [
                (x_hbm.at[0], x_ref),
                (ws_hbm.at[branch], ws_ref),
                (wd_hbm.at[branch], wd_ref),
                (owner_hbm, owner_ref),
                (bias_hbm, table_ref),
                (cot_hbm, cot_ref),
            ]
        )
    ]
    for copy in copies:
        copy.start()
    for copy in copies:
        copy.wait()
    mats = tap_matrices(ws_ref[...], 16, wscr)
    strided_ref[...] = jnp.concatenate(mats, axis=0).T.astype(BF16)
    mats = tap_matrices(wd_ref[...], 9, wscr)
    dilated_ref[...] = jnp.concatenate(mats, axis=0).T.astype(BF16)
    bias_row = table_ref[pl.ds(owner_ref[scene], 1), :]
    bias_ref[...] = jnp.broadcast_to(jnp.broadcast_to(bias_row, (8, CH)).T[:, 0:1], (CH, 128))
    forward_patch(
        x_ref, cot_ref[...].astype(F32)[0:1, :], strided_ref[...], dilated_ref[...], bias_ref[:, 0:1],
        ph_ref, pre_ref, act_ref, send_ref, im_scr,
    )


def later_kernel(
    x_ref, cot_ref, w_strided_ref, w_dilated_ref, bias_ref, sent_ref,
    ph_ref, pre_ref, act_ref, send_ref, both_ref, im_scr,
):
    forward_patch(
        x_ref.at[1], cot_ref[...].astype(F32)[1:2, :], w_strided_ref[...], w_dilated_ref[...],
        bias_ref[:, 0:1], ph_ref, pre_ref, act_ref, send_ref, im_scr,
    )
    both_ref[0] = sent_ref[...]
    both_ref[1] = send_ref[...]


def prepare_kernel(
    pairing_hbm, valid_hbm, owner_hbm, ws_ref, wd_ref, *refs, bias_rows
):
    pre_refs, act_refs, ph_refs, send_refs = (refs[2 * k : 2 * k + 2] for k in range(4))
    (
        slope_first, slope_second, act_first, act_second, ph_first, ph_second,
        wf_ref, wt_ref, select_ref, place_ref, cot_ref,
        pairing_ref, valid_ref, owner_ref, wscr, sems,
    ) = refs[8:]
    copies = [
        pltpu.make_async_copy(source, target, sems.at[i])
        for i, (source, target) in enumerate(
            [(pairing_hbm, pairing_ref), (valid_hbm, valid_ref), (owner_hbm, owner_ref)]
        )
    ]
    for copy in copies:
        copy.start()
    scene, tile = lax.axis_index("scene"), lax.axis_index("tile")
    branch, pair = scene % 2, scene // 2
    mats = tap_matrices(ws_ref[branch], 16, wscr)
    blocks = {}
    for rt in range(4):
        for ct in range(4):
            (pr, dr), (pc, dc) = TAP_LINES[rt], TAP_LINES[ct]
            blocks[pr * 2 + pc, shift_index(-dr, -dc)] = mats[rt * 4 + ct]
    zero = jnp.zeros((CH, CH), F32)
    for phase in range(4):
        row = [blocks.get((phase, s), zero) for s in range(9)]
        wf_ref[phase * CH : (phase + 1) * CH, :] = jnp.concatenate(row, axis=1).astype(BF16)
    mats = tap_matrices(wd_ref[branch], 9, wscr)
    wt_ref[...] = jnp.concatenate(mats[::-1], axis=1).astype(BF16)
    slopes = []
    for pre_ref in pre_refs:
        pre = pre_ref[...]
        gate = 1.0 / (1.0 + jnp.exp(-pre))
        slopes.append(gate * (1.0 + pre * (1.0 - gate)))
    for copy in copies:
        copy.wait()
    total = pairing_ref.shape[0]
    matches = []
    for p in range(2):
        position = tile * 2 + p
        matched, inverse = pairing_ref[position, pair], jnp.int32(0)
        for i in range(total):
            inverse = inverse + jnp.where(pairing_ref[i, pair] == position, i, 0)
        matched = jnp.where(branch == 0, matched, inverse)
        matches.append(jnp.where(matched // 2 == tile, 0, 2) + matched % 2)
    swapped = matches[0] == 3
    slope_first[...] = jnp.where(swapped, slopes[1], slopes[0])
    slope_second[...] = jnp.where(swapped, slopes[0], slopes[1])
    for first, second, pairs in ((act_first, act_second, act_refs), (ph_first, ph_second, ph_refs)):
        first[...] = jnp.where(swapped, pairs[1][...], pairs[0][...])
        second[...] = jnp.where(swapped, pairs[0][...], pairs[1][...])
    rows = send_refs[0].shape[0] - 16
    cots = [ref[rows:, :].astype(F32) for ref in send_refs]
    cot_ref[0:16, :] = jnp.where(swapped, cots[1], cots[0])
    cot_ref[16:32, :] = jnp.where(swapped, cots[0], cots[1])
    row = lax.broadcasted_iota(jnp.int32, select_ref.shape, 0)
    select = jnp.zeros(select_ref.shape, F32)
    for p in range(2):
        position = jnp.where(swapped, 1 - p, p)
        live = jnp.where(tile * 2 + p < valid_ref[pair], 8 + position, -1)
        select = jnp.where((row == position * 4 + matches[p]) | (row == live), 1.0, select)
    select_ref[...] = jnp.where(row == jnp.where(swapped, 10, -1), 1.0, select)
    row = lax.broadcasted_iota(jnp.int32, place_ref.shape, 0)
    here = scene // 2 % 4
    place = jnp.zeros(place_ref.shape, F32)
    for k, source in enumerate((scene, scene ^ 1)):
        owner = owner_ref[source]
        target = owner // (2 * bias_rows)
        half = jnp.where(target // 8 == branch, 0, 1)
        wanted = k * 64 + ((target // 2 % 4) ^ here) * 16 + half * 8 + owner % (2 * bias_rows)
        place = jnp.where(row == jnp.where(target % 2 == branch, wanted, -1), 1.0, place)
    place_ref[...] = place


def strided_product(pre_b, ph_ref, shift_scr):
    side = math.isqrt(pre_b.shape[1])
    near = shifted_masks(side, 1)
    for s, (dr, dc) in enumerate(SHIFTS):
        shift_scr[s * CH : (s + 1) * CH, :] = shifted(pre_b, dr, dc, side, 1, near)
    return dot_nt(shift_scr[...], ph_ref[...])


def backward_patch(position, candidates, select_ref, cot_ref, wt_ref, act_ref, slope_ref, shift_scr):
    side = math.isqrt(act_ref.shape[1])
    lanes = side * side // 128
    far = shifted_masks(side, 2)
    partner = None
    for k, payload in enumerate(candidates):
        term = payload * select_ref[position * 4 + k : position * 4 + k + 1, :].astype(BF16)
        partner = term if partner is None else partner + term
    live = select_ref[8 + position : 9 + position, :]
    signal = (cot_ref[position * 16 : position * 16 + 16, :] + partner[lanes * CH :, :].astype(F32)) * live
    out_grad = jnp.concatenate(
        [
            (signal[j : j + 1, :] * partner[j * CH : (j + 1) * CH, :].astype(F32)).astype(BF16)
            for j in range(lanes)
        ],
        axis=1,
    )
    for tap, (dr, dc) in enumerate(SHIFTS):
        shift_scr[tap * CH : (tap + 1) * CH, :] = shifted(out_grad, dr, dc, side, 2, far)
    act_grad = dot(wt_ref[...], shift_scr[...])
    act = act_ref[...]
    dilated = dot_nt(shift_scr[...], jnp.concatenate([act, act], axis=0))
    pre_grad = act_grad * slope_ref[...]
    bias = jnp.sum(pre_grad, axis=1, keepdims=True)
    return pre_grad.astype(BF16), bias, dilated


def backward_first_kernel(
    far0_ref, near_ref, select_ref, cot_ref, wt_ref, act_ref, slope_ref, ph_ref,
    pre_b_ref, bias_ref, dilated_ref, strided_ref, shift_scr,
):
    pre_b, bias, dilated = backward_patch(
        0, (near_ref[0], near_ref[1], far0_ref[...]), select_ref, cot_ref, wt_ref, act_ref, slope_ref, shift_scr
    )
    pre_b_ref[...] = pre_b
    bias_ref[...] = jnp.broadcast_to(bias, bias_ref.shape)
    dilated_ref[...] = dilated
    strided_ref[...] = strided_product(pre_b, ph_ref, shift_scr)


def backward_second_kernel(
    far1_ref, far0_ref, near_ref, select_ref, cot_ref, wt_ref, act_ref, slope_ref, ph_ref,
    other_ref, bias_ref, dilated_ref, strided_ref, *refs, chunked,
):
    pre_b0_ref, pre_b1_ref = refs[:2]
    if chunked:
        keep_ref, give_ref, shift_scr, dil_scr, grad_acc, grad_scr = refs[2:]
    else:
        grad_scr, bias_out_ref, shift_scr, dil_scr, grad_acc = refs[2:]
    pre_b, bias, dilated = backward_patch(
        1, (near_ref[0], near_ref[1], far0_ref[...], far1_ref[...]),
        select_ref, cot_ref, wt_ref, act_ref, slope_ref, shift_scr,
    )
    swapped = select_ref[10:11, 0:1].astype(BF16)
    straight = 1.0 - swapped
    pre_b0_ref[...] = other_ref[...] * straight + pre_b * swapped
    pre_b1_ref[...] = other_ref[...] * swapped + pre_b * straight
    dil_scr[...] = dilated + dilated_ref[...]
    grad_acc[...] = strided_product(pre_b, ph_ref, shift_scr) + strided_ref[...]
    lower = lax.broadcasted_iota(jnp.int32, (CH, 2 * CH), 1) < CH

    def strided_piece(pr, shift):
        return grad_acc[shift * CH : (shift + 1) * CH, pr * 2 * CH : (pr + 1) * 2 * CH]

    for rt in range(4):
        pr, dr = TAP_LINES[rt]
        for k in range(2):
            low_dc, high_dc = (0, 0) if k == 0 else (1, -1)
            low = strided_piece(pr, shift_index(-dr, -low_dc))
            high = strided_piece(pr, shift_index(-dr, -high_dc))
            grad_scr[rt * 2 + k] = low if k == 0 else jnp.where(lower, low, high)
    for j in range(5):
        low = dil_scr[(8 - 2 * j) * CH : (9 - 2 * j) * CH, :]
        high = dil_scr[(7 - 2 * j) * CH : (8 - 2 * j) * CH, :] if j < 4 else jnp.zeros_like(low)
        grad_scr[8 + j] = jnp.where(lower, low, high)
    bias_wide = (bias + bias_ref[...]).T[0:8, :]
    bias_wide = jnp.concatenate([bias_wide, jnp.zeros_like(bias_wide)], axis=1)
    if not chunked:
        bias_out_ref[...] = bias_wide
        return
    scene = lax.axis_index("scene")
    here, branch = scene // 2 % 4, scene % 2
    for ref, core in ((keep_ref, branch), (give_ref, 1 - branch)):
        for d in range(4):
            row = pl.multiple_of(((here ^ d) * 2 + core) * 8, 8)
            pieces = [grad_scr[block, pl.ds(row, 8), :] for block in range(BLOCKS - 1)]
            ref[d] = jnp.concatenate(pieces + [bias_wide], axis=0).astype(BF16)


def spread_kernel(place_ref, keep_ref, got_ref, *out_refs):
    rows = keep_ref.shape[1]
    top = lax.broadcasted_iota(jnp.int32, (16, 128), 0) < 8
    mine = keep_ref[0, rows - 16 :, :].astype(F32)[8:9, :]
    theirs = got_ref[0, rows - 16 :, :].astype(F32)[8:9, :]
    for d, out_ref in enumerate(out_refs):
        for half, ref in enumerate((keep_ref, got_ref)):
            at = d * 16 + half * 8
            bias = place_ref[at : at + 8, :] * mine + place_ref[64 + at : 72 + at, :] * theirs
            last = ref[d, rows - 16 :, :].astype(F32)
            last = jnp.where(top, last, jnp.concatenate([bias, bias], axis=0))
            out_ref[half * rows : (half + 1) * rows - 16, :] = ref[d, : rows - 16, :]
            out_ref[(half + 1) * rows - 16 : (half + 1) * rows, :] = last.astype(BF16)


def join_kernel(own_ref, a_ref, b_ref, c_ref, keep_ref, stay_ref, cross_ref):
    scene = lax.axis_index("scene")
    rows = keep_ref.shape[0]
    total = (own_ref[...].astype(F32) + a_ref[...].astype(F32)) + (
        b_ref[...].astype(F32) + c_ref[...].astype(F32)
    )
    mine, theirs = total[:rows, :], total[rows:, :]
    first = scene // 8 == scene % 2
    kept = jnp.where(first, mine, theirs)
    keep_ref[...] = kept
    stay_ref[...] = kept.astype(BF16)
    cross_ref[...] = jnp.where(first, theirs, mine).astype(BF16)


def finish_kernel(
    own_ref, a_ref, b_ref, c_ref, late_ref, features_in_hbm, weights_hbm, bias_hbm, features_hbm,
    weights_ref, bias_ref, tap_scr, turn_scr, dilated_scr, sems, *, weight_scale, bias_scale,
):
    tile = lax.axis_index("tile")
    late = pltpu.make_async_copy(late_ref, features_hbm.at[1], sems.at[0])
    late.start()
    total = (own_ref[...] + a_ref[...].astype(F32)) + (b_ref[...].astype(F32) + c_ref[...].astype(F32))
    bias = total[(BLOCKS - 1) * 8 :, :] * bias_scale
    index = lax.broadcasted_iota(jnp.int32, bias.shape, 0)
    bias_ref[...] = jnp.sum(jnp.where(index == tile, bias, 0.0), axis=0, keepdims=True)[:, 0:CH]
    bias_out = pltpu.make_async_copy(bias_ref, bias_hbm, sems.at[1])
    bias_out.start()
    total = total * weight_scale
    other = pltpu.roll(total, CH, 1)
    for block in range(8):
        for half, source in enumerate((total, other)):
            tap = block // 2 * 4 + ((1, 2), (3, 0))[block % 2][half]
            tap_scr[pl.ds(tap, 8, stride=16), :] = source[block * 8 : block * 8 + 8, :]
    lines = tap_scr[...].T[0:CH, :].reshape(8, 8, 128)
    sub = lax.broadcasted_iota(jnp.int32, lines.shape, 1)
    chunk = lax.broadcasted_iota(jnp.int32, lines.shape, 2) // 16
    for step in (1, 2, 4):
        up = pltpu.roll(pltpu.roll(lines, 8 - step, 1), 16 * step, 2)
        down = pltpu.roll(pltpu.roll(lines, step, 1), 128 - 16 * step, 2)
        high, wide = sub // step % 2, chunk // step % 2
        lines = jnp.where(high == wide, lines, jnp.where(high == 0, up, down))
    for block in range(8):
        weights_ref[:, block * 128 : (block + 1) * 128] = lines[block]
    strided_part, dilated_part = pl.ds(0, 16 * CH), pl.ds(16 * CH, DIL_TAPS * CH)
    strided_out = pltpu.make_async_copy(weights_ref.at[:, strided_part], weights_hbm.at[:, strided_part], sems.at[2])
    strided_out.start()
    turn_scr[0:40, :] = total[64:104, :]
    turned = turn_scr[...].T
    for tap in range(DIL_TAPS):
        half = tap % 2
        dilated_scr[pl.ds(tap, CH, stride=DIL_TAPS), :] = turned[half * CH : (half + 1) * CH, :]
    spread = dilated_scr[...].T
    tap = lax.broadcasted_iota(jnp.int32, (8, DIL_TAPS * CH), 1) % DIL_TAPS
    result = spread[0:8, :]
    for j in range(1, 5):
        result = jnp.where(tap // 2 == j, spread[8 * j : 8 * j + 8, :], result)
    weights_ref[:, 16 * CH :] = result
    dilated_out = pltpu.make_async_copy(weights_ref.at[:, dilated_part], weights_hbm.at[:, dilated_part], sems.at[3])
    dilated_out.start()
    for copy in (late, bias_out, strided_out, dilated_out):
        copy.wait()


def feature_patch(pre_b_ref, wf_ref, out_ref, shift_scr):
    side = math.isqrt(pre_b_ref.shape[1])
    near = shifted_masks(side, 1)
    merge = phase_matrix(side, True)
    run, wide = 16 * side, 4 * side
    pre_b = pre_b_ref[...]
    for s, (dr, dc) in enumerate(SHIFTS):
        shift_scr[s * CH : (s + 1) * CH, :] = shifted(pre_b, dr, dc, side, 1, near)
    phases = dot(wf_ref[...], shift_scr[...]).astype(BF16)
    runs = out_ref.shape[1] // run
    stacked = jnp.concatenate(
        [
            jnp.concatenate(
                [phases[k * CH : (k + 1) * CH, q * wide : (q + 1) * wide] for k in range(4)], axis=1
            )
            for q in range(runs)
        ],
        axis=0,
    )
    merged = dot(stacked, merge).astype(BF16)
    for q in range(runs):
        out_ref[:, q * run : (q + 1) * run] = merged[q * CH : (q + 1) * CH, :]


def feature_first_kernel(pre_b_ref, wf_ref, out_ref, shift_scr):
    feature_patch(pre_b_ref, wf_ref, out_ref, shift_scr)


def feature_second_kernel(pre_b_ref, wf_ref, first_ref, out_ref, features_hbm, shift_scr, sem):
    copy = pltpu.make_async_copy(first_ref, features_hbm.at[0], sem)
    copy.start()
    feature_patch(pre_b_ref, wf_ref, out_ref, shift_scr)
    copy.wait()


SPACES = {"s": pltpu.SMEM, "v": pltpu.VMEM, "h": pltpu.HBM, "a": pl.ANY}


def call(kernel, outs, ins, scratch, *args, flops=0, out_spaces="", aliases=None):
    args = [
        pltpu.with_memory_space_constraint(arg, pltpu.HBM) if space == "h" else arg
        for space, arg in zip(ins, args)
    ]
    return pl.pallas_call(
        kernel,
        out_shape=[jax.ShapeDtypeStruct(shape, kind) for shape, kind in outs],
        in_specs=[pl.BlockSpec(memory_space=SPACES[space]) for space in ins],
        out_specs=[pl.BlockSpec(memory_space=SPACES[space]) for space in out_spaces or "v" * len(outs)],
        scratch_shapes=[pltpu.VMEM(*item) if isinstance(item, tuple) else item for item in scratch],
        input_output_aliases=aliases or {},
        compiler_params=pltpu.CompilerParams(vmem_limit_bytes=VMEM_LIMIT),
        cost_estimate=pl.CostEstimate(flops=flops, bytes_accessed=1 << 20, transcendentals=0),
    )(*args)


def device_pairs(x, pairs):
    tiles = lax.axis_size("tile")
    flat = [(source[0] * tiles + source[1], target[0] * tiles + target[1]) for source, target in pairs]
    return lax.ppermute(x, ("scene", "tile"), flat)


def scene_xor(x, distance):
    return lax.ppermute(x, "scene", [(i, i ^ distance) for i in range(lax.axis_size("scene"))])


def device_xor(x, scene_distance, tile_distance):
    scenes, tiles = range(lax.axis_size("scene")), range(lax.axis_size("tile"))
    return device_pairs(
        x, [((s, t), (s ^ scene_distance, t ^ tile_distance)) for s in scenes for t in tiles]
    )


def reduce_anywhere(blocks, bias_row, tile_owner, bias_rows, weight_scale, bias_scale):
    channels = blocks.shape[1]
    scene = lax.axis_index("scene")
    scenes, tiles = lax.axis_size("scene"), lax.axis_size("tile")
    halves = blocks.reshape(BLOCKS - 1, channels, 2, channels)
    strided, dilated = [None] * 16, []
    for block in range(8):
        for half in range(2):
            strided[block // 2 * 4 + ((1, 2), (3, 0))[block % 2][half]] = halves[block, :, half]
    for tap in range(DIL_TAPS):
        dilated.append(halves[8 + tap // 2, :, tap % 2])
    row = jnp.concatenate(
        [
            jnp.stack(strided, axis=-1).reshape(channels, 16 * channels),
            jnp.stack(dilated, axis=-1).reshape(channels, DIL_TAPS * channels),
        ],
        axis=1,
    )
    hit = jnp.arange(2, dtype=jnp.int32)[:, None, None] == scene % 2
    term = jnp.where(hit, row[None] * weight_scale, 0.0).reshape(2 * channels, 25 * channels)
    weights = lax.psum(lax.psum_scatter(term, "scene", scatter_dimension=0, tiled=True), "tile")
    tile_id = lax.dynamic_index_in_dim(tile_owner, scene, 0, keepdims=False)
    owned = jnp.arange(scenes * tiles * bias_rows, dtype=jnp.int32) == tile_id
    bias = jnp.where(owned[:, None], bias_row[None, :channels] * bias_scale, 0.0)
    return weights, lax.psum_scatter(bias, ("scene", "tile"), scatter_dimension=0, tiled=True)


def local(
    features_in,
    strided_weights,
    dilated_weights,
    tile_bias,
    cost_cotangent,
    footprint_pairing,
    valid_counts,
    tile_owner,
):
    features, own_cot = features_in[0], cost_cotangent[0]
    patches, channels, cells_in = features.shape
    cells = own_cot.shape[1]
    scenes, tiles = lax.axis_size("scene"), lax.axis_size("tile")
    weight_scale = 1.0 / math.sqrt(scenes * patches * tiles * cells)
    bias_scale = 1.0 / math.sqrt(patches * tiles * cells)
    bias_rows = tile_bias.shape[0] // (scenes * tiles)
    grid = (channels, cells)
    payload = (cells * channels // 128 + 16, 128)
    chunked = scenes == 16 and tiles == 2 and patches == 2 and bias_rows == 1
    wscr = ((16 * channels, 2 * channels), F32)
    im_scr = ((16 * channels, cells), BF16)
    patch_outs = [((4 * channels, cells), BF16), (grid, F32), (grid, BF16), (payload, BF16)]
    first_outs = patch_outs + [
        ((channels, 16 * channels), BF16),
        ((channels, 9 * channels), BF16),
        ((channels, 128), F32),
    ]
    *part, w_strided, w_dilated, bias_col = call(
        first_kernel,
        first_outs,
        "hhhhhh",
        [
            ((channels, cells_in), BF16),
            (strided_weights.shape[1:], BF16),
            (dilated_weights.shape[1:], BF16),
            (own_cot.shape, BF16),
            (tile_bias.shape, F32),
            pltpu.SMEM(tile_owner.shape, jnp.int32),
            wscr,
            im_scr,
            pltpu.SemaphoreType.DMA((6,)),
        ],
        tile_owner, features, strided_weights, dilated_weights, tile_bias, own_cot,
        flops=10**9,
    )
    far = [device_xor(part[3], 1, 1)]
    *late, both = call(
        later_kernel,
        patch_outs + [((2,) + payload, BF16)],
        "vvvvvv",
        [im_scr],
        features, own_cot, w_strided, w_dilated, bias_col, part[3],
        flops=10**10,
    )
    far.append(device_xor(late[3], 1, 1))
    near = scene_xor(both, 1)
    phases, pre, act, send = zip(part, late)
    ordered = [(grid, F32)] * 2 + [(grid, BF16)] * 2 + [((4 * channels, cells), BF16)] * 2
    *both, w_feature, w_act, select, place, cots = call(
        functools.partial(prepare_kernel, bias_rows=bias_rows),
        ordered
        + [
            ((4 * channels, 9 * channels), BF16),
            ((channels, 9 * channels), BF16),
            ((16, 128), F32),
            ((128, 128), F32),
            ((32, 128), F32),
        ],
        "hhhvvvvvvvvvv",
        [
            pltpu.SMEM(footprint_pairing.shape[::-1], jnp.int32),
            pltpu.SMEM(valid_counts.shape, jnp.int32),
            pltpu.SMEM(tile_owner.shape, jnp.int32),
            wscr,
            pltpu.SemaphoreType.DMA((3,)),
        ],
        footprint_pairing.T, valid_counts, tile_owner, strided_weights, dilated_weights,
        *pre, *act, *phases, *send,
        flops=10**10,
    )
    slope, act, phases = both[0:2], both[2:4], both[4:6]
    shift_scr = ((9 * channels, cells), BF16)
    sums = [((9 * channels, 128), F32), ((9 * channels, 4 * channels), F32)]
    first = call(
        backward_first_kernel,
        [(grid, BF16), ((channels, 128), F32)] + sums,
        "v" * 8,
        [shift_scr],
        far[0], near, select, cots, w_act, act[0], slope[0], phases[0],
        flops=10**9,
    )
    block_shape = ((BLOCKS - 1, channels, 128), F32)
    half_shape = ((4, BLOCKS * 8, 128), BF16)
    results = call(
        functools.partial(backward_second_kernel, chunked=chunked),
        [(grid, BF16)] * 2 + ([half_shape] * 2 if chunked else [block_shape, ((8, 128), F32)]),
        "v" * 13,
        [shift_scr] + sums + ([block_shape] if chunked else []),
        far[1], far[0], near, select, cots, w_act, act[1], slope[1], phases[1], *first,
        flops=10**9,
    )
    pre_b, grads = results[:2], results[2:]
    feature_shape = ((channels, cells_in), BF16)
    if chunked:
        keep, give = grads
        got = scene_xor(give, 1)
        stage = ((2 * BLOCKS * 8, 128), BF16)
        own, by_y, by_z, by_zy = call(spread_kernel, [stage] * 4, "vvv", [], place, keep, got)
        by_zy, by_z, by_y = scene_xor(by_zy, 6), scene_xor(by_z, 4), scene_xor(by_y, 2)
    (feature_first,) = call(
        feature_first_kernel, [feature_shape], "vv", [shift_scr], pre_b[0], w_feature, flops=10**9
    )
    chunk = (BLOCKS * 8, 128)
    if chunked:
        feature_first, own = lax.optimization_barrier((feature_first, own))
        kept, stay, cross = call(
            join_kernel, [(chunk, F32), (chunk, BF16), (chunk, BF16)], "vvvv", [], own, by_zy, by_z, by_y
        )
        by_zx, by_z, by_x = device_xor(cross, 8, 1), device_xor(cross, 8, 0), device_xor(stay, 0, 1)
    feature_last, feature_grads = call(
        feature_second_kernel,
        [feature_shape, (features.shape, BF16)],
        "vvv",
        [shift_scr, pltpu.SemaphoreType.DMA],
        pre_b[1], w_feature, feature_first,
        flops=10**9,
        out_spaces="vh",
    )
    if not chunked:
        feature_grads = feature_grads.at[1].set(feature_last)
        grad_weights, grad_bias = reduce_anywhere(
            grads[0], grads[1][0], tile_owner, bias_rows, weight_scale, bias_scale
        )
        return (feature_grads[None], grad_weights, grad_bias)
    grad_weights, grad_bias, feature_grads = call(
        functools.partial(finish_kernel, weight_scale=weight_scale, bias_scale=bias_scale),
        [((8, 25 * channels), F32), ((1, channels), F32), (features.shape, BF16)],
        "vvvvva",
        [
            ((8, 25 * channels), F32),
            ((1, channels), F32),
            ((128, 128), F32),
            ((128, 128), F32),
            ((9 * channels, 128), F32),
            pltpu.SemaphoreType.DMA((4,)),
        ],
        kept, by_zx, by_z, by_x, feature_last, feature_grads,
        out_spaces="hhh",
        aliases={5: 2},
    )
    return (feature_grads[None], grad_weights, grad_bias)


def solution(mesh):
    return jax.shard_map(
        local,
        mesh=mesh,
        in_specs=(
            P("scene", "tile", None, None),
            P(),
            P(),
            P(),
            P("scene", "tile", None),
            P(),
            P(),
            P(),
        ),
        out_specs=(P("scene", "tile", None, None), P("scene", None), P(("scene", "tile"), None)),
        check_vma=False,
    )
```

```python
import functools
import math

import jax
import jax.numpy as jnp
from jax import lax
from jax.experimental import pallas as pl
from jax.experimental.pallas import tpu as pltpu
from jax.sharding import PartitionSpec as P

CH = 64
ROW_TAPS = 4
DIL_TAPS = 9
BLOCKS = 14
SHIFTS = [(dr, dc) for dr in (-1, 0, 1) for dc in (-1, 0, 1)]
F32 = jnp.float32
BF16 = jnp.bfloat16
VMEM_LIMIT = 24 * 1024 * 1024


def shift_index(dr, dc):
    return (dr + 1) * 3 + dc + 1


def dot(a, b):
    return lax.dot_general(a, b, (((1,), (0,)), ((), ())), preferred_element_type=F32)


def dot_nt(a, b):
    return lax.dot_general(a, b, (((1,), (1,)), ((), ())), preferred_element_type=F32)


def shifted_masks(side, reach):
    cell = lax.broadcasted_iota(jnp.int32, (1, side * side), 1)
    row, col = cell // side, cell % side
    masks = {}
    for dr, dc in SHIFTS:
        ok = (
            (row + dr * reach >= 0)
            & (row + dr * reach < side)
            & (col + dc * reach >= 0)
            & (col + dc * reach < side)
        )
        masks[dr, dc] = ok.astype(F32).astype(BF16)
    return masks


def shifted(x, dr, dc, side, reach, masks):
    if dr == 0 and dc == 0:
        return x
    cells = side * side
    return pltpu.roll(x, (-(dr * side + dc) * reach) % cells, 1) * masks[dr, dc]


def phase_matrix(side, transposed):
    size = 16 * side
    dims = (size, size)
    source = lax.broadcasted_iota(jnp.int32, dims, 1 if transposed else 0)
    target = lax.broadcasted_iota(jnp.int32, dims, 0 if transposed else 1)
    phase, cell = target // (4 * side), target % (4 * side)
    row, col = cell // side, cell % side
    wanted = (2 * row + phase // 2) * (2 * side) + 2 * col + phase % 2
    return jnp.where(source == wanted, 1.0, 0.0).astype(BF16)


def halves(values, core):
    even = jnp.concatenate([values[16 * m : 16 * m + 8] for m in range(CH // 16)], axis=0)
    odd = jnp.concatenate([values[16 * m + 8 : 16 * m + 16] for m in range(CH // 16)], axis=0)
    return jnp.where(core == 0, odd, even), jnp.where(core == 0, even, odd)


TAP_LINES = {0: (1, -1), 1: (0, 0), 2: (1, 0), 3: (0, 1)}


def tap_matrices(weight, taps, scratch):
    scratch[0 : CH * taps, 0:CH] = weight.astype(F32).T
    return [scratch[pl.ds(tap, CH, stride=taps), 0:CH] for tap in range(taps)]


def forward_patch(x_ref, cot, w_strided, w_dilated, bias_col, ph_ref, pre_ref, act_ref, send_ref, im_scr):
    side = math.isqrt(x_ref.shape[1]) // 2
    run, lanes = 16 * side, side * side // 128
    split = phase_matrix(side, False)
    near, far = shifted_masks(side, 1), shifted_masks(side, 2)
    runs = x_ref.shape[1] // run
    stacked = jnp.concatenate([x_ref[:, q * run : (q + 1) * run] for q in range(runs)], axis=0)
    parts = dot(stacked, split).astype(BF16)
    for q in range(runs):
        for phase in range(4):
            ph_ref[phase * CH : (phase + 1) * CH, q * 4 * side : (q + 1) * 4 * side] = parts[
                q * CH : (q + 1) * CH, phase * 4 * side : (phase + 1) * 4 * side
            ]
    for rt in range(4):
        for ct in range(4):
            (pr, dr), (pc, dc) = TAP_LINES[rt], TAP_LINES[ct]
            phase, tap = pr * 2 + pc, rt * 4 + ct
            im_scr[tap * CH : (tap + 1) * CH, :] = shifted(
                ph_ref[phase * CH : (phase + 1) * CH, :], dr, dc, side, 1, near
            )
    pre = dot(w_strided, im_scr[...]) + bias_col
    pre_ref[...] = pre
    act = (pre * (1.0 / (1.0 + jnp.exp(-pre)))).astype(BF16)
    act_ref[...] = act
    for tap, (dr, dc) in enumerate(SHIFTS):
        im_scr[tap * CH : (tap + 1) * CH, :] = shifted(act, dr, dc, side, 2, far)
    out = dot(w_dilated, im_scr[0 : DIL_TAPS * CH, :]).astype(BF16)
    for lane in range(lanes):
        send_ref[lane * CH : (lane + 1) * CH, :] = out[:, lane * 128 : (lane + 1) * 128]
    rows = [cot[:, lane * 128 : (lane + 1) * 128] for lane in range(lanes)]
    rows.append(jnp.zeros((16 - lanes, 128), F32))
    send_ref[lanes * CH :, :] = jnp.concatenate(rows, axis=0).astype(BF16)


def first_kernel(
    owner_hbm, x_hbm, ws_hbm, wd_hbm, bias_hbm, cot_hbm,
    ph_ref, pre_ref, act_ref, send_ref, strided_ref, dilated_ref, bias_ref, cot_ref,
    x_ref, ws_ref, wd_ref, table_ref, owner_ref, wscr, im_scr, sems,
):
    scene = lax.axis_index("scene")
    branch = scene % 2
    copies = [
        pltpu.make_async_copy(source, target, sems.at[i])
        for i, (source, target) in enumerate(
            [
                (x_hbm.at[0], x_ref),
                (ws_hbm.at[branch], ws_ref),
                (wd_hbm.at[branch], wd_ref),
                (owner_hbm, owner_ref),
                (bias_hbm, table_ref),
                (cot_hbm, cot_ref),
            ]
        )
    ]
    for copy in copies:
        copy.start()
    for copy in copies:
        copy.wait()
    mats = tap_matrices(ws_ref[...], 16, wscr)
    strided_ref[...] = jnp.concatenate(mats, axis=0).T.astype(BF16)
    mats = tap_matrices(wd_ref[...], 9, wscr)
    dilated_ref[...] = jnp.concatenate(mats, axis=0).T.astype(BF16)
    bias_row = table_ref[pl.ds(owner_ref[scene], 1), :]
    bias_ref[...] = jnp.broadcast_to(jnp.broadcast_to(bias_row, (8, CH)).T[:, 0:1], (CH, 128))
    forward_patch(
        x_ref, cot_ref[...].astype(F32)[0:1, :], strided_ref[...], dilated_ref[...], bias_ref[:, 0:1],
        ph_ref, pre_ref, act_ref, send_ref, im_scr,
    )


def later_kernel(
    x_ref, cot_ref, w_strided_ref, w_dilated_ref, bias_ref, sent_ref,
    ph_ref, pre_ref, act_ref, send_ref, both_ref, im_scr,
):
    forward_patch(
        x_ref.at[1], cot_ref[...].astype(F32)[1:2, :], w_strided_ref[...], w_dilated_ref[...],
        bias_ref[:, 0:1], ph_ref, pre_ref, act_ref, send_ref, im_scr,
    )
    both_ref[0] = sent_ref[...]
    both_ref[1] = send_ref[...]


def prepare_kernel(
    pairing_hbm, valid_hbm, owner_hbm, ws_ref, wd_ref, *refs, bias_rows
):
    pre_refs, act_refs, ph_refs, send_refs = (refs[2 * k : 2 * k + 2] for k in range(4))
    (
        slope_first, slope_second, act_first, act_second, ph_first, ph_second,
        wf_ref, wt_ref, select_ref, place_ref, cot_ref,
        pairing_ref, valid_ref, owner_ref, wscr, sems,
    ) = refs[8:]
    copies = [
        pltpu.make_async_copy(source, target, sems.at[i])
        for i, (source, target) in enumerate(
            [(pairing_hbm, pairing_ref), (valid_hbm, valid_ref), (owner_hbm, owner_ref)]
        )
    ]
    for copy in copies:
        copy.start()
    scene, tile = lax.axis_index("scene"), lax.axis_index("tile")
    branch, pair = scene % 2, scene // 2
    mats = tap_matrices(ws_ref[branch], 16, wscr)
    blocks = {}
    for rt in range(4):
        for ct in range(4):
            (pr, dr), (pc, dc) = TAP_LINES[rt], TAP_LINES[ct]
            blocks[pr * 2 + pc, shift_index(-dr, -dc)] = mats[rt * 4 + ct]
    zero = jnp.zeros((CH, CH), F32)
    for phase in range(4):
        row = [blocks.get((phase, s), zero) for s in range(9)]
        wf_ref[phase * CH : (phase + 1) * CH, :] = jnp.concatenate(row, axis=1).astype(BF16)
    give, keep = halves(wd_ref[branch].astype(F32), branch)
    mats = tap_matrices(jnp.concatenate([give, keep], axis=0), 9, wscr)[::-1]
    half = CH // 2
    wt_ref[...] = jnp.concatenate(
        [mat[:, h * half : (h + 1) * half] for h in range(2) for mat in mats], axis=1
    ).astype(BF16)
    slopes = []
    for pre_ref in pre_refs:
        pre = pre_ref[...]
        gate = 1.0 / (1.0 + jnp.exp(-pre))
        slopes.append(gate * (1.0 + pre * (1.0 - gate)))
    for copy in copies:
        copy.wait()
    total = pairing_ref.shape[0]
    matches = []
    for p in range(2):
        position = tile * 2 + p
        matched, inverse = pairing_ref[position, pair], jnp.int32(0)
        for i in range(total):
            inverse = inverse + jnp.where(pairing_ref[i, pair] == position, i, 0)
        matched = jnp.where(branch == 0, matched, inverse)
        matches.append(jnp.where(matched // 2 == tile, 0, 2) + matched % 2)
    swapped = matches[0] == 3
    slope_first[...] = jnp.where(swapped, slopes[1], slopes[0])
    slope_second[...] = jnp.where(swapped, slopes[0], slopes[1])
    for first, second, pairs in ((act_first, act_second, act_refs), (ph_first, ph_second, ph_refs)):
        first[...] = jnp.where(swapped, pairs[1][...], pairs[0][...])
        second[...] = jnp.where(swapped, pairs[0][...], pairs[1][...])
    rows = send_refs[0].shape[0] - 16
    cots = [ref[rows:, :].astype(F32) for ref in send_refs]
    cot_ref[0:16, :] = jnp.where(swapped, cots[1], cots[0])
    cot_ref[16:32, :] = jnp.where(swapped, cots[0], cots[1])
    row = lax.broadcasted_iota(jnp.int32, select_ref.shape, 0)
    select = jnp.zeros(select_ref.shape, F32)
    for p in range(2):
        position = jnp.where(swapped, 1 - p, p)
        live = jnp.where(tile * 2 + p < valid_ref[pair], 8 + position, -1)
        select = jnp.where((row == position * 4 + matches[p]) | (row == live), 1.0, select)
    select_ref[...] = jnp.where(row == jnp.where(swapped, 10, -1), 1.0, select)
    row = lax.broadcasted_iota(jnp.int32, place_ref.shape, 0)
    here = scene // 2 % 4
    place = jnp.zeros(place_ref.shape, F32)
    for k, source in enumerate((scene, scene ^ 1)):
        owner = owner_ref[source]
        target = owner // (2 * bias_rows)
        half = jnp.where(target // 8 == branch, 0, 1)
        wanted = k * 64 + ((target // 2 % 4) ^ here) * 16 + half * 8 + owner % (2 * bias_rows)
        place = jnp.where(row == jnp.where(target % 2 == branch, wanted, -1), 1.0, place)
    place_ref[...] = place


HALF = 9 * CH // 2


def shift_rows(pieces, reach, side, target):
    masks = shifted_masks(side, reach)
    rows = CH // 2
    for h, piece in enumerate(pieces):
        for s, (dr, dc) in enumerate(SHIFTS):
            at = h * HALF + s * rows
            target[at : at + rows, :] = shifted(piece, dr, dc, side, reach, masks)


def backward_patch(position, candidates, select_ref, cot_ref, wt_ref, slope_ref, shift_scr):
    side = math.isqrt(slope_ref.shape[1])
    lanes = side * side // 128
    core = lax.axis_index("scene") % 2
    partner = None
    for k, payload in enumerate(candidates):
        term = payload * select_ref[position * 4 + k : position * 4 + k + 1, :].astype(BF16)
        partner = term if partner is None else partner + term
    live = select_ref[8 + position : 9 + position, :]
    signal = (cot_ref[position * 16 : position * 16 + 16, :] + partner[lanes * CH :, :].astype(F32)) * live
    out_grad = jnp.concatenate(
        [signal[j : j + 1, :] * partner[j * CH : (j + 1) * CH, :].astype(F32) for j in range(lanes)], axis=1
    )
    shift_rows([piece.astype(BF16) for piece in halves(out_grad, core)], 2, side, shift_scr)
    return dot(wt_ref[...], shift_scr[...]) * slope_ref[...]


def backward_first_kernel(
    far0_ref, near_ref, select_ref, cot_ref, wt_ref, act_ref, slope_ref, ph_ref,
    pre_b_ref, bias_ref, dilated_ref, strided_ref, shift_scr,
):
    side = math.isqrt(slope_ref.shape[1])
    core = lax.axis_index("scene") % 2
    candidates = (near_ref[0], near_ref[1], far0_ref[...])
    pre_grad = backward_patch(0, candidates, select_ref, cot_ref, wt_ref, slope_ref, shift_scr)
    act = act_ref[...]
    dilated_ref[...] = dot_nt(shift_scr[...], jnp.concatenate([act, act], axis=0))
    bias_ref[...] = jnp.broadcast_to(jnp.sum(pre_grad, axis=1, keepdims=True), bias_ref.shape)
    pre_b_ref[...] = pre_grad.astype(BF16)
    shift_rows([piece.astype(BF16) for piece in halves(pre_grad, core)], 1, side, shift_scr)
    strided_ref[...] = dot_nt(shift_scr[...], ph_ref[...])


def tap_blocks(strided, dilated):
    rows = CH // 2
    lower = lax.broadcasted_iota(jnp.int32, (rows, 2 * CH), 1) < CH

    def strided_piece(pr, shift):
        return strided[shift * rows : (shift + 1) * rows, pr * 2 * CH : (pr + 1) * 2 * CH]

    blocks = []
    for rt in range(4):
        pr, dr = TAP_LINES[rt]
        blocks.append(strided_piece(pr, shift_index(-dr, 0)))
        blocks.append(
            jnp.where(lower, strided_piece(pr, shift_index(-dr, -1)), strided_piece(pr, shift_index(-dr, 1)))
        )
    for j in range(5):
        low = dilated[(8 - 2 * j) * rows : (9 - 2 * j) * rows, :]
        high = dilated[(7 - 2 * j) * rows : (8 - 2 * j) * rows, :] if j < 4 else jnp.zeros_like(low)
        blocks.append(jnp.where(lower, low, high))
    return blocks


def write_blocks(blocks, bias_wide, ref, chunked):
    if not chunked:
        for i, block in enumerate(blocks):
            ref[i] = block
        return
    here = lax.axis_index("scene") // 2 % 4
    for m in range(4):
        pieces = [block[8 * m : 8 * m + 8] for block in blocks] + [bias_wide]
        ref[here ^ m] = jnp.concatenate(pieces, axis=0).astype(BF16)


def backward_second_kernel(
    far1_ref, far0_ref, near_ref, select_ref, cot_ref, wt_ref, act_ref, slope_ref, ph_ref,
    other_ref, other_bias_ref, other_dilated_ref, other_strided_ref,
    pre_b0_ref, pre_b1_ref, bias_ref, give_ref, out_shifts_ref, kept_ref, shift_scr, *, chunked,
):
    side = math.isqrt(slope_ref.shape[1])
    core = lax.axis_index("scene") % 2
    candidates = (near_ref[0], near_ref[1], far0_ref[...], far1_ref[...])
    pre_grad = backward_patch(1, candidates, select_ref, cot_ref, wt_ref, slope_ref, out_shifts_ref)
    act = act_ref[...]
    dilated = dot_nt(out_shifts_ref[0:HALF, :], jnp.concatenate([act, act], axis=0))
    give, keep = (piece.astype(BF16) for piece in halves(pre_grad, core))
    shift_rows([give], 1, side, shift_scr)
    strided = dot_nt(shift_scr[...], ph_ref[...])
    kept_ref[...] = keep
    bias_wide = (jnp.sum(pre_grad, axis=1, keepdims=True) + other_bias_ref[...]).T[0:8, :]
    bias_wide = jnp.concatenate([bias_wide, jnp.zeros_like(bias_wide)], axis=1)
    bias_ref[...] = bias_wide
    blocks = tap_blocks(strided + other_strided_ref[0:HALF, :], dilated + other_dilated_ref[0:HALF, :])
    write_blocks(blocks, bias_wide, give_ref, chunked)
    pre_b = pre_grad.astype(BF16)
    swapped = select_ref[10:11, 0:1].astype(BF16)
    straight = 1.0 - swapped
    pre_b0_ref[...] = other_ref[...] * straight + pre_b * swapped
    pre_b1_ref[...] = other_ref[...] * swapped + pre_b * straight


def backward_kept_kernel(
    out_shifts_ref, kept_pre_ref, act_ref, ph_ref, other_dilated_ref, other_strided_ref, keep_ref, shift_scr, *, chunked
):
    side = math.isqrt(act_ref.shape[1])
    act = act_ref[...]
    dilated = dot_nt(out_shifts_ref[HALF:, :], jnp.concatenate([act, act], axis=0))
    shift_rows([kept_pre_ref[...]], 1, side, shift_scr)
    strided = dot_nt(shift_scr[...], ph_ref[...])
    blocks = tap_blocks(strided + other_strided_ref[HALF:, :], dilated + other_dilated_ref[HALF:, :])
    write_blocks(blocks, jnp.zeros((8, 2 * CH), F32), keep_ref, chunked)


def spread_kernel(place_ref, bias_ref, keep_ref, got_ref, *out_refs):
    rows = keep_ref.shape[1]
    top = lax.broadcasted_iota(jnp.int32, (16, 128), 0) < 8
    mine = bias_ref[0:1, :]
    theirs = got_ref[0, rows - 16 :, :].astype(F32)[8:9, :]
    for d, out_ref in enumerate(out_refs):
        for half, ref in enumerate((keep_ref, got_ref)):
            at = d * 16 + half * 8
            bias = place_ref[at : at + 8, :] * mine + place_ref[64 + at : 72 + at, :] * theirs
            last = ref[d, rows - 16 :, :].astype(F32)
            last = jnp.where(top, last, jnp.concatenate([bias, bias], axis=0))
            out_ref[half * rows : (half + 1) * rows - 16, :] = ref[d, : rows - 16, :]
            out_ref[(half + 1) * rows - 16 : (half + 1) * rows, :] = last.astype(BF16)


def join_kernel(own_ref, a_ref, b_ref, c_ref, keep_ref, stay_ref, cross_ref):
    scene = lax.axis_index("scene")
    rows = keep_ref.shape[0]
    total = (own_ref[...].astype(F32) + a_ref[...].astype(F32)) + (
        b_ref[...].astype(F32) + c_ref[...].astype(F32)
    )
    mine, theirs = total[:rows, :], total[rows:, :]
    first = scene // 8 == scene % 2
    kept = jnp.where(first, mine, theirs)
    keep_ref[...] = kept
    stay_ref[...] = kept.astype(BF16)
    cross_ref[...] = jnp.where(first, theirs, mine).astype(BF16)


def finish_kernel(
    own_ref, a_ref, b_ref, c_ref, late_ref, features_in_hbm, weights_hbm, bias_hbm, features_hbm,
    weights_ref, bias_ref, tap_scr, turn_scr, dilated_scr, sems, *, weight_scale, bias_scale,
):
    tile = lax.axis_index("tile")
    late = pltpu.make_async_copy(late_ref, features_hbm.at[1], sems.at[0])
    late.start()
    total = (own_ref[...] + a_ref[...].astype(F32)) + (b_ref[...].astype(F32) + c_ref[...].astype(F32))
    bias = total[(BLOCKS - 1) * 8 :, :] * bias_scale
    index = lax.broadcasted_iota(jnp.int32, bias.shape, 0)
    bias_ref[...] = jnp.sum(jnp.where(index == tile, bias, 0.0), axis=0, keepdims=True)[:, 0:CH]
    bias_out = pltpu.make_async_copy(bias_ref, bias_hbm, sems.at[1])
    bias_out.start()
    total = total * weight_scale
    other = pltpu.roll(total, CH, 1)
    for block in range(8):
        for half, source in enumerate((total, other)):
            tap = block // 2 * 4 + ((1, 2), (3, 0))[block % 2][half]
            tap_scr[pl.ds(tap, 8, stride=16), :] = source[block * 8 : block * 8 + 8, :]
    lines = tap_scr[...].T[0:CH, :].reshape(8, 8, 128)
    sub = lax.broadcasted_iota(jnp.int32, lines.shape, 1)
    chunk = lax.broadcasted_iota(jnp.int32, lines.shape, 2) // 16
    for step in (1, 2, 4):
        up = pltpu.roll(pltpu.roll(lines, 8 - step, 1), 16 * step, 2)
        down = pltpu.roll(pltpu.roll(lines, step, 1), 128 - 16 * step, 2)
        high, wide = sub // step % 2, chunk // step % 2
        lines = jnp.where(high == wide, lines, jnp.where(high == 0, up, down))
    for block in range(8):
        weights_ref[:, block * 128 : (block + 1) * 128] = lines[block]
    strided_part, dilated_part = pl.ds(0, 16 * CH), pl.ds(16 * CH, DIL_TAPS * CH)
    strided_out = pltpu.make_async_copy(weights_ref.at[:, strided_part], weights_hbm.at[:, strided_part], sems.at[2])
    strided_out.start()
    turn_scr[0:40, :] = total[64:104, :]
    turned = turn_scr[...].T
    for tap in range(DIL_TAPS):
        half = tap % 2
        dilated_scr[pl.ds(tap, CH, stride=DIL_TAPS), :] = turned[half * CH : (half + 1) * CH, :]
    spread = dilated_scr[...].T
    tap = lax.broadcasted_iota(jnp.int32, (8, DIL_TAPS * CH), 1) % DIL_TAPS
    result = spread[0:8, :]
    for j in range(1, 5):
        result = jnp.where(tap // 2 == j, spread[8 * j : 8 * j + 8, :], result)
    weights_ref[:, 16 * CH :] = result
    dilated_out = pltpu.make_async_copy(weights_ref.at[:, dilated_part], weights_hbm.at[:, dilated_part], sems.at[3])
    dilated_out.start()
    for copy in (late, bias_out, strided_out, dilated_out):
        copy.wait()


def feature_patch(pre_b_ref, wf_ref, out_ref, shift_scr):
    side = math.isqrt(pre_b_ref.shape[1])
    near = shifted_masks(side, 1)
    merge = phase_matrix(side, True)
    run, wide = 16 * side, 4 * side
    pre_b = pre_b_ref[...]
    for s, (dr, dc) in enumerate(SHIFTS):
        shift_scr[s * CH : (s + 1) * CH, :] = shifted(pre_b, dr, dc, side, 1, near)
    phases = dot(wf_ref[...], shift_scr[...]).astype(BF16)
    runs = out_ref.shape[1] // run
    stacked = jnp.concatenate(
        [
            jnp.concatenate(
                [phases[k * CH : (k + 1) * CH, q * wide : (q + 1) * wide] for k in range(4)], axis=1
            )
            for q in range(runs)
        ],
        axis=0,
    )
    merged = dot(stacked, merge).astype(BF16)
    for q in range(runs):
        out_ref[:, q * run : (q + 1) * run] = merged[q * CH : (q + 1) * CH, :]


def feature_first_kernel(pre_b_ref, wf_ref, out_ref, shift_scr):
    feature_patch(pre_b_ref, wf_ref, out_ref, shift_scr)


def feature_second_kernel(pre_b_ref, wf_ref, first_ref, out_ref, features_hbm, shift_scr, sem):
    copy = pltpu.make_async_copy(first_ref, features_hbm.at[0], sem)
    copy.start()
    feature_patch(pre_b_ref, wf_ref, out_ref, shift_scr)
    copy.wait()


SPACES = {"s": pltpu.SMEM, "v": pltpu.VMEM, "h": pltpu.HBM, "a": pl.ANY}


def call(kernel, outs, ins, scratch, *args, flops=0, out_spaces="", aliases=None):
    args = [
        pltpu.with_memory_space_constraint(arg, pltpu.HBM) if space == "h" else arg
        for space, arg in zip(ins, args)
    ]
    return pl.pallas_call(
        kernel,
        out_shape=[jax.ShapeDtypeStruct(shape, kind) for shape, kind in outs],
        in_specs=[pl.BlockSpec(memory_space=SPACES[space]) for space in ins],
        out_specs=[pl.BlockSpec(memory_space=SPACES[space]) for space in out_spaces or "v" * len(outs)],
        scratch_shapes=[pltpu.VMEM(*item) if isinstance(item, tuple) else item for item in scratch],
        input_output_aliases=aliases or {},
        compiler_params=pltpu.CompilerParams(vmem_limit_bytes=VMEM_LIMIT),
        cost_estimate=pl.CostEstimate(flops=flops, bytes_accessed=1 << 20, transcendentals=0),
    )(*args)


def device_pairs(x, pairs):
    tiles = lax.axis_size("tile")
    flat = [(source[0] * tiles + source[1], target[0] * tiles + target[1]) for source, target in pairs]
    return lax.ppermute(x, ("scene", "tile"), flat)


def scene_xor(x, distance):
    return lax.ppermute(x, "scene", [(i, i ^ distance) for i in range(lax.axis_size("scene"))])


def device_xor(x, scene_distance, tile_distance):
    scenes, tiles = range(lax.axis_size("scene")), range(lax.axis_size("tile"))
    return device_pairs(
        x, [((s, t), (s ^ scene_distance, t ^ tile_distance)) for s in scenes for t in tiles]
    )


def join_halves(give, keep):
    parts = [half.reshape(BLOCKS - 1, -1, 8, half.shape[-1]) for half in (give, keep)]
    first = lax.axis_index("scene") % 2 == 0
    pair = jnp.stack([jnp.where(first, parts[1], parts[0]), jnp.where(first, parts[0], parts[1])], axis=2)
    return pair.reshape(BLOCKS - 1, -1, pair.shape[-1])


def reduce_anywhere(blocks, bias_row, tile_owner, bias_rows, weight_scale, bias_scale):
    channels = blocks.shape[1]
    scene = lax.axis_index("scene")
    scenes, tiles = lax.axis_size("scene"), lax.axis_size("tile")
    halves = blocks.reshape(BLOCKS - 1, channels, 2, channels)
    strided, dilated = [None] * 16, []
    for block in range(8):
        for half in range(2):
            strided[block // 2 * 4 + ((1, 2), (3, 0))[block % 2][half]] = halves[block, :, half]
    for tap in range(DIL_TAPS):
        dilated.append(halves[8 + tap // 2, :, tap % 2])
    row = jnp.concatenate(
        [
            jnp.stack(strided, axis=-1).reshape(channels, 16 * channels),
            jnp.stack(dilated, axis=-1).reshape(channels, DIL_TAPS * channels),
        ],
        axis=1,
    )
    hit = jnp.arange(2, dtype=jnp.int32)[:, None, None] == scene % 2
    term = jnp.where(hit, row[None] * weight_scale, 0.0).reshape(2 * channels, 25 * channels)
    weights = lax.psum(lax.psum_scatter(term, "scene", scatter_dimension=0, tiled=True), "tile")
    tile_id = lax.dynamic_index_in_dim(tile_owner, scene, 0, keepdims=False)
    owned = jnp.arange(scenes * tiles * bias_rows, dtype=jnp.int32) == tile_id
    bias = jnp.where(owned[:, None], bias_row[None, :channels] * bias_scale, 0.0)
    return weights, lax.psum_scatter(bias, ("scene", "tile"), scatter_dimension=0, tiled=True)


def local(
    features_in,
    strided_weights,
    dilated_weights,
    tile_bias,
    cost_cotangent,
    footprint_pairing,
    valid_counts,
    tile_owner,
):
    features, own_cot = features_in[0], cost_cotangent[0]
    patches, channels, cells_in = features.shape
    cells = own_cot.shape[1]
    scenes, tiles = lax.axis_size("scene"), lax.axis_size("tile")
    weight_scale = 1.0 / math.sqrt(scenes * patches * tiles * cells)
    bias_scale = 1.0 / math.sqrt(patches * tiles * cells)
    bias_rows = tile_bias.shape[0] // (scenes * tiles)
    grid = (channels, cells)
    payload = (cells * channels // 128 + 16, 128)
    chunked = scenes == 16 and tiles == 2 and patches == 2 and bias_rows == 1
    wscr = ((16 * channels, 2 * channels), F32)
    im_scr = ((16 * channels, cells), BF16)
    patch_outs = [((4 * channels, cells), BF16), (grid, F32), (grid, BF16), (payload, BF16)]
    first_outs = patch_outs + [
        ((channels, 16 * channels), BF16),
        ((channels, 9 * channels), BF16),
        ((channels, 128), F32),
        (own_cot.shape, BF16),
    ]
    *part, w_strided, w_dilated, bias_col, cot = call(
        first_kernel,
        first_outs,
        "hhhhhh",
        [
            ((channels, cells_in), BF16),
            (strided_weights.shape[1:], BF16),
            (dilated_weights.shape[1:], BF16),
            (tile_bias.shape, F32),
            pltpu.SMEM(tile_owner.shape, jnp.int32),
            wscr,
            im_scr,
            pltpu.SemaphoreType.DMA((6,)),
        ],
        tile_owner, features, strided_weights, dilated_weights, tile_bias, own_cot,
        flops=10**9,
    )
    far = [device_xor(part[3], 1, 1)]
    *late, both = call(
        later_kernel,
        patch_outs + [((2,) + payload, BF16)],
        "vvvvvv",
        [im_scr],
        features, cot, w_strided, w_dilated, bias_col, part[3],
        flops=10**10,
    )
    far.append(device_xor(late[3], 1, 1))
    near = scene_xor(both, 1)
    phases, pre, act, send = zip(part, late)
    ordered = [(grid, F32)] * 2 + [(grid, BF16)] * 2 + [((4 * channels, cells), BF16)] * 2
    *both, w_feature, w_act, select, place, cots = call(
        functools.partial(prepare_kernel, bias_rows=bias_rows),
        ordered
        + [
            ((4 * channels, 9 * channels), BF16),
            ((channels, 9 * channels), BF16),
            ((16, 128), F32),
            ((128, 128), F32),
            ((32, 128), F32),
        ],
        "hhhvvvvvvvvvv",
        [
            pltpu.SMEM(footprint_pairing.shape[::-1], jnp.int32),
            pltpu.SMEM(valid_counts.shape, jnp.int32),
            pltpu.SMEM(tile_owner.shape, jnp.int32),
            wscr,
            pltpu.SemaphoreType.DMA((3,)),
        ],
        footprint_pairing.T, valid_counts, tile_owner, strided_weights, dilated_weights,
        *pre, *act, *phases, *send,
        flops=10**10,
    )
    slope, act, phases = both[0:2], both[2:4], both[4:6]
    shift_scr = ((9 * channels, cells), BF16)
    sums = [((9 * channels, 128), F32), ((9 * channels, 4 * channels), F32)]
    first = call(
        backward_first_kernel,
        [(grid, BF16), ((channels, 128), F32)] + sums,
        "v" * 8,
        [shift_scr],
        far[0], near, select, cots, w_act, act[0], slope[0], phases[0],
        flops=10**9,
    )
    half_shift = ((9 * channels // 2, cells), BF16)
    grads_shape = ((4, BLOCKS * 8, 128), BF16) if chunked else ((BLOCKS - 1, channels // 2, 128), F32)
    *pre_b, bias, give, out_shifts, kept_rows = call(
        functools.partial(backward_second_kernel, chunked=chunked),
        [(grid, BF16)] * 2 + [((8, 128), F32), grads_shape, shift_scr, ((channels // 2, cells), BF16)],
        "v" * 13,
        [half_shift],
        far[1], far[0], near, select, cots, w_act, act[1], slope[1], phases[1], *first,
        flops=10**9,
    )
    if chunked:
        got = scene_xor(give, 1)
    (keep,) = call(
        functools.partial(backward_kept_kernel, chunked=chunked),
        [grads_shape],
        "v" * 6,
        [half_shift],
        out_shifts, kept_rows, act[1], phases[1], *first[2:],
        flops=10**9,
    )
    feature_shape = ((channels, cells_in), BF16)
    if chunked:
        stage = ((2 * BLOCKS * 8, 128), BF16)
        own, by_y, by_z, by_zy = call(spread_kernel, [stage] * 4, "vvvv", [], place, bias, keep, got)
        by_zy, by_z, by_y = scene_xor(by_zy, 6), scene_xor(by_z, 4), scene_xor(by_y, 2)
    (feature_first,) = call(
        feature_first_kernel, [feature_shape], "vv", [shift_scr], pre_b[0], w_feature, flops=10**9
    )
    chunk = (BLOCKS * 8, 128)
    if chunked:
        feature_first, own = lax.optimization_barrier((feature_first, own))
        kept, stay, cross = call(
            join_kernel, [(chunk, F32), (chunk, BF16), (chunk, BF16)], "vvvv", [], own, by_zy, by_z, by_y
        )
        by_zx, by_z, by_x = device_xor(cross, 8, 1), device_xor(cross, 8, 0), device_xor(stay, 0, 1)
    feature_last, feature_grads = call(
        feature_second_kernel,
        [feature_shape, (features.shape, BF16)],
        "vvv",
        [shift_scr, pltpu.SemaphoreType.DMA],
        pre_b[1], w_feature, feature_first,
        flops=10**9,
        out_spaces="vh",
    )
    if not chunked:
        feature_grads = feature_grads.at[1].set(feature_last)
        grad_weights, grad_bias = reduce_anywhere(
            join_halves(give, keep), bias[0], tile_owner, bias_rows, weight_scale, bias_scale
        )
        return (feature_grads[None], grad_weights, grad_bias)
    grad_weights, grad_bias, feature_grads = call(
        functools.partial(finish_kernel, weight_scale=weight_scale, bias_scale=bias_scale),
        [((8, 25 * channels), F32), ((1, channels), F32), (features.shape, BF16)],
        "vvvvva",
        [
            ((8, 25 * channels), F32),
            ((1, channels), F32),
            ((128, 128), F32),
            ((128, 128), F32),
            ((9 * channels, 128), F32),
            pltpu.SemaphoreType.DMA((4,)),
        ],
        kept, by_zx, by_z, by_x, feature_last, feature_grads,
        out_spaces="hhh",
        aliases={5: 2},
    )
    return (feature_grads[None], grad_weights, grad_bias)


def solution(mesh):
    return jax.shard_map(
        local,
        mesh=mesh,
        in_specs=(
            P("scene", "tile", None, None),
            P(),
            P(),
            P(),
            P("scene", "tile", None),
            P(),
            P(),
            P(),
        ),
        out_specs=(P("scene", "tile", None, None), P("scene", None), P(("scene", "tile"), None)),
        check_vma=False,
    )
```

```python
import functools
import math

import jax
import jax.numpy as jnp
from jax import lax
from jax.experimental import pallas as pl
from jax.experimental.pallas import tpu as pltpu
from jax.sharding import PartitionSpec as P

CH = 64
ROW_TAPS = 4
DIL_TAPS = 9
BLOCKS = 14
SHIFTS = [(dr, dc) for dr in (-1, 0, 1) for dc in (-1, 0, 1)]
F32 = jnp.float32
BF16 = jnp.bfloat16
VMEM_LIMIT = 24 * 1024 * 1024


def shift_index(dr, dc):
    return (dr + 1) * 3 + dc + 1


def dot(a, b):
    return lax.dot_general(a, b, (((1,), (0,)), ((), ())), preferred_element_type=F32)


def dot_nt(a, b):
    return lax.dot_general(a, b, (((1,), (1,)), ((), ())), preferred_element_type=F32)


def shifted_masks(side, reach):
    cell = lax.broadcasted_iota(jnp.int32, (1, side * side), 1)
    row, col = cell // side, cell % side
    masks = {}
    for dr, dc in SHIFTS:
        ok = (
            (row + dr * reach >= 0)
            & (row + dr * reach < side)
            & (col + dc * reach >= 0)
            & (col + dc * reach < side)
        )
        masks[dr, dc] = ok.astype(F32).astype(BF16)
    return masks


def shifted(x, dr, dc, side, reach, masks):
    if dr == 0 and dc == 0:
        return x
    cells = side * side
    return pltpu.roll(x, (-(dr * side + dc) * reach) % cells, 1) * masks[dr, dc].astype(x.dtype)


def merge_matrix(side):
    size = 16 * side
    dims = (size, size)
    source = lax.broadcasted_iota(jnp.int32, dims, 1)
    target = lax.broadcasted_iota(jnp.int32, dims, 0)
    phase, cell = target // (4 * side), target % (4 * side)
    row, col = cell // side, cell % side
    wanted = (2 * row + phase // 2) * (2 * side) + 2 * col + phase % 2
    return jnp.where(source == wanted, 1.0, 0.0).astype(BF16)


def halves(values, core):
    even = jnp.concatenate([values[16 * m : 16 * m + 8] for m in range(CH // 16)], axis=0)
    odd = jnp.concatenate([values[16 * m + 8 : 16 * m + 16] for m in range(CH // 16)], axis=0)
    return jnp.where(core == 0, odd, even), jnp.where(core == 0, even, odd)


def half_run_matrix(side, odd):
    dims = (8 * side, 8 * side)
    source, target = (lax.broadcasted_iota(jnp.int32, dims, k) for k in range(2))
    phase, cell = target // (2 * side) ^ odd, target % (2 * side)
    row, col = cell // side, cell % side
    wanted = (2 * row + phase // 2) * (2 * side) + 2 * col + phase % 2
    return jnp.where(source == wanted, 1.0, 0.0).astype(BF16)


TAP_LINES = {0: (1, -1), 1: (0, 0), 2: (1, 0), 3: (0, 1)}
ROW_ORDER = (1, 3, 2, 0)


def tap_matrices(weight, taps, scratch):
    scratch[0 : CH * taps, 0:CH] = weight.astype(F32).T
    return [scratch[pl.ds(tap, CH, stride=taps), 0:CH] for tap in range(taps)]


def forward_patch(x_ref, cot, w_strided, w_dilated, bias_col, ph_ref, pre_ref, act_ref, send_ref, im_scr):
    side = math.isqrt(x_ref.shape[1]) // 2
    run, lanes = 16 * side, side * side // 128
    near, far = shifted_masks(side, 1), shifted_masks(side, 2)
    runs, wide = x_ref.shape[1] // run, 4 * side
    even, odd = (
        dot(
            jnp.concatenate(
                [x_ref[:, q * run + h * run // 2 : q * run + (h + 1) * run // 2] for q in range(runs)], axis=0
            ),
            half_run_matrix(side, h),
        )
        for h in range(2)
    )
    lower = lax.broadcasted_iota(jnp.int32, (runs * CH, wide), 1) < wide // 2
    for pr in range(2):
        one, two = even[:, pr * wide : (pr + 1) * wide], odd[:, pr * wide : (pr + 1) * wide]
        first = jnp.where(lower, one, two).astype(BF16)
        second = pltpu.roll(jnp.where(lower, two, one).astype(BF16), wide // 2, 1)
        for pc, lines in ((0, first), (1, second)):
            for q in range(runs):
                at = (pr * 2 + pc) * CH
                ph_ref[at : at + CH, q * wide : (q + 1) * wide] = lines[q * CH : (q + 1) * CH]
    sums = []
    for pr in range(2):
        for ct in range(4):
            pc, dc = TAP_LINES[ct]
            at, phase = (pr * 4 + ct) * CH, pr * 2 + pc
            im_scr[at : at + CH, :] = shifted(ph_ref[phase * CH : (phase + 1) * CH, :], 0, dc, side, 1, near)
        both = dot(w_strided[pr * 2 * CH : (pr + 1) * 2 * CH], im_scr[pr * 4 * CH : (pr + 1) * 4 * CH, :])
        dr = TAP_LINES[ROW_ORDER[2 * pr + 1]][1]
        sums.append(both[:CH] + shifted(both[CH:], dr, 0, side, 1, near))
    pre = sums[0] + sums[1] + bias_col
    pre_ref[...] = pre
    act = (pre * (1.0 / (1.0 + jnp.exp(-pre)))).astype(BF16)
    act_ref[...] = act
    for k in range(3):
        im_scr[k * CH : (k + 1) * CH, :] = shifted(act, 0, k - 1, side, 2, far)
    rows = dot(w_dilated, im_scr[0 : 3 * CH, :])
    out = rows[CH : 2 * CH]
    for k in (0, 2):
        out = out + shifted(rows[k * CH : (k + 1) * CH], k - 1, 0, side, 2, far)
    out = out.astype(BF16)
    for lane in range(lanes):
        send_ref[lane * CH : (lane + 1) * CH, :] = out[:, lane * 128 : (lane + 1) * 128]
    rows = [cot[:, lane * 128 : (lane + 1) * 128] for lane in range(lanes)]
    rows.append(jnp.zeros((16 - lanes, 128), F32))
    send_ref[lanes * CH :, :] = jnp.concatenate(rows, axis=0).astype(BF16)


def first_kernel(
    owner_hbm, x_hbm, ws_hbm, wd_hbm, bias_hbm, cot_hbm,
    ph_ref, pre_ref, act_ref, send_ref, strided_ref, dilated_ref, bias_ref, cot_ref,
    x_ref, ws_ref, wd_ref, table_ref, owner_ref, wscr, im_scr, sems,
):
    scene = lax.axis_index("scene")
    branch = scene % 2
    copies = [
        pltpu.make_async_copy(source, target, sems.at[i])
        for i, (source, target) in enumerate(
            [
                (x_hbm.at[0], x_ref),
                (ws_hbm.at[branch], ws_ref),
                (wd_hbm.at[branch], wd_ref),
                (owner_hbm, owner_ref),
                (bias_hbm, table_ref),
                (cot_hbm, cot_ref),
            ]
        )
    ]
    for copy in copies:
        copy.start()
    for copy in copies:
        copy.wait()
    mats = tap_matrices(ws_ref[...], 16, wscr)
    for k, rt in enumerate(ROW_ORDER):
        line = jnp.concatenate(mats[rt * 4 : rt * 4 + 4], axis=0)
        strided_ref[k * CH : (k + 1) * CH, :] = line.T.astype(BF16)
    mats = tap_matrices(wd_ref[...], 9, wscr)
    for k in range(3):
        line = jnp.concatenate(mats[3 * k : 3 * k + 3], axis=0)
        dilated_ref[k * CH : (k + 1) * CH, :] = line.T.astype(BF16)
    bias_row = table_ref[pl.ds(owner_ref[scene], 1), :]
    bias_ref[...] = jnp.broadcast_to(jnp.broadcast_to(bias_row, (8, CH)).T[:, 0:1], (CH, 128))
    forward_patch(
        x_ref, cot_ref[...].astype(F32)[0:1, :], strided_ref[...], dilated_ref[...], bias_ref[:, 0:1],
        ph_ref, pre_ref, act_ref, send_ref, im_scr,
    )


def later_kernel(
    x_ref, cot_ref, w_strided_ref, w_dilated_ref, bias_ref, sent_ref,
    ph_ref, pre_ref, act_ref, send_ref, both_ref, im_scr,
):
    forward_patch(
        x_ref.at[1], cot_ref[...].astype(F32)[1:2, :], w_strided_ref[...], w_dilated_ref[...],
        bias_ref[:, 0:1], ph_ref, pre_ref, act_ref, send_ref, im_scr,
    )
    both_ref[0] = sent_ref[...]
    both_ref[1] = send_ref[...]


def prepare_kernel(
    pairing_hbm, valid_hbm, owner_hbm, ws_ref, wd_ref, *refs, bias_rows
):
    pre_refs, act_refs, ph_refs, send_refs = (refs[2 * k : 2 * k + 2] for k in range(4))
    (
        slope_first, slope_second, act_first, act_second, ph_first, ph_second,
        wf_ref, wt_ref, select_ref, place_ref, cot_ref,
        pairing_ref, valid_ref, owner_ref, wscr, sems,
    ) = refs[8:]
    copies = [
        pltpu.make_async_copy(source, target, sems.at[i])
        for i, (source, target) in enumerate(
            [(pairing_hbm, pairing_ref), (valid_hbm, valid_ref), (owner_hbm, owner_ref)]
        )
    ]
    for copy in copies:
        copy.start()
    scene, tile = lax.axis_index("scene"), lax.axis_index("tile")
    branch, pair = scene % 2, scene // 2
    mats = tap_matrices(ws_ref[branch], 16, wscr)
    blocks = {}
    for rt in range(4):
        for ct in range(4):
            (pr, dr), (pc, dc) = TAP_LINES[rt], TAP_LINES[ct]
            blocks[pr * 2 + pc, shift_index(-dr, -dc)] = mats[rt * 4 + ct]
    zero = jnp.zeros((CH, CH), F32)
    for phase in range(4):
        row = [blocks.get((phase, s), zero) for s in range(9)]
        wf_ref[phase * CH : (phase + 1) * CH, :] = jnp.concatenate(row, axis=1).astype(BF16)
    give, keep = halves(wd_ref[branch].astype(F32), branch)
    mats = tap_matrices(jnp.concatenate([give, keep], axis=0), 9, wscr)[::-1]
    half = CH // 2
    wt_ref[...] = jnp.concatenate(
        [mat[:, h * half : (h + 1) * half] for h in range(2) for mat in mats], axis=1
    ).astype(BF16)
    slopes = []
    for pre_ref in pre_refs:
        pre = pre_ref[...]
        gate = 1.0 / (1.0 + jnp.exp(-pre))
        slopes.append(gate * (1.0 + pre * (1.0 - gate)))
    for copy in copies:
        copy.wait()
    total = pairing_ref.shape[0]
    matches = []
    for p in range(2):
        position = tile * 2 + p
        matched, inverse = pairing_ref[position, pair], jnp.int32(0)
        for i in range(total):
            inverse = inverse + jnp.where(pairing_ref[i, pair] == position, i, 0)
        matched = jnp.where(branch == 0, matched, inverse)
        matches.append(jnp.where(matched // 2 == tile, 0, 2) + matched % 2)
    swapped = matches[0] == 3
    slope_first[...] = jnp.where(swapped, slopes[1], slopes[0])
    slope_second[...] = jnp.where(swapped, slopes[0], slopes[1])
    for first, second, pairs in ((act_first, act_second, act_refs), (ph_first, ph_second, ph_refs)):
        first[...] = jnp.where(swapped, pairs[1][...], pairs[0][...])
        second[...] = jnp.where(swapped, pairs[0][...], pairs[1][...])
    rows = send_refs[0].shape[0] - 16
    cots = [ref[rows:, :].astype(F32) for ref in send_refs]
    cot_ref[0:16, :] = jnp.where(swapped, cots[1], cots[0])
    cot_ref[16:32, :] = jnp.where(swapped, cots[0], cots[1])
    row = lax.broadcasted_iota(jnp.int32, select_ref.shape, 0)
    select = jnp.zeros(select_ref.shape, F32)
    for p in range(2):
        position = jnp.where(swapped, 1 - p, p)
        live = jnp.where(tile * 2 + p < valid_ref[pair], 8 + position, -1)
        select = jnp.where((row == position * 4 + matches[p]) | (row == live), 1.0, select)
    select_ref[...] = jnp.where(row == jnp.where(swapped, 10, -1), 1.0, select)
    row = lax.broadcasted_iota(jnp.int32, place_ref.shape, 0)
    here = scene // 2 % 4
    place = jnp.zeros(place_ref.shape, F32)
    for k, source in enumerate((scene, scene ^ 1)):
        owner = owner_ref[source]
        target = owner // (2 * bias_rows)
        half = jnp.where(target // 8 == branch, 0, 1)
        wanted = k * 64 + ((target // 2 % 4) ^ here) * 16 + half * 8 + owner % (2 * bias_rows)
        place = jnp.where(row == jnp.where(target % 2 == branch, wanted, -1), 1.0, place)
    place_ref[...] = place


HALF = 9 * CH // 2


def shift_rows(pieces, reach, side, target):
    masks = shifted_masks(side, reach)
    rows = CH // 2
    for h, piece in enumerate(pieces):
        for s, (dr, dc) in enumerate(SHIFTS):
            at = h * HALF + s * rows
            target[at : at + rows, :] = shifted(piece, dr, dc, side, reach, masks)


def pick(position, candidates, select_ref, first=0):
    partner = None
    for k, payload in enumerate(candidates, first):
        term = payload * select_ref[position * 4 + k : position * 4 + k + 1, :].astype(BF16)
        partner = term if partner is None else partner + term
    return partner


def backward_patch(position, partner, select_ref, cot_ref, wt_ref, slope_ref, shift_scr):
    side = math.isqrt(slope_ref.shape[1])
    lanes = side * side // 128
    core = lax.axis_index("scene") % 2
    live = select_ref[8 + position : 9 + position, :]
    signal = (cot_ref[position * 16 : position * 16 + 16, :] + partner[lanes * CH :, :].astype(F32)) * live
    out_grad = jnp.concatenate(
        [signal[j : j + 1, :] * partner[j * CH : (j + 1) * CH, :].astype(F32) for j in range(lanes)], axis=1
    )
    shift_rows([piece.astype(BF16) for piece in halves(out_grad, core)], 2, side, shift_scr)
    return dot(wt_ref[...], shift_scr[...]) * slope_ref[...]


def backward_first_kernel(
    far0_ref, near_ref, select_ref, cot_ref, wt_ref, act_ref, slope_ref, ph_ref,
    pick_ref, pre_b_ref, bias_ref, dilated_ref, strided_ref, shift_scr,
):
    side = math.isqrt(slope_ref.shape[1])
    core = lax.axis_index("scene") % 2
    candidates = (near_ref[0], near_ref[1], far0_ref[...])
    pick_ref[...] = pick(1, candidates, select_ref)
    pre_grad = backward_patch(0, pick(0, candidates, select_ref), select_ref, cot_ref, wt_ref, slope_ref, shift_scr)
    act = act_ref[...]
    dilated_ref[...] = dot_nt(shift_scr[...], jnp.concatenate([act, act], axis=0))
    bias_ref[...] = jnp.broadcast_to(jnp.sum(pre_grad, axis=1, keepdims=True), bias_ref.shape)
    pre_b_ref[...] = pre_grad.astype(BF16)
    shift_rows([piece.astype(BF16) for piece in halves(pre_grad, core)], 1, side, shift_scr)
    strided_ref[...] = dot_nt(shift_scr[...], ph_ref[...])


def tap_blocks(strided, dilated):
    rows = CH // 2
    lower = lax.broadcasted_iota(jnp.int32, (rows, 2 * CH), 1) < CH

    def strided_piece(pr, shift):
        return strided[shift * rows : (shift + 1) * rows, pr * 2 * CH : (pr + 1) * 2 * CH]

    blocks = []
    for rt in range(4):
        pr, dr = TAP_LINES[rt]
        blocks.append(strided_piece(pr, shift_index(-dr, 0)))
        blocks.append(
            jnp.where(lower, strided_piece(pr, shift_index(-dr, -1)), strided_piece(pr, shift_index(-dr, 1)))
        )
    for j in range(5):
        low = dilated[(8 - 2 * j) * rows : (9 - 2 * j) * rows, :]
        high = dilated[(7 - 2 * j) * rows : (8 - 2 * j) * rows, :] if j < 4 else jnp.zeros_like(low)
        blocks.append(jnp.where(lower, low, high))
    return blocks


def write_blocks(blocks, bias_wide, ref, chunked):
    if not chunked:
        for i, block in enumerate(blocks):
            ref[i] = block
        return
    here = lax.axis_index("scene") // 2 % 4
    for m in range(4):
        pieces = [block[8 * m : 8 * m + 8] for block in blocks] + [bias_wide]
        ref[here ^ m] = jnp.concatenate(pieces, axis=0).astype(BF16)


def backward_second_kernel(
    far1_ref, pick_ref, select_ref, cot_ref, wt_ref, act_ref, slope_ref, ph_ref,
    other_bias_ref, other_dilated_ref, other_strided_ref,
    pre_b_ref, bias_ref, give_ref, out_shifts_ref, shift_scr, *, chunked,
):
    side = math.isqrt(slope_ref.shape[1])
    core = lax.axis_index("scene") % 2
    partner = pick_ref[...] + pick(1, (far1_ref[...],), select_ref, 3)
    pre_grad = backward_patch(1, partner, select_ref, cot_ref, wt_ref, slope_ref, out_shifts_ref)
    act = act_ref[...]
    dilated = dot_nt(out_shifts_ref[0:HALF, :], jnp.concatenate([act, act], axis=0))
    give, _ = halves(pre_grad, core)
    shift_rows([give.astype(BF16)], 1, side, shift_scr)
    strided = dot_nt(shift_scr[...], ph_ref[...])
    pre_b_ref[...] = pre_grad.astype(BF16)
    bias_wide = (jnp.sum(pre_grad, axis=1, keepdims=True) + other_bias_ref[...]).T[0:8, :]
    bias_wide = jnp.concatenate([bias_wide, jnp.zeros_like(bias_wide)], axis=1)
    bias_ref[...] = bias_wide
    blocks = tap_blocks(strided + other_strided_ref[0:HALF, :], dilated + other_dilated_ref[0:HALF, :])
    write_blocks(blocks, bias_wide, give_ref, chunked)


def backward_kept_kernel(
    select_ref, out_shifts_ref, pre_b_ref, other_ref, act_ref, ph_ref, other_dilated_ref, other_strided_ref,
    keep_ref, pre_b0_ref, pre_b1_ref, shift_scr, *, chunked,
):
    side = math.isqrt(act_ref.shape[1])
    act = act_ref[...]
    dilated = dot_nt(out_shifts_ref[HALF:, :], jnp.concatenate([act, act], axis=0))
    pre_b, other = pre_b_ref[...], other_ref[...]
    _, keep = halves(pre_b.astype(F32), lax.axis_index("scene") % 2)
    shift_rows([keep.astype(BF16)], 1, side, shift_scr)
    strided = dot_nt(shift_scr[...], ph_ref[...])
    blocks = tap_blocks(strided + other_strided_ref[HALF:, :], dilated + other_dilated_ref[HALF:, :])
    write_blocks(blocks, jnp.zeros((8, 2 * CH), F32), keep_ref, chunked)
    swapped = select_ref[10:11, 0:1].astype(BF16)
    straight = 1.0 - swapped
    pre_b0_ref[...] = other * straight + pre_b * swapped
    pre_b1_ref[...] = other * swapped + pre_b * straight


def spread_kernel(place_ref, bias_ref, keep_ref, got_ref, *out_refs):
    rows = keep_ref.shape[1]
    top = lax.broadcasted_iota(jnp.int32, (16, 128), 0) < 8
    mine = bias_ref[0:1, :]
    theirs = got_ref[0, rows - 16 :, :].astype(F32)[8:9, :]
    for d, out_ref in enumerate(out_refs):
        for half, ref in enumerate((keep_ref, got_ref)):
            at = d * 16 + half * 8
            bias = place_ref[at : at + 8, :] * mine + place_ref[64 + at : 72 + at, :] * theirs
            last = ref[d, rows - 16 :, :].astype(F32)
            last = jnp.where(top, last, jnp.concatenate([bias, bias], axis=0))
            out_ref[half * rows : (half + 1) * rows - 16, :] = ref[d, : rows - 16, :]
            out_ref[(half + 1) * rows - 16 : (half + 1) * rows, :] = last.astype(BF16)


def join_kernel(own_ref, a_ref, b_ref, c_ref, keep_ref, stay_ref, cross_ref):
    scene = lax.axis_index("scene")
    rows = keep_ref.shape[0]
    total = (own_ref[...].astype(F32) + a_ref[...].astype(F32)) + (
        b_ref[...].astype(F32) + c_ref[...].astype(F32)
    )
    mine, theirs = total[:rows, :], total[rows:, :]
    first = scene // 8 == scene % 2
    kept = jnp.where(first, mine, theirs)
    keep_ref[...] = kept
    stay_ref[...] = kept.astype(BF16)
    cross_ref[...] = jnp.where(first, theirs, mine).astype(BF16)


def finish_kernel(
    own_ref, a_ref, b_ref, c_ref, late_ref, features_in_hbm, weights_hbm, bias_hbm, features_hbm,
    weights_ref, bias_ref, tap_scr, turn_scr, dilated_scr, sems, *, weight_scale, bias_scale,
):
    tile = lax.axis_index("tile")
    late = pltpu.make_async_copy(late_ref, features_hbm.at[1], sems.at[0])
    late.start()
    total = (own_ref[...] + a_ref[...].astype(F32)) + (b_ref[...].astype(F32) + c_ref[...].astype(F32))
    bias = total[(BLOCKS - 1) * 8 :, :] * bias_scale
    index = lax.broadcasted_iota(jnp.int32, bias.shape, 0)
    bias_ref[...] = jnp.sum(jnp.where(index == tile, bias, 0.0), axis=0, keepdims=True)[:, 0:CH]
    bias_out = pltpu.make_async_copy(bias_ref, bias_hbm, sems.at[1])
    bias_out.start()
    total = total * weight_scale
    other = pltpu.roll(total, CH, 1)
    for block in range(8):
        for half, source in enumerate((total, other)):
            tap = block // 2 * 4 + ((1, 2), (3, 0))[block % 2][half]
            tap_scr[pl.ds(tap, 8, stride=16), :] = source[block * 8 : block * 8 + 8, :]
    lines = tap_scr[...].T[0:CH, :].reshape(8, 8, 128)
    sub = lax.broadcasted_iota(jnp.int32, lines.shape, 1)
    chunk = lax.broadcasted_iota(jnp.int32, lines.shape, 2) // 16
    for step in (1, 2, 4):
        up = pltpu.roll(pltpu.roll(lines, 8 - step, 1), 16 * step, 2)
        down = pltpu.roll(pltpu.roll(lines, step, 1), 128 - 16 * step, 2)
        high, wide = sub // step % 2, chunk // step % 2
        lines = jnp.where(high == wide, lines, jnp.where(high == 0, up, down))
    for block in range(8):
        weights_ref[:, block * 128 : (block + 1) * 128] = lines[block]
    strided_part, dilated_part = pl.ds(0, 16 * CH), pl.ds(16 * CH, DIL_TAPS * CH)
    strided_out = pltpu.make_async_copy(weights_ref.at[:, strided_part], weights_hbm.at[:, strided_part], sems.at[2])
    strided_out.start()
    turn_scr[0:40, :] = total[64:104, :]
    turned = turn_scr[...].T
    for tap in range(DIL_TAPS):
        half = tap % 2
        dilated_scr[pl.ds(tap, CH, stride=DIL_TAPS), :] = turned[half * CH : (half + 1) * CH, :]
    spread = dilated_scr[...].T
    tap = lax.broadcasted_iota(jnp.int32, (8, DIL_TAPS * CH), 1) % DIL_TAPS
    result = spread[0:8, :]
    for j in range(1, 5):
        result = jnp.where(tap // 2 == j, spread[8 * j : 8 * j + 8, :], result)
    weights_ref[:, 16 * CH :] = result
    dilated_out = pltpu.make_async_copy(weights_ref.at[:, dilated_part], weights_hbm.at[:, dilated_part], sems.at[3])
    dilated_out.start()
    for copy in (late, bias_out, strided_out, dilated_out):
        copy.wait()


def feature_patch(pre_b_ref, wf_ref, out_ref, shift_scr):
    side = math.isqrt(pre_b_ref.shape[1])
    near = shifted_masks(side, 1)
    merge = merge_matrix(side)
    run, wide = 16 * side, 4 * side
    pre_b = pre_b_ref[...]
    for s, (dr, dc) in enumerate(SHIFTS):
        shift_scr[s * CH : (s + 1) * CH, :] = shifted(pre_b, dr, dc, side, 1, near)
    phases = dot(wf_ref[...], shift_scr[...]).astype(BF16)
    runs = out_ref.shape[1] // run
    stacked = jnp.concatenate(
        [
            jnp.concatenate(
                [phases[k * CH : (k + 1) * CH, q * wide : (q + 1) * wide] for k in range(4)], axis=1
            )
            for q in range(runs)
        ],
        axis=0,
    )
    merged = dot(stacked, merge).astype(BF16)
    for q in range(runs):
        out_ref[:, q * run : (q + 1) * run] = merged[q * CH : (q + 1) * CH, :]


def feature_first_kernel(pre_b_ref, wf_ref, out_ref, shift_scr):
    feature_patch(pre_b_ref, wf_ref, out_ref, shift_scr)


def feature_second_kernel(pre_b_ref, wf_ref, first_ref, out_ref, features_hbm, shift_scr, sem):
    copy = pltpu.make_async_copy(first_ref, features_hbm.at[0], sem)
    copy.start()
    feature_patch(pre_b_ref, wf_ref, out_ref, shift_scr)
    copy.wait()


SPACES = {"s": pltpu.SMEM, "v": pltpu.VMEM, "h": pltpu.HBM, "a": pl.ANY}


def call(kernel, outs, ins, scratch, *args, flops=0, out_spaces="", aliases=None):
    args = [
        pltpu.with_memory_space_constraint(arg, pltpu.HBM) if space == "h" else arg
        for space, arg in zip(ins, args)
    ]
    return pl.pallas_call(
        kernel,
        out_shape=[jax.ShapeDtypeStruct(shape, kind) for shape, kind in outs],
        in_specs=[pl.BlockSpec(memory_space=SPACES[space]) for space in ins],
        out_specs=[pl.BlockSpec(memory_space=SPACES[space]) for space in out_spaces or "v" * len(outs)],
        scratch_shapes=[pltpu.VMEM(*item) if isinstance(item, tuple) else item for item in scratch],
        input_output_aliases=aliases or {},
        compiler_params=pltpu.CompilerParams(vmem_limit_bytes=VMEM_LIMIT),
        cost_estimate=pl.CostEstimate(flops=flops, bytes_accessed=1 << 20, transcendentals=0),
    )(*args)


def device_pairs(x, pairs):
    tiles = lax.axis_size("tile")
    flat = [(source[0] * tiles + source[1], target[0] * tiles + target[1]) for source, target in pairs]
    return lax.ppermute(x, ("scene", "tile"), flat)


def scene_xor(x, distance):
    return lax.ppermute(x, "scene", [(i, i ^ distance) for i in range(lax.axis_size("scene"))])


def device_xor(x, scene_distance, tile_distance):
    scenes, tiles = range(lax.axis_size("scene")), range(lax.axis_size("tile"))
    return device_pairs(
        x, [((s, t), (s ^ scene_distance, t ^ tile_distance)) for s in scenes for t in tiles]
    )


def join_halves(give, keep):
    parts = [half.reshape(BLOCKS - 1, -1, 8, half.shape[-1]) for half in (give, keep)]
    first = lax.axis_index("scene") % 2 == 0
    pair = jnp.stack([jnp.where(first, parts[1], parts[0]), jnp.where(first, parts[0], parts[1])], axis=2)
    return pair.reshape(BLOCKS - 1, -1, pair.shape[-1])


def reduce_anywhere(blocks, bias_row, tile_owner, bias_rows, weight_scale, bias_scale):
    channels = blocks.shape[1]
    scene = lax.axis_index("scene")
    scenes, tiles = lax.axis_size("scene"), lax.axis_size("tile")
    halves = blocks.reshape(BLOCKS - 1, channels, 2, channels)
    strided, dilated = [None] * 16, []
    for block in range(8):
        for half in range(2):
            strided[block // 2 * 4 + ((1, 2), (3, 0))[block % 2][half]] = halves[block, :, half]
    for tap in range(DIL_TAPS):
        dilated.append(halves[8 + tap // 2, :, tap % 2])
    row = jnp.concatenate(
        [
            jnp.stack(strided, axis=-1).reshape(channels, 16 * channels),
            jnp.stack(dilated, axis=-1).reshape(channels, DIL_TAPS * channels),
        ],
        axis=1,
    )
    hit = jnp.arange(2, dtype=jnp.int32)[:, None, None] == scene % 2
    term = jnp.where(hit, row[None] * weight_scale, 0.0).reshape(2 * channels, 25 * channels)
    weights = lax.psum(lax.psum_scatter(term, "scene", scatter_dimension=0, tiled=True), "tile")
    tile_id = lax.dynamic_index_in_dim(tile_owner, scene, 0, keepdims=False)
    owned = jnp.arange(scenes * tiles * bias_rows, dtype=jnp.int32) == tile_id
    bias = jnp.where(owned[:, None], bias_row[None, :channels] * bias_scale, 0.0)
    return weights, lax.psum_scatter(bias, ("scene", "tile"), scatter_dimension=0, tiled=True)


def local(
    features_in,
    strided_weights,
    dilated_weights,
    tile_bias,
    cost_cotangent,
    footprint_pairing,
    valid_counts,
    tile_owner,
):
    features, own_cot = features_in[0], cost_cotangent[0]
    patches, channels, cells_in = features.shape
    cells = own_cot.shape[1]
    scenes, tiles = lax.axis_size("scene"), lax.axis_size("tile")
    weight_scale = 1.0 / math.sqrt(scenes * patches * tiles * cells)
    bias_scale = 1.0 / math.sqrt(patches * tiles * cells)
    bias_rows = tile_bias.shape[0] // (scenes * tiles)
    grid = (channels, cells)
    payload = (cells * channels // 128 + 16, 128)
    chunked = scenes == 16 and tiles == 2 and patches == 2 and bias_rows == 1
    wscr = ((16 * channels, 2 * channels), F32)
    im_scr = ((8 * channels, cells), BF16)
    patch_outs = [((4 * channels, cells), BF16), (grid, F32), (grid, BF16), (payload, BF16)]
    first_outs = patch_outs + [
        ((4 * channels, 4 * channels), BF16),
        ((3 * channels, 3 * channels), BF16),
        ((channels, 128), F32),
        (own_cot.shape, BF16),
    ]
    *part, w_strided, w_dilated, bias_col, cot = call(
        first_kernel,
        first_outs,
        "hhhhhh",
        [
            ((channels, cells_in), BF16),
            (strided_weights.shape[1:], BF16),
            (dilated_weights.shape[1:], BF16),
            (tile_bias.shape, F32),
            pltpu.SMEM(tile_owner.shape, jnp.int32),
            wscr,
            im_scr,
            pltpu.SemaphoreType.DMA((6,)),
        ],
        tile_owner, features, strided_weights, dilated_weights, tile_bias, own_cot,
        flops=10**9,
    )
    far = [device_xor(part[3], 1, 1)]
    *late, both = call(
        later_kernel,
        patch_outs + [((2,) + payload, BF16)],
        "vvvvvv",
        [im_scr],
        features, cot, w_strided, w_dilated, bias_col, part[3],
        flops=10**10,
    )
    far.append(device_xor(late[3], 1, 1))
    near = scene_xor(both, 1)
    phases, pre, act, send = zip(part, late)
    ordered = [(grid, F32)] * 2 + [(grid, BF16)] * 2 + [((4 * channels, cells), BF16)] * 2
    *both, w_feature, w_act, select, place, cots = call(
        functools.partial(prepare_kernel, bias_rows=bias_rows),
        ordered
        + [
            ((4 * channels, 9 * channels), BF16),
            ((channels, 9 * channels), BF16),
            ((16, 128), F32),
            ((128, 128), F32),
            ((32, 128), F32),
        ],
        "hhhvvvvvvvvvv",
        [
            pltpu.SMEM(footprint_pairing.shape[::-1], jnp.int32),
            pltpu.SMEM(valid_counts.shape, jnp.int32),
            pltpu.SMEM(tile_owner.shape, jnp.int32),
            wscr,
            pltpu.SemaphoreType.DMA((3,)),
        ],
        footprint_pairing.T, valid_counts, tile_owner, strided_weights, dilated_weights,
        *pre, *act, *phases, *send,
        flops=10**10,
    )
    slope, act, phases = both[0:2], both[2:4], both[4:6]
    shift_scr = ((9 * channels, cells), BF16)
    sums = [((9 * channels, 128), F32), ((9 * channels, 4 * channels), F32)]
    picked, *first = call(
        backward_first_kernel,
        [(payload, BF16), (grid, BF16), ((channels, 128), F32)] + sums,
        "v" * 8,
        [shift_scr],
        far[0], near, select, cots, w_act, act[0], slope[0], phases[0],
        flops=10**9,
    )
    half_shift = ((9 * channels // 2, cells), BF16)
    grads_shape = ((4, BLOCKS * 8, 128), BF16) if chunked else ((BLOCKS - 1, channels // 2, 128), F32)
    last, bias, give, out_shifts = call(
        functools.partial(backward_second_kernel, chunked=chunked),
        [(grid, BF16), ((8, 128), F32), grads_shape, shift_scr],
        "v" * 11,
        [half_shift],
        far[1], picked, select, cots, w_act, act[1], slope[1], phases[1], *first[1:],
        flops=10**9,
    )
    if chunked:
        got = scene_xor(give, 1)
    keep, *pre_b = call(
        functools.partial(backward_kept_kernel, chunked=chunked),
        [grads_shape] + [(grid, BF16)] * 2,
        "v" * 8,
        [half_shift],
        select, out_shifts, last, first[0], act[1], phases[1], *first[2:],
        flops=10**9,
    )
    feature_shape = ((channels, cells_in), BF16)
    if chunked:
        stage = ((2 * BLOCKS * 8, 128), BF16)
        own, by_y, by_z, by_zy = call(spread_kernel, [stage] * 4, "vvvv", [], place, bias, keep, got)
        by_zy, by_z, by_y = scene_xor(by_zy, 6), scene_xor(by_z, 4), scene_xor(by_y, 2)
    (feature_first,) = call(
        feature_first_kernel, [feature_shape], "vv", [shift_scr], pre_b[0], w_feature, flops=10**9
    )
    chunk = (BLOCKS * 8, 128)
    if chunked:
        feature_first, own = lax.optimization_barrier((feature_first, own))
        kept, stay, cross = call(
            join_kernel, [(chunk, F32), (chunk, BF16), (chunk, BF16)], "vvvv", [], own, by_zy, by_z, by_y
        )
        by_zx, by_z, by_x = device_xor(cross, 8, 1), device_xor(cross, 8, 0), device_xor(stay, 0, 1)
    feature_last, feature_grads = call(
        feature_second_kernel,
        [feature_shape, (features.shape, BF16)],
        "vvv",
        [shift_scr, pltpu.SemaphoreType.DMA],
        pre_b[1], w_feature, feature_first,
        flops=10**9,
        out_spaces="vh",
    )
    if not chunked:
        feature_grads = feature_grads.at[1].set(feature_last)
        grad_weights, grad_bias = reduce_anywhere(
            join_halves(give, keep), bias[0], tile_owner, bias_rows, weight_scale, bias_scale
        )
        return (feature_grads[None], grad_weights, grad_bias)
    grad_weights, grad_bias, feature_grads = call(
        functools.partial(finish_kernel, weight_scale=weight_scale, bias_scale=bias_scale),
        [((8, 25 * channels), F32), ((1, channels), F32), (features.shape, BF16)],
        "vvvvva",
        [
            ((8, 25 * channels), F32),
            ((1, channels), F32),
            ((128, 128), F32),
            ((128, 128), F32),
            ((9 * channels, 128), F32),
            pltpu.SemaphoreType.DMA((4,)),
        ],
        kept, by_zx, by_z, by_x, feature_last, feature_grads,
        out_spaces="hhh",
        aliases={5: 2},
    )
    return (feature_grads[None], grad_weights, grad_bias)


def solution(mesh):
    return jax.shard_map(
        local,
        mesh=mesh,
        in_specs=(
            P("scene", "tile", None, None),
            P(),
            P(),
            P(),
            P("scene", "tile", None),
            P(),
            P(),
            P(),
        ),
        out_specs=(P("scene", "tile", None, None), P("scene", None), P(("scene", "tile"), None)),
        check_vma=False,
    )
```

```python
import functools
import math

import jax
import jax.numpy as jnp
from jax import lax
from jax.experimental import pallas as pl
from jax.experimental.pallas import tpu as pltpu
from jax.sharding import PartitionSpec as P

CH = 64
ROW_TAPS = 4
DIL_TAPS = 9
BLOCKS = 14
SHIFTS = [(dr, dc) for dr in (-1, 0, 1) for dc in (-1, 0, 1)]
F32 = jnp.float32
BF16 = jnp.bfloat16
VMEM_LIMIT = 24 * 1024 * 1024


def shift_index(dr, dc):
    return (dr + 1) * 3 + dc + 1


def dot(a, b):
    return lax.dot_general(a, b, (((1,), (0,)), ((), ())), preferred_element_type=F32)


def dot_nt(a, b):
    return lax.dot_general(a, b, (((1,), (1,)), ((), ())), preferred_element_type=F32)


def shifted_masks(side, reach):
    cell = lax.broadcasted_iota(jnp.int32, (1, side * side), 1)
    row, col = cell // side, cell % side
    masks = {}
    for dr, dc in SHIFTS:
        ok = (
            (row + dr * reach >= 0)
            & (row + dr * reach < side)
            & (col + dc * reach >= 0)
            & (col + dc * reach < side)
        )
        masks[dr, dc] = ok.astype(F32).astype(BF16)
    return masks


def shifted(x, dr, dc, side, reach, masks):
    if dr == 0 and dc == 0:
        return x
    cells = side * side
    return pltpu.roll(x, (-(dr * side + dc) * reach) % cells, 1) * masks[dr, dc].astype(x.dtype)


def merge_matrix(side):
    size = 16 * side
    dims = (size, size)
    source = lax.broadcasted_iota(jnp.int32, dims, 1)
    target = lax.broadcasted_iota(jnp.int32, dims, 0)
    phase, cell = target // (4 * side), target % (4 * side)
    row, col = cell // side, cell % side
    wanted = (2 * row + phase // 2) * (2 * side) + 2 * col + phase % 2
    return jnp.where(source == wanted, 1.0, 0.0).astype(BF16)


def halves(values, core):
    even = jnp.concatenate([values[16 * m : 16 * m + 8] for m in range(CH // 16)], axis=0)
    odd = jnp.concatenate([values[16 * m + 8 : 16 * m + 16] for m in range(CH // 16)], axis=0)
    return jnp.where(core == 0, odd, even), jnp.where(core == 0, even, odd)


def half_run_matrix(side, odd):
    dims = (8 * side, 8 * side)
    source, target = (lax.broadcasted_iota(jnp.int32, dims, k) for k in range(2))
    phase, cell = target // (2 * side) ^ odd, target % (2 * side)
    row, col = cell // side, cell % side
    wanted = (2 * row + phase // 2) * (2 * side) + 2 * col + phase % 2
    return jnp.where(source == wanted, 1.0, 0.0).astype(BF16)


TAP_LINES = {0: (1, -1), 1: (0, 0), 2: (1, 0), 3: (0, 1)}
ROW_ORDER = (1, 3, 2, 0)


def tap_matrices(weight, taps, scratch):
    scratch[0 : CH * taps, 0:CH] = weight.astype(F32).T
    return [scratch[pl.ds(tap, CH, stride=taps), 0:CH] for tap in range(taps)]


def forward_patch(x_ref, cot, w_strided, w_dilated, bias_col, ph_ref, pre_ref, act_ref, send_ref, im_scr):
    side = math.isqrt(x_ref.shape[1]) // 2
    run, lanes = 16 * side, side * side // 128
    near, far = shifted_masks(side, 1), shifted_masks(side, 2)
    runs, wide = x_ref.shape[1] // run, 4 * side
    even, odd = (
        dot(
            jnp.concatenate(
                [x_ref[:, q * run + h * run // 2 : q * run + (h + 1) * run // 2] for q in range(runs)], axis=0
            ),
            half_run_matrix(side, h),
        )
        for h in range(2)
    )
    lower = lax.broadcasted_iota(jnp.int32, (runs * CH, wide), 1) < wide // 2
    for pr in range(2):
        one, two = even[:, pr * wide : (pr + 1) * wide], odd[:, pr * wide : (pr + 1) * wide]
        first = jnp.where(lower, one, two).astype(BF16)
        second = pltpu.roll(jnp.where(lower, two, one).astype(BF16), wide // 2, 1)
        for pc, lines in ((0, first), (1, second)):
            for q in range(runs):
                at = (pr * 2 + pc) * CH
                ph_ref[at : at + CH, q * wide : (q + 1) * wide] = lines[q * CH : (q + 1) * CH]
    sums = []
    for pr in range(2):
        for ct in range(4):
            pc, dc = TAP_LINES[ct]
            at, phase = (pr * 4 + ct) * CH, pr * 2 + pc
            im_scr[at : at + CH, :] = shifted(ph_ref[phase * CH : (phase + 1) * CH, :], 0, dc, side, 1, near)
        both = dot(w_strided[pr * 2 * CH : (pr + 1) * 2 * CH], im_scr[pr * 4 * CH : (pr + 1) * 4 * CH, :])
        dr = TAP_LINES[ROW_ORDER[2 * pr + 1]][1]
        sums.append(both[:CH] + shifted(both[CH:], dr, 0, side, 1, near))
    pre = sums[0] + sums[1] + bias_col
    pre_ref[...] = pre
    act = (pre * (1.0 / (1.0 + jnp.exp(-pre)))).astype(BF16)
    act_ref[...] = act
    for k in range(3):
        im_scr[k * CH : (k + 1) * CH, :] = shifted(act, 0, k - 1, side, 2, far)
    rows = dot(w_dilated, im_scr[0 : 3 * CH, :])
    out = rows[CH : 2 * CH]
    for k in (0, 2):
        out = out + shifted(rows[k * CH : (k + 1) * CH], k - 1, 0, side, 2, far)
    out = out.astype(BF16)
    for lane in range(lanes):
        send_ref[lane * CH : (lane + 1) * CH, :] = out[:, lane * 128 : (lane + 1) * 128]
    rows = [cot[:, lane * 128 : (lane + 1) * 128] for lane in range(lanes)]
    rows.append(jnp.zeros((16 - lanes, 128), F32))
    send_ref[lanes * CH :, :] = jnp.concatenate(rows, axis=0).astype(BF16)


def first_kernel(
    owner_hbm, x_hbm, ws_hbm, wd_hbm, bias_hbm, cot_hbm,
    ph_ref, pre_ref, act_ref, send_ref, strided_ref, dilated_ref, bias_ref, cot_ref,
    x_ref, ws_ref, wd_ref, table_ref, owner_ref, wscr, im_scr, sems,
):
    scene = lax.axis_index("scene")
    branch = scene % 2
    copies = [
        pltpu.make_async_copy(source, target, sems.at[i])
        for i, (source, target) in enumerate(
            [
                (x_hbm.at[0], x_ref),
                (ws_hbm.at[branch], ws_ref),
                (wd_hbm.at[branch], wd_ref),
                (owner_hbm, owner_ref),
                (bias_hbm, table_ref),
                (cot_hbm, cot_ref),
            ]
        )
    ]
    for copy in copies:
        copy.start()
    for copy in copies:
        copy.wait()
    mats = tap_matrices(ws_ref[...], 16, wscr)
    for k, rt in enumerate(ROW_ORDER):
        line = jnp.concatenate(mats[rt * 4 : rt * 4 + 4], axis=0)
        strided_ref[k * CH : (k + 1) * CH, :] = line.T.astype(BF16)
    mats = tap_matrices(wd_ref[...], 9, wscr)
    for k in range(3):
        line = jnp.concatenate(mats[3 * k : 3 * k + 3], axis=0)
        dilated_ref[k * CH : (k + 1) * CH, :] = line.T.astype(BF16)
    bias_row = table_ref[pl.ds(owner_ref[scene], 1), :]
    bias_ref[...] = jnp.broadcast_to(jnp.broadcast_to(bias_row, (8, CH)).T[:, 0:1], (CH, 128))
    forward_patch(
        x_ref, cot_ref[...].astype(F32)[0:1, :], strided_ref[...], dilated_ref[...], bias_ref[:, 0:1],
        ph_ref, pre_ref, act_ref, send_ref, im_scr,
    )


def later_kernel(
    x_ref, cot_ref, w_strided_ref, w_dilated_ref, bias_ref, sent_ref,
    ph_ref, pre_ref, act_ref, send_ref, both_ref, im_scr,
):
    forward_patch(
        x_ref.at[1], cot_ref[...].astype(F32)[1:2, :], w_strided_ref[...], w_dilated_ref[...],
        bias_ref[:, 0:1], ph_ref, pre_ref, act_ref, send_ref, im_scr,
    )
    both_ref[0] = sent_ref[...]
    both_ref[1] = send_ref[...]


def prepare_kernel(
    pairing_hbm, valid_hbm, owner_hbm, ws_ref, wd_ref, *refs, bias_rows
):
    pre_refs, act_refs, ph_refs, send_refs = (refs[2 * k : 2 * k + 2] for k in range(4))
    (
        slope_first, slope_second, act_first, act_second, ph_first, ph_second,
        wf_ref, wt_ref, select_ref, place_ref, cot_ref,
        pairing_ref, valid_ref, owner_ref, wscr, sems,
    ) = refs[8:]
    copies = [
        pltpu.make_async_copy(source, target, sems.at[i])
        for i, (source, target) in enumerate(
            [(pairing_hbm, pairing_ref), (valid_hbm, valid_ref), (owner_hbm, owner_ref)]
        )
    ]
    for copy in copies:
        copy.start()
    scene, tile = lax.axis_index("scene"), lax.axis_index("tile")
    branch, pair = scene % 2, scene // 2
    mats = tap_matrices(ws_ref[branch], 16, wscr)
    blocks = {}
    for rt in range(4):
        for ct in range(4):
            (pr, dr), (pc, dc) = TAP_LINES[rt], TAP_LINES[ct]
            blocks[pr * 2 + pc, shift_index(-dr, -dc)] = mats[rt * 4 + ct]
    zero = jnp.zeros((CH, CH), F32)
    for phase in range(4):
        row = [blocks.get((phase, s), zero) for s in range(9)]
        wf_ref[phase * CH : (phase + 1) * CH, :] = jnp.concatenate(row, axis=1).astype(BF16)
    give, keep = halves(wd_ref[branch].astype(F32), branch)
    mats = tap_matrices(jnp.concatenate([give, keep], axis=0), 9, wscr)[::-1]
    half = CH // 2
    wt_ref[...] = jnp.concatenate(
        [mat[:, h * half : (h + 1) * half] for h in range(2) for mat in mats], axis=1
    ).astype(BF16)
    slopes = []
    for pre_ref in pre_refs:
        pre = pre_ref[...]
        gate = 1.0 / (1.0 + jnp.exp(-pre))
        slopes.append(gate * (1.0 + pre * (1.0 - gate)))
    for copy in copies:
        copy.wait()
    total = pairing_ref.shape[0]
    matches = []
    for p in range(2):
        position = tile * 2 + p
        matched, inverse = pairing_ref[position, pair], jnp.int32(0)
        for i in range(total):
            inverse = inverse + jnp.where(pairing_ref[i, pair] == position, i, 0)
        matched = jnp.where(branch == 0, matched, inverse)
        matches.append(jnp.where(matched // 2 == tile, 0, 2) + matched % 2)
    swapped = matches[0] == 3
    slope_first[...] = jnp.where(swapped, slopes[1], slopes[0])
    slope_second[...] = jnp.where(swapped, slopes[0], slopes[1])
    for first, second, pairs in ((act_first, act_second, act_refs), (ph_first, ph_second, ph_refs)):
        first[...] = jnp.where(swapped, pairs[1][...], pairs[0][...])
        second[...] = jnp.where(swapped, pairs[0][...], pairs[1][...])
    rows = send_refs[0].shape[0] - 16
    cots = [ref[rows:, :].astype(F32) for ref in send_refs]
    cot_ref[0:16, :] = jnp.where(swapped, cots[1], cots[0])
    cot_ref[16:32, :] = jnp.where(swapped, cots[0], cots[1])
    row = lax.broadcasted_iota(jnp.int32, select_ref.shape, 0)
    select = jnp.zeros(select_ref.shape, F32)
    for p in range(2):
        position = jnp.where(swapped, 1 - p, p)
        live = jnp.where(tile * 2 + p < valid_ref[pair], 8 + position, -1)
        select = jnp.where((row == position * 4 + matches[p]) | (row == live), 1.0, select)
    select_ref[...] = jnp.where(row == jnp.where(swapped, 10, -1), 1.0, select)
    row = lax.broadcasted_iota(jnp.int32, place_ref.shape, 0)
    here = scene // 2 % 4
    place = jnp.zeros(place_ref.shape, F32)
    for k, source in enumerate((scene, scene ^ 1)):
        owner = owner_ref[source]
        target = owner // (2 * bias_rows)
        half = jnp.where(target // 8 == branch, 0, 1)
        wanted = k * 64 + ((target // 2 % 4) ^ here) * 16 + half * 8 + owner % (2 * bias_rows)
        place = jnp.where(row == jnp.where(target % 2 == branch, wanted, -1), 1.0, place)
    place_ref[...] = place


HALF = 9 * CH // 2


def shift_rows(pieces, reach, side, target):
    masks = shifted_masks(side, reach)
    rows = CH // 2
    for h, piece in enumerate(pieces):
        for s, (dr, dc) in enumerate(SHIFTS):
            at = h * HALF + s * rows
            target[at : at + rows, :] = shifted(piece, dr, dc, side, reach, masks)


def pick(position, candidates, select_ref, first=0):
    partner = None
    for k, payload in enumerate(candidates, first):
        term = payload * select_ref[position * 4 + k : position * 4 + k + 1, :].astype(BF16)
        partner = term if partner is None else partner + term
    return partner


def backward_patch(position, partner, select_ref, cot_ref, wt_ref, slope_ref, shift_scr):
    side = math.isqrt(slope_ref.shape[1])
    lanes = side * side // 128
    core = lax.axis_index("scene") % 2
    live = select_ref[8 + position : 9 + position, :]
    signal = (cot_ref[position * 16 : position * 16 + 16, :] + partner[lanes * CH :, :].astype(F32)) * live
    out_grad = jnp.concatenate(
        [signal[j : j + 1, :] * partner[j * CH : (j + 1) * CH, :].astype(F32) for j in range(lanes)], axis=1
    )
    shift_rows([piece.astype(BF16) for piece in halves(out_grad, core)], 2, side, shift_scr)
    return dot(wt_ref[...], shift_scr[...]) * slope_ref[...]


def backward_first_kernel(
    far0_ref, near_ref, select_ref, cot_ref, wt_ref, act_ref, slope_ref, ph_ref,
    pick_ref, pre_b_ref, bias_ref, dilated_ref, strided_ref, shift_scr,
):
    side = math.isqrt(slope_ref.shape[1])
    core = lax.axis_index("scene") % 2
    candidates = (near_ref[0], near_ref[1], far0_ref[...])
    pick_ref[...] = pick(1, candidates, select_ref)
    pre_grad = backward_patch(0, pick(0, candidates, select_ref), select_ref, cot_ref, wt_ref, slope_ref, shift_scr)
    act = act_ref[...]
    dilated_ref[...] = dot_nt(shift_scr[...], jnp.concatenate([act, act], axis=0))
    bias_ref[...] = jnp.broadcast_to(jnp.sum(pre_grad, axis=1, keepdims=True), bias_ref.shape)
    pre_b_ref[...] = pre_grad.astype(BF16)
    shift_rows([piece.astype(BF16) for piece in halves(pre_grad, core)], 1, side, shift_scr)
    strided_ref[...] = dot_nt(shift_scr[...], ph_ref[...])


def tap_blocks(strided, dilated):
    rows = CH // 2
    lower = lax.broadcasted_iota(jnp.int32, (rows, 2 * CH), 1) < CH

    def strided_piece(pr, shift):
        return strided[shift * rows : (shift + 1) * rows, pr * 2 * CH : (pr + 1) * 2 * CH]

    blocks = []
    for rt in range(4):
        pr, dr = TAP_LINES[rt]
        blocks.append(strided_piece(pr, shift_index(-dr, 0)))
        blocks.append(
            jnp.where(lower, strided_piece(pr, shift_index(-dr, -1)), strided_piece(pr, shift_index(-dr, 1)))
        )
    for j in range(5):
        low = dilated[(8 - 2 * j) * rows : (9 - 2 * j) * rows, :]
        high = dilated[(7 - 2 * j) * rows : (8 - 2 * j) * rows, :] if j < 4 else jnp.zeros_like(low)
        blocks.append(jnp.where(lower, low, high))
    return blocks


def write_blocks(blocks, bias_wide, ref, chunked):
    if not chunked:
        for i, block in enumerate(blocks):
            ref[i] = block
        return
    here = lax.axis_index("scene") // 2 % 4
    for m in range(4):
        pieces = [block[8 * m : 8 * m + 8] for block in blocks] + [bias_wide]
        ref[here ^ m] = jnp.concatenate(pieces, axis=0).astype(BF16)


def backward_second_kernel(
    far1_ref, pick_ref, select_ref, cot_ref, wt_ref, act_ref, slope_ref, ph_ref,
    other_bias_ref, other_dilated_ref, other_strided_ref,
    pre_b_ref, bias_ref, give_ref, out_shifts_ref, shift_scr, *, chunked,
):
    side = math.isqrt(slope_ref.shape[1])
    core = lax.axis_index("scene") % 2
    partner = pick_ref[...] + pick(1, (far1_ref[...],), select_ref, 3)
    pre_grad = backward_patch(1, partner, select_ref, cot_ref, wt_ref, slope_ref, out_shifts_ref)
    act = act_ref[...]
    dilated = dot_nt(out_shifts_ref[0:HALF, :], jnp.concatenate([act, act], axis=0))
    give, _ = halves(pre_grad, core)
    shift_rows([give.astype(BF16)], 1, side, shift_scr)
    strided = dot_nt(shift_scr[...], ph_ref[...])
    pre_b_ref[...] = pre_grad.astype(BF16)
    bias_wide = (jnp.sum(pre_grad, axis=1, keepdims=True) + other_bias_ref[...]).T[0:8, :]
    bias_wide = jnp.concatenate([bias_wide, jnp.zeros_like(bias_wide)], axis=1)
    bias_ref[...] = bias_wide
    blocks = tap_blocks(strided + other_strided_ref[0:HALF, :], dilated + other_dilated_ref[0:HALF, :])
    write_blocks(blocks, bias_wide, give_ref, chunked)


def backward_kept_kernel(
    select_ref, out_shifts_ref, pre_b_ref, other_ref, act_ref, ph_ref, other_dilated_ref, other_strided_ref,
    keep_ref, pre_b0_ref, pre_b1_ref, shift_scr, *, chunked,
):
    side = math.isqrt(act_ref.shape[1])
    act = act_ref[...]
    dilated = dot_nt(out_shifts_ref[HALF:, :], jnp.concatenate([act, act], axis=0))
    pre_b, other = pre_b_ref[...], other_ref[...]
    _, keep = halves(pre_b.astype(F32), lax.axis_index("scene") % 2)
    shift_rows([keep.astype(BF16)], 1, side, shift_scr)
    strided = dot_nt(shift_scr[...], ph_ref[...])
    blocks = tap_blocks(strided + other_strided_ref[HALF:, :], dilated + other_dilated_ref[HALF:, :])
    write_blocks(blocks, jnp.zeros((8, 2 * CH), F32), keep_ref, chunked)
    swapped = select_ref[10:11, 0:1].astype(BF16)
    straight = 1.0 - swapped
    pre_b0_ref[...] = other * straight + pre_b * swapped
    pre_b1_ref[...] = other * swapped + pre_b * straight


def spread_kernel(place_ref, bias_ref, keep_ref, got_ref, *out_refs):
    rows = keep_ref.shape[1]
    top = lax.broadcasted_iota(jnp.int32, (16, 128), 0) < 8
    mine = bias_ref[0:1, :]
    theirs = got_ref[0, rows - 16 :, :].astype(F32)[8:9, :]
    for d, out_ref in enumerate(out_refs):
        for half, ref in enumerate((keep_ref, got_ref)):
            at = d * 16 + half * 8
            bias = place_ref[at : at + 8, :] * mine + place_ref[64 + at : 72 + at, :] * theirs
            last = ref[d, rows - 16 :, :].astype(F32)
            last = jnp.where(top, last, jnp.concatenate([bias, bias], axis=0))
            out_ref[half * rows : (half + 1) * rows - 16, :] = ref[d, : rows - 16, :]
            out_ref[(half + 1) * rows - 16 : (half + 1) * rows, :] = last.astype(BF16)


def join_kernel(own_ref, a_ref, b_ref, c_ref, keep_ref, stay_ref, cross_ref):
    scene = lax.axis_index("scene")
    rows = keep_ref.shape[0]
    total = (own_ref[...].astype(F32) + a_ref[...].astype(F32)) + (
        b_ref[...].astype(F32) + c_ref[...].astype(F32)
    )
    mine, theirs = total[:rows, :], total[rows:, :]
    first = scene // 8 == scene % 2
    kept = jnp.where(first, mine, theirs)
    keep_ref[...] = kept
    stay_ref[...] = kept.astype(BF16)
    cross_ref[...] = jnp.where(first, theirs, mine).astype(BF16)


def finish_kernel(
    own_ref, a_ref, b_ref, c_ref, weights_hbm, bias_hbm,
    weights_ref, bias_ref, tap_scr, turn_scr, dilated_scr, sems, *, weight_scale, bias_scale,
):
    tile = lax.axis_index("tile")
    total = (own_ref[...] + a_ref[...].astype(F32)) + (b_ref[...].astype(F32) + c_ref[...].astype(F32))
    bias = total[(BLOCKS - 1) * 8 :, :] * bias_scale
    index = lax.broadcasted_iota(jnp.int32, bias.shape, 0)
    bias_ref[...] = jnp.sum(jnp.where(index == tile, bias, 0.0), axis=0, keepdims=True)[:, 0:CH]
    bias_out = pltpu.make_async_copy(bias_ref, bias_hbm, sems.at[0])
    bias_out.start()
    total = total * weight_scale
    other = pltpu.roll(total, CH, 1)
    for block in range(8):
        for half, source in enumerate((total, other)):
            tap = block // 2 * 4 + ((1, 2), (3, 0))[block % 2][half]
            tap_scr[pl.ds(tap, 8, stride=16), :] = source[block * 8 : block * 8 + 8, :]
    lines = tap_scr[...].T[0:CH, :].reshape(8, 8, 128)
    sub = lax.broadcasted_iota(jnp.int32, lines.shape, 1)
    chunk = lax.broadcasted_iota(jnp.int32, lines.shape, 2) // 16
    for step in (1, 2, 4):
        up = pltpu.roll(pltpu.roll(lines, 8 - step, 1), 16 * step, 2)
        down = pltpu.roll(pltpu.roll(lines, step, 1), 128 - 16 * step, 2)
        high, wide = sub // step % 2, chunk // step % 2
        lines = jnp.where(high == wide, lines, jnp.where(high == 0, up, down))
    for block in range(8):
        weights_ref[:, block * 128 : (block + 1) * 128] = lines[block]
    strided_part, dilated_part = pl.ds(0, 16 * CH), pl.ds(16 * CH, DIL_TAPS * CH)
    strided_out = pltpu.make_async_copy(weights_ref.at[:, strided_part], weights_hbm.at[:, strided_part], sems.at[1])
    strided_out.start()
    turn_scr[0:40, :] = total[64:104, :]
    turned = turn_scr[...].T
    for tap in range(DIL_TAPS):
        half = tap % 2
        dilated_scr[pl.ds(tap, CH, stride=DIL_TAPS), :] = turned[half * CH : (half + 1) * CH, :]
    spread = dilated_scr[...].T
    tap = lax.broadcasted_iota(jnp.int32, (8, DIL_TAPS * CH), 1) % DIL_TAPS
    result = spread[0:8, :]
    for j in range(1, 5):
        result = jnp.where(tap // 2 == j, spread[8 * j : 8 * j + 8, :], result)
    weights_ref[:, 16 * CH :] = result
    dilated_out = pltpu.make_async_copy(weights_ref.at[:, dilated_part], weights_hbm.at[:, dilated_part], sems.at[2])
    dilated_out.start()
    for copy in (bias_out, strided_out, dilated_out):
        copy.wait()


def feature_patch(pre_b_ref, wf_ref, out_ref, shift_scr):
    side = math.isqrt(pre_b_ref.shape[1])
    near = shifted_masks(side, 1)
    merge = merge_matrix(side)
    run, wide = 16 * side, 4 * side
    pre_b = pre_b_ref[...]
    for s, (dr, dc) in enumerate(SHIFTS):
        shift_scr[s * CH : (s + 1) * CH, :] = shifted(pre_b, dr, dc, side, 1, near)
    phases = dot(wf_ref[...], shift_scr[...]).astype(BF16)
    runs = out_ref.shape[1] // run
    stacked = jnp.concatenate(
        [
            jnp.concatenate(
                [phases[k * CH : (k + 1) * CH, q * wide : (q + 1) * wide] for k in range(4)], axis=1
            )
            for q in range(runs)
        ],
        axis=0,
    )
    merged = dot(stacked, merge).astype(BF16)
    for q in range(runs):
        out_ref[:, q * run : (q + 1) * run] = merged[q * CH : (q + 1) * CH, :]


def feature_kernel(pre_b0_ref, pre_b1_ref, wf_ref, out_ref, shift_scr):
    for p, pre_b_ref in enumerate((pre_b0_ref, pre_b1_ref)):
        feature_patch(pre_b_ref, wf_ref, out_ref.at[p], shift_scr)


def store_kernel(features_ref, out_hbm, sem):
    copy = pltpu.make_async_copy(features_ref, out_hbm, sem)
    copy.start()
    copy.wait()


SPACES = {"s": pltpu.SMEM, "v": pltpu.VMEM, "h": pltpu.HBM, "a": pl.ANY}


def call(kernel, outs, ins, scratch, *args, flops=0, out_spaces="", aliases=None):
    args = [
        pltpu.with_memory_space_constraint(arg, pltpu.HBM) if space == "h" else arg
        for space, arg in zip(ins, args)
    ]
    return pl.pallas_call(
        kernel,
        out_shape=[jax.ShapeDtypeStruct(shape, kind) for shape, kind in outs],
        in_specs=[pl.BlockSpec(memory_space=SPACES[space]) for space in ins],
        out_specs=[pl.BlockSpec(memory_space=SPACES[space]) for space in out_spaces or "v" * len(outs)],
        scratch_shapes=[pltpu.VMEM(*item) if isinstance(item, tuple) else item for item in scratch],
        input_output_aliases=aliases or {},
        compiler_params=pltpu.CompilerParams(vmem_limit_bytes=VMEM_LIMIT),
        cost_estimate=pl.CostEstimate(flops=flops, bytes_accessed=1 << 20, transcendentals=0),
    )(*args)


def device_pairs(x, pairs):
    tiles = lax.axis_size("tile")
    flat = [(source[0] * tiles + source[1], target[0] * tiles + target[1]) for source, target in pairs]
    return lax.ppermute(x, ("scene", "tile"), flat)


def scene_xor(x, distance):
    return lax.ppermute(x, "scene", [(i, i ^ distance) for i in range(lax.axis_size("scene"))])


def device_xor(x, scene_distance, tile_distance):
    scenes, tiles = range(lax.axis_size("scene")), range(lax.axis_size("tile"))
    return device_pairs(
        x, [((s, t), (s ^ scene_distance, t ^ tile_distance)) for s in scenes for t in tiles]
    )


def join_halves(give, keep):
    parts = [half.reshape(BLOCKS - 1, -1, 8, half.shape[-1]) for half in (give, keep)]
    first = lax.axis_index("scene") % 2 == 0
    pair = jnp.stack([jnp.where(first, parts[1], parts[0]), jnp.where(first, parts[0], parts[1])], axis=2)
    return pair.reshape(BLOCKS - 1, -1, pair.shape[-1])


def reduce_anywhere(blocks, bias_row, tile_owner, bias_rows, weight_scale, bias_scale):
    channels = blocks.shape[1]
    scene = lax.axis_index("scene")
    scenes, tiles = lax.axis_size("scene"), lax.axis_size("tile")
    halves = blocks.reshape(BLOCKS - 1, channels, 2, channels)
    strided, dilated = [None] * 16, []
    for block in range(8):
        for half in range(2):
            strided[block // 2 * 4 + ((1, 2), (3, 0))[block % 2][half]] = halves[block, :, half]
    for tap in range(DIL_TAPS):
        dilated.append(halves[8 + tap // 2, :, tap % 2])
    row = jnp.concatenate(
        [
            jnp.stack(strided, axis=-1).reshape(channels, 16 * channels),
            jnp.stack(dilated, axis=-1).reshape(channels, DIL_TAPS * channels),
        ],
        axis=1,
    )
    hit = jnp.arange(2, dtype=jnp.int32)[:, None, None] == scene % 2
    term = jnp.where(hit, row[None] * weight_scale, 0.0).reshape(2 * channels, 25 * channels)
    weights = lax.psum(lax.psum_scatter(term, "scene", scatter_dimension=0, tiled=True), "tile")
    tile_id = lax.dynamic_index_in_dim(tile_owner, scene, 0, keepdims=False)
    owned = jnp.arange(scenes * tiles * bias_rows, dtype=jnp.int32) == tile_id
    bias = jnp.where(owned[:, None], bias_row[None, :channels] * bias_scale, 0.0)
    return weights, lax.psum_scatter(bias, ("scene", "tile"), scatter_dimension=0, tiled=True)


def local(
    features_in,
    strided_weights,
    dilated_weights,
    tile_bias,
    cost_cotangent,
    footprint_pairing,
    valid_counts,
    tile_owner,
):
    features, own_cot = features_in[0], cost_cotangent[0]
    patches, channels, cells_in = features.shape
    cells = own_cot.shape[1]
    scenes, tiles = lax.axis_size("scene"), lax.axis_size("tile")
    weight_scale = 1.0 / math.sqrt(scenes * patches * tiles * cells)
    bias_scale = 1.0 / math.sqrt(patches * tiles * cells)
    bias_rows = tile_bias.shape[0] // (scenes * tiles)
    grid = (channels, cells)
    payload = (cells * channels // 128 + 16, 128)
    chunked = scenes == 16 and tiles == 2 and patches == 2 and bias_rows == 1
    wscr = ((16 * channels, 2 * channels), F32)
    im_scr = ((8 * channels, cells), BF16)
    patch_outs = [((4 * channels, cells), BF16), (grid, F32), (grid, BF16), (payload, BF16)]
    first_outs = patch_outs + [
        ((4 * channels, 4 * channels), BF16),
        ((3 * channels, 3 * channels), BF16),
        ((channels, 128), F32),
        (own_cot.shape, BF16),
    ]
    *part, w_strided, w_dilated, bias_col, cot = call(
        first_kernel,
        first_outs,
        "hhhhhh",
        [
            ((channels, cells_in), BF16),
            (strided_weights.shape[1:], BF16),
            (dilated_weights.shape[1:], BF16),
            (tile_bias.shape, F32),
            pltpu.SMEM(tile_owner.shape, jnp.int32),
            wscr,
            im_scr,
            pltpu.SemaphoreType.DMA((6,)),
        ],
        tile_owner, features, strided_weights, dilated_weights, tile_bias, own_cot,
        flops=10**9,
    )
    far = [device_xor(part[3], 1, 1)]
    *late, both = call(
        later_kernel,
        patch_outs + [((2,) + payload, BF16)],
        "vvvvvv",
        [im_scr],
        features, cot, w_strided, w_dilated, bias_col, part[3],
        flops=10**10,
    )
    far.append(device_xor(late[3], 1, 1))
    near = scene_xor(both, 1)
    phases, pre, act, send = zip(part, late)
    ordered = [(grid, F32)] * 2 + [(grid, BF16)] * 2 + [((4 * channels, cells), BF16)] * 2
    *both, w_feature, w_act, select, place, cots = call(
        functools.partial(prepare_kernel, bias_rows=bias_rows),
        ordered
        + [
            ((4 * channels, 9 * channels), BF16),
            ((channels, 9 * channels), BF16),
            ((16, 128), F32),
            ((128, 128), F32),
            ((32, 128), F32),
        ],
        "hhhvvvvvvvvvv",
        [
            pltpu.SMEM(footprint_pairing.shape[::-1], jnp.int32),
            pltpu.SMEM(valid_counts.shape, jnp.int32),
            pltpu.SMEM(tile_owner.shape, jnp.int32),
            wscr,
            pltpu.SemaphoreType.DMA((3,)),
        ],
        footprint_pairing.T, valid_counts, tile_owner, strided_weights, dilated_weights,
        *pre, *act, *phases, *send,
        flops=10**10,
    )
    slope, act, phases = both[0:2], both[2:4], both[4:6]
    shift_scr = ((9 * channels, cells), BF16)
    sums = [((9 * channels, 128), F32), ((9 * channels, 4 * channels), F32)]
    picked, *first = call(
        backward_first_kernel,
        [(payload, BF16), (grid, BF16), ((channels, 128), F32)] + sums,
        "v" * 8,
        [shift_scr],
        far[0], near, select, cots, w_act, act[0], slope[0], phases[0],
        flops=10**9,
    )
    half_shift = ((9 * channels // 2, cells), BF16)
    grads_shape = ((4, BLOCKS * 8, 128), BF16) if chunked else ((BLOCKS - 1, channels // 2, 128), F32)
    last, bias, give, out_shifts = call(
        functools.partial(backward_second_kernel, chunked=chunked),
        [(grid, BF16), ((8, 128), F32), grads_shape, shift_scr],
        "v" * 11,
        [half_shift],
        far[1], picked, select, cots, w_act, act[1], slope[1], phases[1], *first[1:],
        flops=10**9,
    )
    if chunked:
        got = scene_xor(give, 1)
    keep, *pre_b = call(
        functools.partial(backward_kept_kernel, chunked=chunked),
        [grads_shape] + [(grid, BF16)] * 2,
        "v" * 8,
        [half_shift],
        select, out_shifts, last, first[0], act[1], phases[1], *first[2:],
        flops=10**9,
    )
    wide_scr = ((9 * channels, cells), BF16)
    if chunked:
        stage = ((2 * BLOCKS * 8, 128), BF16)
        own, by_y, by_z, by_zy = call(spread_kernel, [stage] * 4, "vvvv", [], place, bias, keep, got)
        by_zy, by_z, by_y = scene_xor(by_zy, 6), scene_xor(by_z, 4), scene_xor(by_y, 2)
    (feature_grads,) = call(
        feature_kernel, [(features.shape, BF16)], "vvv", [wide_scr], *pre_b, w_feature, flops=10**9
    )
    chunk = (BLOCKS * 8, 128)
    if chunked:
        feature_grads, own = lax.optimization_barrier((feature_grads, own))
        kept, stay, cross = call(
            join_kernel, [(chunk, F32), (chunk, BF16), (chunk, BF16)], "vvvv", [], own, by_zy, by_z, by_y
        )
        by_zx, by_z, by_x = device_xor(cross, 8, 1), device_xor(cross, 8, 0), device_xor(stay, 0, 1)
    (feature_grads,) = call(
        store_kernel,
        [(features.shape, BF16)],
        "v",
        [pltpu.SemaphoreType.DMA],
        feature_grads,
        flops=10**9,
        out_spaces="h",
    )
    if not chunked:
        grad_weights, grad_bias = reduce_anywhere(
            join_halves(give, keep), bias[0], tile_owner, bias_rows, weight_scale, bias_scale
        )
        return (feature_grads[None], grad_weights, grad_bias)
    feature_grads, kept = lax.optimization_barrier((feature_grads, kept))
    grad_weights, grad_bias = call(
        functools.partial(finish_kernel, weight_scale=weight_scale, bias_scale=bias_scale),
        [((8, 25 * channels), F32), ((1, channels), F32)],
        "vvvv",
        [
            ((8, 25 * channels), F32),
            ((1, channels), F32),
            ((128, 128), F32),
            ((128, 128), F32),
            ((9 * channels, 128), F32),
            pltpu.SemaphoreType.DMA((3,)),
        ],
        kept, by_zx, by_z, by_x,
        out_spaces="hh",
    )
    return (feature_grads[None], grad_weights, grad_bias)


def solution(mesh):
    return jax.shard_map(
        local,
        mesh=mesh,
        in_specs=(
            P("scene", "tile", None, None),
            P(),
            P(),
            P(),
            P("scene", "tile", None),
            P(),
            P(),
            P(),
        ),
        out_specs=(P("scene", "tile", None, None), P("scene", None), P(("scene", "tile"), None)),
        check_vma=False,
    )
```

```python
import functools
import math

import jax
import jax.numpy as jnp
from jax import lax
from jax.experimental import pallas as pl
from jax.experimental.pallas import tpu as pltpu
from jax.sharding import PartitionSpec as P

CH = 64
ROW_TAPS = 4
DIL_TAPS = 9
BLOCKS = 14
SHIFTS = [(dr, dc) for dr in (-1, 0, 1) for dc in (-1, 0, 1)]
F32 = jnp.float32
BF16 = jnp.bfloat16
VMEM_LIMIT = 24 * 1024 * 1024


def shift_index(dr, dc):
    return (dr + 1) * 3 + dc + 1


def dot(a, b):
    return lax.dot_general(a, b, (((1,), (0,)), ((), ())), preferred_element_type=F32)


def dot_nt(a, b):
    return lax.dot_general(a, b, (((1,), (1,)), ((), ())), preferred_element_type=F32)


def shifted_masks(side, reach):
    cell = lax.broadcasted_iota(jnp.int32, (1, side * side), 1)
    row, col = cell // side, cell % side
    masks = {}
    for dr, dc in SHIFTS:
        ok = (
            (row + dr * reach >= 0)
            & (row + dr * reach < side)
            & (col + dc * reach >= 0)
            & (col + dc * reach < side)
        )
        masks[dr, dc] = ok.astype(F32).astype(BF16)
    return masks


def shifted(x, dr, dc, side, reach, masks):
    if dr == 0 and dc == 0:
        return x
    cells = side * side
    return pltpu.roll(x, (-(dr * side + dc) * reach) % cells, 1) * masks[dr, dc].astype(x.dtype)


def merge_matrix(side):
    size = 16 * side
    dims = (size, size)
    source = lax.broadcasted_iota(jnp.int32, dims, 1)
    target = lax.broadcasted_iota(jnp.int32, dims, 0)
    phase, cell = target // (4 * side), target % (4 * side)
    row, col = cell // side, cell % side
    wanted = (2 * row + phase // 2) * (2 * side) + 2 * col + phase % 2
    return jnp.where(source == wanted, 1.0, 0.0).astype(BF16)


def halves(values, core):
    even = jnp.concatenate([values[16 * m : 16 * m + 8] for m in range(CH // 16)], axis=0)
    odd = jnp.concatenate([values[16 * m + 8 : 16 * m + 16] for m in range(CH // 16)], axis=0)
    return jnp.where(core == 0, odd, even), jnp.where(core == 0, even, odd)


def half_run_matrix(side, odd):
    dims = (8 * side, 8 * side)
    source, target = (lax.broadcasted_iota(jnp.int32, dims, k) for k in range(2))
    phase, cell = target // (2 * side) ^ odd, target % (2 * side)
    row, col = cell // side, cell % side
    wanted = (2 * row + phase // 2) * (2 * side) + 2 * col + phase % 2
    return jnp.where(source == wanted, 1.0, 0.0).astype(BF16)


TAP_LINES = {0: (1, -1), 1: (0, 0), 2: (1, 0), 3: (0, 1)}
ROW_ORDER = (1, 3, 2, 0)


def tap_matrices(weight, taps, scratch):
    scratch[0 : CH * taps, 0:CH] = weight.astype(F32).T
    return [scratch[pl.ds(tap, CH, stride=taps), 0:CH] for tap in range(taps)]


def forward_patch(x_ref, cot, w_strided, w_dilated, bias_col, ph_ref, pre_ref, act_ref, send_ref, im_scr):
    side = math.isqrt(x_ref.shape[1]) // 2
    run, lanes = 16 * side, side * side // 128
    near, far = shifted_masks(side, 1), shifted_masks(side, 2)
    runs, wide = x_ref.shape[1] // run, 4 * side
    even, odd = (
        dot(
            jnp.concatenate(
                [x_ref[:, q * run + h * run // 2 : q * run + (h + 1) * run // 2] for q in range(runs)], axis=0
            ),
            half_run_matrix(side, h),
        )
        for h in range(2)
    )
    lower = lax.broadcasted_iota(jnp.int32, (runs * CH, wide), 1) < wide // 2
    for pr in range(2):
        one, two = even[:, pr * wide : (pr + 1) * wide], odd[:, pr * wide : (pr + 1) * wide]
        first = jnp.where(lower, one, two).astype(BF16)
        second = pltpu.roll(jnp.where(lower, two, one).astype(BF16), wide // 2, 1)
        for pc, lines in ((0, first), (1, second)):
            for q in range(runs):
                at = (pr * 2 + pc) * CH
                ph_ref[at : at + CH, q * wide : (q + 1) * wide] = lines[q * CH : (q + 1) * CH]
    sums = []
    for pr in range(2):
        for ct in range(4):
            pc, dc = TAP_LINES[ct]
            at, phase = (pr * 4 + ct) * CH, pr * 2 + pc
            im_scr[at : at + CH, :] = shifted(ph_ref[phase * CH : (phase + 1) * CH, :], 0, dc, side, 1, near)
        both = dot(w_strided[pr * 2 * CH : (pr + 1) * 2 * CH], im_scr[pr * 4 * CH : (pr + 1) * 4 * CH, :])
        dr = TAP_LINES[ROW_ORDER[2 * pr + 1]][1]
        sums.append(both[:CH] + shifted(both[CH:], dr, 0, side, 1, near))
    pre = sums[0] + sums[1] + bias_col
    pre_ref[...] = pre
    act = (pre * (1.0 / (1.0 + jnp.exp(-pre)))).astype(BF16)
    act_ref[...] = act
    for k in range(3):
        im_scr[k * CH : (k + 1) * CH, :] = shifted(act, 0, k - 1, side, 2, far)
    rows = dot(w_dilated, im_scr[0 : 3 * CH, :])
    out = rows[CH : 2 * CH]
    for k in (0, 2):
        out = out + shifted(rows[k * CH : (k + 1) * CH], k - 1, 0, side, 2, far)
    out = out.astype(BF16)
    for lane in range(lanes):
        send_ref[lane * CH : (lane + 1) * CH, :] = out[:, lane * 128 : (lane + 1) * 128]
    rows = [cot[:, lane * 128 : (lane + 1) * 128] for lane in range(lanes)]
    rows.append(jnp.zeros((16 - lanes, 128), F32))
    send_ref[lanes * CH :, :] = jnp.concatenate(rows, axis=0).astype(BF16)


def first_kernel(
    owner_hbm, x_hbm, ws_hbm, wd_hbm, bias_hbm, cot_hbm,
    ph_ref, pre_ref, act_ref, send_ref, strided_ref, dilated_ref, bias_ref, cot_ref,
    x_ref, ws_ref, wd_ref, table_ref, owner_ref, wscr, im_scr, sems,
):
    scene = lax.axis_index("scene")
    branch = scene % 2
    copies = [
        pltpu.make_async_copy(source, target, sems.at[i])
        for i, (source, target) in enumerate(
            [
                (x_hbm.at[0], x_ref),
                (ws_hbm.at[branch], ws_ref),
                (wd_hbm.at[branch], wd_ref),
                (owner_hbm, owner_ref),
                (bias_hbm, table_ref),
                (cot_hbm, cot_ref),
            ]
        )
    ]
    for copy in copies:
        copy.start()
    for copy in copies:
        copy.wait()
    mats = tap_matrices(ws_ref[...], 16, wscr)
    for k, rt in enumerate(ROW_ORDER):
        line = jnp.concatenate(mats[rt * 4 : rt * 4 + 4], axis=0)
        strided_ref[k * CH : (k + 1) * CH, :] = line.T.astype(BF16)
    mats = tap_matrices(wd_ref[...], 9, wscr)
    for k in range(3):
        line = jnp.concatenate(mats[3 * k : 3 * k + 3], axis=0)
        dilated_ref[k * CH : (k + 1) * CH, :] = line.T.astype(BF16)
    bias_row = table_ref[pl.ds(owner_ref[scene], 1), :]
    bias_ref[...] = jnp.broadcast_to(jnp.broadcast_to(bias_row, (8, CH)).T[:, 0:1], (CH, 128))
    forward_patch(
        x_ref, cot_ref[...].astype(F32)[0:1, :], strided_ref[...], dilated_ref[...], bias_ref[:, 0:1],
        ph_ref, pre_ref, act_ref, send_ref, im_scr,
    )


def later_kernel(
    x_ref, cot_ref, w_strided_ref, w_dilated_ref, bias_ref, sent_ref,
    ph_ref, pre_ref, act_ref, send_ref, both_ref, im_scr,
):
    forward_patch(
        x_ref.at[1], cot_ref[...].astype(F32)[1:2, :], w_strided_ref[...], w_dilated_ref[...],
        bias_ref[:, 0:1], ph_ref, pre_ref, act_ref, send_ref, im_scr,
    )
    both_ref[0] = sent_ref[...]
    both_ref[1] = send_ref[...]


def prepare_kernel(
    pairing_hbm, valid_hbm, owner_hbm, ws_ref, wd_ref, *refs, bias_rows
):
    pre_refs, act_refs, ph_refs, send_refs = (refs[2 * k : 2 * k + 2] for k in range(4))
    (
        slope_first, slope_second, act_first, act_second, ph_first, ph_second,
        wf_ref, wt_ref, select_ref, place_ref, cot_ref,
        pairing_ref, valid_ref, owner_ref, wscr, sems,
    ) = refs[8:]
    copies = [
        pltpu.make_async_copy(source, target, sems.at[i])
        for i, (source, target) in enumerate(
            [(pairing_hbm, pairing_ref), (valid_hbm, valid_ref), (owner_hbm, owner_ref)]
        )
    ]
    for copy in copies:
        copy.start()
    scene, tile = lax.axis_index("scene"), lax.axis_index("tile")
    branch, pair = scene % 2, scene // 2
    mats = tap_matrices(ws_ref[branch], 16, wscr)
    blocks = {}
    for rt in range(4):
        for ct in range(4):
            (pr, dr), (pc, dc) = TAP_LINES[rt], TAP_LINES[ct]
            blocks[pr * 2 + pc, shift_index(-dr, -dc)] = mats[rt * 4 + ct]
    zero = jnp.zeros((CH, CH), F32)
    for phase in range(4):
        row = [blocks.get((phase, s), zero) for s in range(9)]
        wf_ref[phase * CH : (phase + 1) * CH, :] = jnp.concatenate(row, axis=1).astype(BF16)
    give, keep = halves(wd_ref[branch].astype(F32), branch)
    mats = tap_matrices(jnp.concatenate([give, keep], axis=0), 9, wscr)[::-1]
    half = CH // 2
    wt_ref[...] = jnp.concatenate(
        [mat[:, h * half : (h + 1) * half] for h in range(2) for mat in mats], axis=1
    ).astype(BF16)
    slopes = []
    for pre_ref in pre_refs:
        pre = pre_ref[...]
        gate = 1.0 / (1.0 + jnp.exp(-pre))
        slopes.append(gate * (1.0 + pre * (1.0 - gate)))
    for copy in copies:
        copy.wait()
    total = pairing_ref.shape[0]
    matches = []
    for p in range(2):
        position = tile * 2 + p
        matched, inverse = pairing_ref[position, pair], jnp.int32(0)
        for i in range(total):
            inverse = inverse + jnp.where(pairing_ref[i, pair] == position, i, 0)
        matched = jnp.where(branch == 0, matched, inverse)
        matches.append(jnp.where(matched // 2 == tile, 0, 2) + matched % 2)
    swapped = matches[0] == 3
    slope_first[...] = jnp.where(swapped, slopes[1], slopes[0])
    slope_second[...] = jnp.where(swapped, slopes[0], slopes[1])
    for first, second, pairs in ((act_first, act_second, act_refs), (ph_first, ph_second, ph_refs)):
        first[...] = jnp.where(swapped, pairs[1][...], pairs[0][...])
        second[...] = jnp.where(swapped, pairs[0][...], pairs[1][...])
    rows = send_refs[0].shape[0] - 16
    cots = [ref[rows:, :].astype(F32) for ref in send_refs]
    cot_ref[0:16, :] = jnp.where(swapped, cots[1], cots[0])
    cot_ref[16:32, :] = jnp.where(swapped, cots[0], cots[1])
    row = lax.broadcasted_iota(jnp.int32, select_ref.shape, 0)
    select = jnp.zeros(select_ref.shape, F32)
    for p in range(2):
        position = jnp.where(swapped, 1 - p, p)
        live = jnp.where(tile * 2 + p < valid_ref[pair], 8 + position, -1)
        select = jnp.where((row == position * 4 + matches[p]) | (row == live), 1.0, select)
    select_ref[...] = jnp.where(row == jnp.where(swapped, 10, -1), 1.0, select)
    row = lax.broadcasted_iota(jnp.int32, place_ref.shape, 0)
    here = scene // 2 % 4
    place = jnp.zeros(place_ref.shape, F32)
    for k, source in enumerate((scene, scene ^ 1)):
        owner = owner_ref[source]
        target = owner // (2 * bias_rows)
        half = jnp.where(target // 8 == branch, 0, 1)
        wanted = k * 64 + ((target // 2 % 4) ^ here) * 16 + half * 8 + owner % (2 * bias_rows)
        place = jnp.where(row == jnp.where(target % 2 == branch, wanted, -1), 1.0, place)
    place_ref[...] = place


HALF = 9 * CH // 2


def shift_rows(pieces, reach, side, target):
    masks = shifted_masks(side, reach)
    rows = CH // 2
    for h, piece in enumerate(pieces):
        for s, (dr, dc) in enumerate(SHIFTS):
            at = h * HALF + s * rows
            target[at : at + rows, :] = shifted(piece, dr, dc, side, reach, masks)


def pick(position, candidates, select_ref, first=0):
    partner = None
    for k, payload in enumerate(candidates, first):
        term = payload * select_ref[position * 4 + k : position * 4 + k + 1, :].astype(BF16)
        partner = term if partner is None else partner + term
    return partner


def backward_patch(position, partner, select_ref, cot_ref, wt_ref, slope_ref, shift_scr):
    side = math.isqrt(slope_ref.shape[1])
    lanes = side * side // 128
    core = lax.axis_index("scene") % 2
    live = select_ref[8 + position : 9 + position, :]
    signal = (cot_ref[position * 16 : position * 16 + 16, :] + partner[lanes * CH :, :].astype(F32)) * live
    out_grad = jnp.concatenate(
        [signal[j : j + 1, :] * partner[j * CH : (j + 1) * CH, :].astype(F32) for j in range(lanes)], axis=1
    )
    shift_rows([piece.astype(BF16) for piece in halves(out_grad, core)], 2, side, shift_scr)
    return dot(wt_ref[...], shift_scr[...]) * slope_ref[...]


def backward_first_kernel(
    far0_ref, near_ref, select_ref, cot_ref, wt_ref, act_ref, slope_ref, ph_ref,
    pick_ref, pre_b_ref, bias_ref, dilated_ref, strided_ref, shift_scr,
):
    side = math.isqrt(slope_ref.shape[1])
    core = lax.axis_index("scene") % 2
    candidates = (near_ref[0], near_ref[1], far0_ref[...])
    pick_ref[...] = pick(1, candidates, select_ref)
    pre_grad = backward_patch(0, pick(0, candidates, select_ref), select_ref, cot_ref, wt_ref, slope_ref, shift_scr)
    act = act_ref[...]
    dilated_ref[...] = dot_nt(shift_scr[...], jnp.concatenate([act, act], axis=0))
    bias_ref[...] = jnp.broadcast_to(jnp.sum(pre_grad, axis=1, keepdims=True), bias_ref.shape)
    pre_b_ref[...] = pre_grad.astype(BF16)
    shift_rows([piece.astype(BF16) for piece in halves(pre_grad, core)], 1, side, shift_scr)
    strided_ref[...] = dot_nt(shift_scr[...], ph_ref[...])


def tap_blocks(strided, dilated):
    rows = CH // 2
    lower = lax.broadcasted_iota(jnp.int32, (rows, 2 * CH), 1) < CH

    def strided_piece(pr, shift):
        return strided[shift * rows : (shift + 1) * rows, pr * 2 * CH : (pr + 1) * 2 * CH]

    blocks = []
    for rt in range(4):
        pr, dr = TAP_LINES[rt]
        blocks.append(strided_piece(pr, shift_index(-dr, 0)))
        blocks.append(
            jnp.where(lower, strided_piece(pr, shift_index(-dr, -1)), strided_piece(pr, shift_index(-dr, 1)))
        )
    for j in range(5):
        low = dilated[(8 - 2 * j) * rows : (9 - 2 * j) * rows, :]
        high = dilated[(7 - 2 * j) * rows : (8 - 2 * j) * rows, :] if j < 4 else jnp.zeros_like(low)
        blocks.append(jnp.where(lower, low, high))
    return blocks


def write_blocks(blocks, bias_wide, ref, chunked):
    if not chunked:
        for i, block in enumerate(blocks):
            ref[i] = block
        return
    here = lax.axis_index("scene") // 2 % 4
    for m in range(4):
        pieces = [block[8 * m : 8 * m + 8] for block in blocks] + [bias_wide]
        ref[here ^ m] = jnp.concatenate(pieces, axis=0).astype(BF16)


def backward_second_kernel(
    far1_ref, pick_ref, select_ref, cot_ref, wt_ref, act_ref, slope_ref, ph_ref,
    other_bias_ref, other_dilated_ref, other_strided_ref,
    pre_b_ref, bias_ref, give_ref, out_shifts_ref, shift_scr, *, chunked,
):
    side = math.isqrt(slope_ref.shape[1])
    core = lax.axis_index("scene") % 2
    partner = pick_ref[...] + pick(1, (far1_ref[...],), select_ref, 3)
    pre_grad = backward_patch(1, partner, select_ref, cot_ref, wt_ref, slope_ref, out_shifts_ref)
    act = act_ref[...]
    dilated = dot_nt(out_shifts_ref[0:HALF, :], jnp.concatenate([act, act], axis=0))
    give, _ = halves(pre_grad, core)
    shift_rows([give.astype(BF16)], 1, side, shift_scr)
    strided = dot_nt(shift_scr[...], ph_ref[...])
    pre_b_ref[...] = pre_grad.astype(BF16)
    bias_wide = (jnp.sum(pre_grad, axis=1, keepdims=True) + other_bias_ref[...]).T[0:8, :]
    bias_wide = jnp.concatenate([bias_wide, jnp.zeros_like(bias_wide)], axis=1)
    bias_ref[...] = bias_wide
    blocks = tap_blocks(strided + other_strided_ref[0:HALF, :], dilated + other_dilated_ref[0:HALF, :])
    write_blocks(blocks, bias_wide, give_ref, chunked)


def backward_kept_kernel(
    select_ref, out_shifts_ref, pre_b_ref, other_ref, act_ref, ph_ref, other_dilated_ref, other_strided_ref,
    keep_ref, pre_b0_ref, pre_b1_ref, shift_scr, *, chunked,
):
    side = math.isqrt(act_ref.shape[1])
    act = act_ref[...]
    dilated = dot_nt(out_shifts_ref[HALF:, :], jnp.concatenate([act, act], axis=0))
    pre_b, other = pre_b_ref[...], other_ref[...]
    _, keep = halves(pre_b.astype(F32), lax.axis_index("scene") % 2)
    shift_rows([keep.astype(BF16)], 1, side, shift_scr)
    strided = dot_nt(shift_scr[...], ph_ref[...])
    blocks = tap_blocks(strided + other_strided_ref[HALF:, :], dilated + other_dilated_ref[HALF:, :])
    write_blocks(blocks, jnp.zeros((8, 2 * CH), F32), keep_ref, chunked)
    swapped = select_ref[10:11, 0:1].astype(BF16)
    straight = 1.0 - swapped
    pre_b0_ref[...] = other * straight + pre_b * swapped
    pre_b1_ref[...] = other * swapped + pre_b * straight


def spread_kernel(place_ref, bias_ref, keep_ref, got_ref, *out_refs):
    rows = keep_ref.shape[1]
    top = lax.broadcasted_iota(jnp.int32, (16, 128), 0) < 8
    mine = bias_ref[0:1, :]
    theirs = got_ref[0, rows - 16 :, :].astype(F32)[8:9, :]
    for d, out_ref in enumerate(out_refs):
        for half, ref in enumerate((keep_ref, got_ref)):
            at = d * 16 + half * 8
            bias = place_ref[at : at + 8, :] * mine + place_ref[64 + at : 72 + at, :] * theirs
            last = ref[d, rows - 16 :, :].astype(F32)
            last = jnp.where(top, last, jnp.concatenate([bias, bias], axis=0))
            out_ref[half * rows : (half + 1) * rows - 16, :] = ref[d, : rows - 16, :]
            out_ref[(half + 1) * rows - 16 : (half + 1) * rows, :] = last.astype(BF16)


def join_kernel(own_ref, a_ref, b_ref, c_ref, keep_ref, stay_ref, cross_ref):
    scene = lax.axis_index("scene")
    rows = keep_ref.shape[0]
    total = (own_ref[...].astype(F32) + a_ref[...].astype(F32)) + (
        b_ref[...].astype(F32) + c_ref[...].astype(F32)
    )
    mine, theirs = total[:rows, :], total[rows:, :]
    first = scene // 8 == scene % 2
    kept = jnp.where(first, mine, theirs)
    keep_ref[...] = kept
    stay_ref[...] = kept.astype(BF16)
    cross_ref[...] = jnp.where(first, theirs, mine).astype(BF16)


def finish_kernel(
    own_ref, a_ref, b_ref, c_ref, weights_hbm, bias_hbm,
    weights_ref, bias_ref, tap_scr, turn_scr, dilated_scr, sems, *, weight_scale, bias_scale,
):
    tile = lax.axis_index("tile")
    total = (own_ref[...] + a_ref[...].astype(F32)) + (b_ref[...].astype(F32) + c_ref[...].astype(F32))
    bias = total[(BLOCKS - 1) * 8 :, :] * bias_scale
    index = lax.broadcasted_iota(jnp.int32, bias.shape, 0)
    bias_ref[...] = jnp.sum(jnp.where(index == tile, bias, 0.0), axis=0, keepdims=True)[:, 0:CH]
    bias_out = pltpu.make_async_copy(bias_ref, bias_hbm, sems.at[0])
    bias_out.start()
    total = total * weight_scale
    other = pltpu.roll(total, CH, 1)
    for block in range(8):
        for half, source in enumerate((total, other)):
            tap = block // 2 * 4 + ((1, 2), (3, 0))[block % 2][half]
            tap_scr[pl.ds(tap, 8, stride=16), :] = source[block * 8 : block * 8 + 8, :]
    lines = tap_scr[0:128, :].T[0:CH, :].reshape(8, 8, 128)
    sub = lax.broadcasted_iota(jnp.int32, lines.shape, 1)
    chunk = lax.broadcasted_iota(jnp.int32, lines.shape, 2) // 16
    for step in (1, 2, 4):
        up = pltpu.roll(pltpu.roll(lines, 8 - step, 1), 16 * step, 2)
        down = pltpu.roll(pltpu.roll(lines, step, 1), 128 - 16 * step, 2)
        high, wide = sub // step % 2, chunk // step % 2
        lines = jnp.where(high == wide, lines, jnp.where(high == 0, up, down))
    for block in range(8):
        weights_ref[:, block * 128 : (block + 1) * 128] = lines[block]
    strided_part, dilated_part = pl.ds(0, 16 * CH), pl.ds(16 * CH, DIL_TAPS * CH)
    strided_out = pltpu.make_async_copy(weights_ref.at[:, strided_part], weights_hbm.at[:, strided_part], sems.at[1])
    strided_out.start()
    turn_scr[0:40, :] = total[64:104, :]
    turned = turn_scr[...].T
    for tap in range(DIL_TAPS):
        half = tap % 2
        dilated_scr[pl.ds(tap, CH, stride=DIL_TAPS), :] = turned[half * CH : (half + 1) * CH, :]
    spread = dilated_scr[0 : DIL_TAPS * CH, :].T
    tap = lax.broadcasted_iota(jnp.int32, (8, DIL_TAPS * CH), 1) % DIL_TAPS
    result = spread[0:8, :]
    for j in range(1, 5):
        result = jnp.where(tap // 2 == j, spread[8 * j : 8 * j + 8, :], result)
    weights_ref[:, 16 * CH :] = result
    dilated_out = pltpu.make_async_copy(weights_ref.at[:, dilated_part], weights_hbm.at[:, dilated_part], sems.at[2])
    dilated_out.start()
    for copy in (bias_out, strided_out, dilated_out):
        copy.wait()


def feature_patch(pre_b_ref, wf_ref, out_ref, shift_scr):
    side = math.isqrt(pre_b_ref.shape[1])
    near = shifted_masks(side, 1)
    merge = merge_matrix(side)
    run, wide = 16 * side, 4 * side
    pre_b = pre_b_ref[...]
    for s, (dr, dc) in enumerate(SHIFTS):
        shift_scr[s * CH : (s + 1) * CH, :] = shifted(pre_b, dr, dc, side, 1, near)
    phases = dot(wf_ref[...], shift_scr[...]).astype(BF16)
    runs = out_ref.shape[1] // run
    stacked = jnp.concatenate(
        [
            jnp.concatenate(
                [phases[k * CH : (k + 1) * CH, q * wide : (q + 1) * wide] for k in range(4)], axis=1
            )
            for q in range(runs)
        ],
        axis=0,
    )
    merged = dot(stacked, merge).astype(BF16)
    for q in range(runs):
        out_ref[:, q * run : (q + 1) * run] = merged[q * CH : (q + 1) * CH, :]


def feature_kernel(pre_b0_ref, pre_b1_ref, wf_ref, out_ref, shift_scr):
    for p, pre_b_ref in enumerate((pre_b0_ref, pre_b1_ref)):
        feature_patch(pre_b_ref, wf_ref, out_ref.at[p], shift_scr)


def store_kernel(features_ref, out_hbm, sem):
    copy = pltpu.make_async_copy(features_ref, out_hbm, sem)
    copy.start()
    copy.wait()


SPACES = {"s": pltpu.SMEM, "v": pltpu.VMEM, "h": pltpu.HBM, "a": pl.ANY}


def call(kernel, outs, ins, scratch, *args, flops=0, out_spaces="", aliases=None):
    args = [
        pltpu.with_memory_space_constraint(arg, pltpu.HBM) if space == "h" else arg
        for space, arg in zip(ins, args)
    ]
    return pl.pallas_call(
        kernel,
        out_shape=[jax.ShapeDtypeStruct(shape, kind) for shape, kind in outs],
        in_specs=[pl.BlockSpec(memory_space=SPACES[space]) for space in ins],
        out_specs=[pl.BlockSpec(memory_space=SPACES[space]) for space in out_spaces or "v" * len(outs)],
        scratch_shapes=[pltpu.VMEM(*item) if isinstance(item, tuple) else item for item in scratch],
        input_output_aliases=aliases or {},
        compiler_params=pltpu.CompilerParams(vmem_limit_bytes=VMEM_LIMIT),
        cost_estimate=pl.CostEstimate(flops=flops, bytes_accessed=1 << 20, transcendentals=0),
    )(*args)


def device_pairs(x, pairs):
    tiles = lax.axis_size("tile")
    flat = [(source[0] * tiles + source[1], target[0] * tiles + target[1]) for source, target in pairs]
    return lax.ppermute(x, ("scene", "tile"), flat)


def scene_xor(x, distance):
    return lax.ppermute(x, "scene", [(i, i ^ distance) for i in range(lax.axis_size("scene"))])


def device_xor(x, scene_distance, tile_distance):
    scenes, tiles = range(lax.axis_size("scene")), range(lax.axis_size("tile"))
    return device_pairs(
        x, [((s, t), (s ^ scene_distance, t ^ tile_distance)) for s in scenes for t in tiles]
    )


def join_halves(give, keep):
    parts = [half.reshape(BLOCKS - 1, -1, 8, half.shape[-1]) for half in (give, keep)]
    first = lax.axis_index("scene") % 2 == 0
    pair = jnp.stack([jnp.where(first, parts[1], parts[0]), jnp.where(first, parts[0], parts[1])], axis=2)
    return pair.reshape(BLOCKS - 1, -1, pair.shape[-1])


def reduce_anywhere(blocks, bias_row, tile_owner, bias_rows, weight_scale, bias_scale):
    channels = blocks.shape[1]
    scene = lax.axis_index("scene")
    scenes, tiles = lax.axis_size("scene"), lax.axis_size("tile")
    halves = blocks.reshape(BLOCKS - 1, channels, 2, channels)
    strided, dilated = [None] * 16, []
    for block in range(8):
        for half in range(2):
            strided[block // 2 * 4 + ((1, 2), (3, 0))[block % 2][half]] = halves[block, :, half]
    for tap in range(DIL_TAPS):
        dilated.append(halves[8 + tap // 2, :, tap % 2])
    row = jnp.concatenate(
        [
            jnp.stack(strided, axis=-1).reshape(channels, 16 * channels),
            jnp.stack(dilated, axis=-1).reshape(channels, DIL_TAPS * channels),
        ],
        axis=1,
    )
    hit = jnp.arange(2, dtype=jnp.int32)[:, None, None] == scene % 2
    term = jnp.where(hit, row[None] * weight_scale, 0.0).reshape(2 * channels, 25 * channels)
    weights = lax.psum(lax.psum_scatter(term, "scene", scatter_dimension=0, tiled=True), "tile")
    tile_id = lax.dynamic_index_in_dim(tile_owner, scene, 0, keepdims=False)
    owned = jnp.arange(scenes * tiles * bias_rows, dtype=jnp.int32) == tile_id
    bias = jnp.where(owned[:, None], bias_row[None, :channels] * bias_scale, 0.0)
    return weights, lax.psum_scatter(bias, ("scene", "tile"), scatter_dimension=0, tiled=True)


def local(
    features_in,
    strided_weights,
    dilated_weights,
    tile_bias,
    cost_cotangent,
    footprint_pairing,
    valid_counts,
    tile_owner,
):
    features, own_cot = features_in[0], cost_cotangent[0]
    patches, channels, cells_in = features.shape
    cells = own_cot.shape[1]
    scenes, tiles = lax.axis_size("scene"), lax.axis_size("tile")
    weight_scale = 1.0 / math.sqrt(scenes * patches * tiles * cells)
    bias_scale = 1.0 / math.sqrt(patches * tiles * cells)
    bias_rows = tile_bias.shape[0] // (scenes * tiles)
    grid = (channels, cells)
    payload = (cells * channels // 128 + 16, 128)
    chunked = scenes == 16 and tiles == 2 and patches == 2 and bias_rows == 1
    wscr = ((16 * channels + 16, 2 * channels), F32)
    im_scr = ((8 * channels, cells), BF16)
    patch_outs = [((4 * channels, cells), BF16), (grid, F32), (grid, BF16), (payload, BF16)]
    first_outs = patch_outs + [
        ((4 * channels, 4 * channels), BF16),
        ((3 * channels, 3 * channels), BF16),
        ((channels, 128), F32),
        (own_cot.shape, BF16),
    ]
    *part, w_strided, w_dilated, bias_col, cot = call(
        first_kernel,
        first_outs,
        "hhhhhh",
        [
            ((channels, cells_in), BF16),
            (strided_weights.shape[1:], BF16),
            (dilated_weights.shape[1:], BF16),
            (tile_bias.shape, F32),
            pltpu.SMEM(tile_owner.shape, jnp.int32),
            wscr,
            im_scr,
            pltpu.SemaphoreType.DMA((6,)),
        ],
        tile_owner, features, strided_weights, dilated_weights, tile_bias, own_cot,
        flops=10**9,
    )
    far = [device_xor(part[3], 1, 1)]
    *late, both = call(
        later_kernel,
        patch_outs + [((2,) + payload, BF16)],
        "vvvvvv",
        [im_scr],
        features, cot, w_strided, w_dilated, bias_col, part[3],
        flops=10**10,
    )
    far.append(device_xor(late[3], 1, 1))
    near = scene_xor(both, 1)
    phases, pre, act, send = zip(part, late)
    ordered = [(grid, F32)] * 2 + [(grid, BF16)] * 2 + [((4 * channels, cells), BF16)] * 2
    *both, w_feature, w_act, select, place, cots = call(
        functools.partial(prepare_kernel, bias_rows=bias_rows),
        ordered
        + [
            ((4 * channels, 9 * channels), BF16),
            ((channels, 9 * channels), BF16),
            ((16, 128), F32),
            ((128, 128), F32),
            ((32, 128), F32),
        ],
        "hhhvvvvvvvvvv",
        [
            pltpu.SMEM(footprint_pairing.shape[::-1], jnp.int32),
            pltpu.SMEM(valid_counts.shape, jnp.int32),
            pltpu.SMEM(tile_owner.shape, jnp.int32),
            wscr,
            pltpu.SemaphoreType.DMA((3,)),
        ],
        footprint_pairing.T, valid_counts, tile_owner, strided_weights, dilated_weights,
        *pre, *act, *phases, *send,
        flops=10**10,
    )
    slope, act, phases = both[0:2], both[2:4], both[4:6]
    shift_scr = ((9 * channels, cells), BF16)
    sums = [((9 * channels, 128), F32), ((9 * channels, 4 * channels), F32)]
    picked, *first = call(
        backward_first_kernel,
        [(payload, BF16), (grid, BF16), ((channels, 128), F32)] + sums,
        "v" * 8,
        [shift_scr],
        far[0], near, select, cots, w_act, act[0], slope[0], phases[0],
        flops=10**9,
    )
    half_shift = ((9 * channels // 2, cells), BF16)
    grads_shape = ((4, BLOCKS * 8, 128), BF16) if chunked else ((BLOCKS - 1, channels // 2, 128), F32)
    last, bias, give, out_shifts = call(
        functools.partial(backward_second_kernel, chunked=chunked),
        [(grid, BF16), ((8, 128), F32), grads_shape, shift_scr],
        "v" * 11,
        [half_shift],
        far[1], picked, select, cots, w_act, act[1], slope[1], phases[1], *first[1:],
        flops=10**9,
    )
    if chunked:
        got = scene_xor(give, 1)
    keep, *pre_b = call(
        functools.partial(backward_kept_kernel, chunked=chunked),
        [grads_shape] + [(grid, BF16)] * 2,
        "v" * 8,
        [half_shift],
        select, out_shifts, last, first[0], act[1], phases[1], *first[2:],
        flops=10**9,
    )
    wide_scr = ((9 * channels, cells), BF16)
    if chunked:
        stage = ((2 * BLOCKS * 8, 128), BF16)
        own, by_y, by_z, by_zy = call(spread_kernel, [stage] * 4, "vvvv", [], place, bias, keep, got)
        by_zy, by_z, by_y = scene_xor(by_zy, 6), scene_xor(by_z, 4), scene_xor(by_y, 2)
    (feature_grads,) = call(
        feature_kernel, [(features.shape, BF16)], "vvv", [wide_scr], *pre_b, w_feature, flops=10**9
    )
    chunk = (BLOCKS * 8, 128)
    if chunked:
        feature_grads, own = lax.optimization_barrier((feature_grads, own))
        kept, stay, cross = call(
            join_kernel, [(chunk, F32), (chunk, BF16), (chunk, BF16)], "vvvv", [], own, by_zy, by_z, by_y
        )
        by_zx, by_z, by_x = device_xor(cross, 8, 1), device_xor(cross, 8, 0), device_xor(stay, 0, 1)
    (feature_grads,) = call(
        store_kernel,
        [(features.shape, BF16)],
        "v",
        [pltpu.SemaphoreType.DMA],
        feature_grads,
        flops=10**9,
        out_spaces="h",
    )
    if not chunked:
        grad_weights, grad_bias = reduce_anywhere(
            join_halves(give, keep), bias[0], tile_owner, bias_rows, weight_scale, bias_scale
        )
        return (feature_grads[None], grad_weights, grad_bias)
    feature_grads, kept = lax.optimization_barrier((feature_grads, kept))
    grad_weights, grad_bias = call(
        functools.partial(finish_kernel, weight_scale=weight_scale, bias_scale=bias_scale),
        [((8, 25 * channels), F32), ((1, channels), F32)],
        "vvvv",
        [
            ((8, 25 * channels), F32),
            ((1, channels), F32),
            ((144, 128), F32),
            ((128, 128), F32),
            ((9 * channels + 16, 128), F32),
            pltpu.SemaphoreType.DMA((3,)),
        ],
        kept, by_zx, by_z, by_x,
        out_spaces="hh",
    )
    return (feature_grads[None], grad_weights, grad_bias)


def solution(mesh):
    return jax.shard_map(
        local,
        mesh=mesh,
        in_specs=(
            P("scene", "tile", None, None),
            P(),
            P(),
            P(),
            P("scene", "tile", None),
            P(),
            P(),
            P(),
        ),
        out_specs=(P("scene", "tile", None, None), P("scene", None), P(("scene", "tile"), None)),
        check_vma=False,
    )
```

```python
import functools
import math

import jax
import jax.numpy as jnp
from jax import lax
from jax.experimental import pallas as pl
from jax.experimental.pallas import tpu as pltpu
from jax.sharding import PartitionSpec as P

CH = 64
ROW_TAPS = 4
DIL_TAPS = 9
BLOCKS = 14
SHIFTS = [(dr, dc) for dr in (-1, 0, 1) for dc in (-1, 0, 1)]
F32 = jnp.float32
BF16 = jnp.bfloat16
VMEM_LIMIT = 24 * 1024 * 1024


def shift_index(dr, dc):
    return (dr + 1) * 3 + dc + 1


def dot(a, b):
    return lax.dot_general(a, b, (((1,), (0,)), ((), ())), preferred_element_type=F32)


def dot_nt(a, b):
    return lax.dot_general(a, b, (((1,), (1,)), ((), ())), preferred_element_type=F32)


def shifted_masks(side, reach):
    cell = lax.broadcasted_iota(jnp.int32, (1, side * side), 1)
    row, col = cell // side, cell % side
    masks = {}
    for dr, dc in SHIFTS:
        ok = (
            (row + dr * reach >= 0)
            & (row + dr * reach < side)
            & (col + dc * reach >= 0)
            & (col + dc * reach < side)
        )
        masks[dr, dc] = ok.astype(F32).astype(BF16)
    return masks


def shifted(x, dr, dc, side, reach, masks):
    if dr == 0 and dc == 0:
        return x
    cells = side * side
    return pltpu.roll(x, (-(dr * side + dc) * reach) % cells, 1) * masks[dr, dc].astype(x.dtype)


def merge_matrix(side):
    size = 16 * side
    dims = (size, size)
    source = lax.broadcasted_iota(jnp.int32, dims, 1)
    target = lax.broadcasted_iota(jnp.int32, dims, 0)
    phase, cell = target // (4 * side), target % (4 * side)
    row, col = cell // side, cell % side
    wanted = (2 * row + phase // 2) * (2 * side) + 2 * col + phase % 2
    return jnp.where(source == wanted, 1.0, 0.0).astype(BF16)


def halves(values, core):
    even = jnp.concatenate([values[16 * m : 16 * m + 8] for m in range(CH // 16)], axis=0)
    odd = jnp.concatenate([values[16 * m + 8 : 16 * m + 16] for m in range(CH // 16)], axis=0)
    return jnp.where(core == 0, odd, even), jnp.where(core == 0, even, odd)


def half_run_matrix(side, odd):
    dims = (8 * side, 8 * side)
    source, target = (lax.broadcasted_iota(jnp.int32, dims, k) for k in range(2))
    phase, cell = target // (2 * side) ^ odd, target % (2 * side)
    row, col = cell // side, cell % side
    wanted = (2 * row + phase // 2) * (2 * side) + 2 * col + phase % 2
    return jnp.where(source == wanted, 1.0, 0.0).astype(BF16)


TAP_LINES = {0: (1, -1), 1: (0, 0), 2: (1, 0), 3: (0, 1)}
ROW_ORDER = (1, 3, 2, 0)


def tap_matrices(weight, taps, scratch):
    scratch[0 : CH * taps, 0:CH] = weight.astype(F32).T
    return [scratch[pl.ds(tap, CH, stride=taps), 0:CH] for tap in range(taps)]


def forward_patch(x_ref, cot, w_strided, w_dilated, bias_col, ph_ref, pre_ref, act_ref, send_ref, im_scr):
    side = math.isqrt(x_ref.shape[1]) // 2
    run, lanes = 16 * side, side * side // 128
    near, far = shifted_masks(side, 1), shifted_masks(side, 2)
    runs, wide = x_ref.shape[1] // run, 4 * side
    even, odd = (
        dot(
            jnp.concatenate(
                [x_ref[:, q * run + h * run // 2 : q * run + (h + 1) * run // 2] for q in range(runs)], axis=0
            ),
            half_run_matrix(side, h),
        )
        for h in range(2)
    )
    lower = lax.broadcasted_iota(jnp.int32, (runs * CH, wide), 1) < wide // 2
    for pr in range(2):
        one, two = even[:, pr * wide : (pr + 1) * wide], odd[:, pr * wide : (pr + 1) * wide]
        first = jnp.where(lower, one, two).astype(BF16)
        second = pltpu.roll(jnp.where(lower, two, one).astype(BF16), wide // 2, 1)
        for pc, lines in ((0, first), (1, second)):
            for q in range(runs):
                at = (pr * 2 + pc) * CH
                ph_ref[at : at + CH, q * wide : (q + 1) * wide] = lines[q * CH : (q + 1) * CH]
    sums = []
    for pr in range(2):
        for ct in range(4):
            pc, dc = TAP_LINES[ct]
            at, phase = (pr * 4 + ct) * CH, pr * 2 + pc
            im_scr[at : at + CH, :] = shifted(ph_ref[phase * CH : (phase + 1) * CH, :], 0, dc, side, 1, near)
        both = dot(w_strided[pr * 2 * CH : (pr + 1) * 2 * CH], im_scr[pr * 4 * CH : (pr + 1) * 4 * CH, :])
        dr = TAP_LINES[ROW_ORDER[2 * pr + 1]][1]
        sums.append(both[:CH] + shifted(both[CH:], dr, 0, side, 1, near))
    pre = sums[0] + sums[1] + bias_col
    pre_ref[...] = pre
    act = (pre * (1.0 / (1.0 + jnp.exp(-pre)))).astype(BF16)
    act_ref[...] = act
    for k in range(3):
        im_scr[k * CH : (k + 1) * CH, :] = shifted(act, 0, k - 1, side, 2, far)
    rows = dot(w_dilated, im_scr[0 : 3 * CH, :])
    out = rows[CH : 2 * CH]
    for k in (0, 2):
        out = out + shifted(rows[k * CH : (k + 1) * CH], k - 1, 0, side, 2, far)
    out = out.astype(BF16)
    for lane in range(lanes):
        send_ref[lane * CH : (lane + 1) * CH, :] = out[:, lane * 128 : (lane + 1) * 128]
    rows = [cot[:, lane * 128 : (lane + 1) * 128] for lane in range(lanes)]
    rows.append(jnp.zeros((16 - lanes, 128), F32))
    send_ref[lanes * CH :, :] = jnp.concatenate(rows, axis=0).astype(BF16)


def first_kernel(
    owner_hbm, x_hbm, ws_hbm, wd_hbm, bias_hbm, cot_hbm,
    ph_ref, pre_ref, act_ref, send_ref, strided_ref, dilated_ref, bias_ref, cot_ref, later_ref,
    x_ref, ws_ref, wd_ref, table_ref, owner_ref, wscr, im_scr, sems,
):
    scene = lax.axis_index("scene")
    branch = scene % 2
    copies = [
        pltpu.make_async_copy(source, target, sems.at[i])
        for i, (source, target) in enumerate(
            [
                (x_hbm.at[0], x_ref),
                (ws_hbm.at[branch], ws_ref),
                (wd_hbm.at[branch], wd_ref),
                (owner_hbm, owner_ref),
                (bias_hbm, table_ref),
                (cot_hbm, cot_ref),
            ]
        )
    ]
    for copy in copies:
        copy.start()
    for copy in copies:
        copy.wait()
    later = pltpu.make_async_copy(x_hbm.at[1], later_ref, sems.at[6])
    later.start()
    mats = tap_matrices(ws_ref[...], 16, wscr)
    for k, rt in enumerate(ROW_ORDER):
        line = jnp.concatenate(mats[rt * 4 : rt * 4 + 4], axis=0)
        strided_ref[k * CH : (k + 1) * CH, :] = line.T.astype(BF16)
    mats = tap_matrices(wd_ref[...], 9, wscr)
    for k in range(3):
        line = jnp.concatenate(mats[3 * k : 3 * k + 3], axis=0)
        dilated_ref[k * CH : (k + 1) * CH, :] = line.T.astype(BF16)
    bias_row = table_ref[pl.ds(owner_ref[scene], 1), :]
    bias_ref[...] = jnp.broadcast_to(jnp.broadcast_to(bias_row, (8, CH)).T[:, 0:1], (CH, 128))
    forward_patch(
        x_ref, cot_ref[...].astype(F32)[0:1, :], strided_ref[...], dilated_ref[...], bias_ref[:, 0:1],
        ph_ref, pre_ref, act_ref, send_ref, im_scr,
    )
    later.wait()


def later_kernel(
    x_ref, cot_ref, w_strided_ref, w_dilated_ref, bias_ref, sent_ref,
    ph_ref, pre_ref, act_ref, send_ref, both_ref, im_scr,
):
    forward_patch(
        x_ref, cot_ref[...].astype(F32)[1:2, :], w_strided_ref[...], w_dilated_ref[...],
        bias_ref[:, 0:1], ph_ref, pre_ref, act_ref, send_ref, im_scr,
    )
    both_ref[0] = sent_ref[...]
    both_ref[1] = send_ref[...]


def prepare_kernel(
    pairing_hbm, valid_hbm, owner_hbm, ws_ref, wd_ref, *refs, bias_rows
):
    pre_refs, act_refs, ph_refs, send_refs = (refs[2 * k : 2 * k + 2] for k in range(4))
    (
        slope_first, slope_second, act_first, act_second, ph_first, ph_second,
        wf_ref, wt_ref, select_ref, place_ref, cot_ref,
        pairing_ref, valid_ref, owner_ref, wscr, sems,
    ) = refs[8:]
    copies = [
        pltpu.make_async_copy(source, target, sems.at[i])
        for i, (source, target) in enumerate(
            [(pairing_hbm, pairing_ref), (valid_hbm, valid_ref), (owner_hbm, owner_ref)]
        )
    ]
    for copy in copies:
        copy.start()
    scene, tile = lax.axis_index("scene"), lax.axis_index("tile")
    branch, pair = scene % 2, scene // 2
    mats = tap_matrices(ws_ref[branch], 16, wscr)
    blocks = {}
    for rt in range(4):
        for ct in range(4):
            (pr, dr), (pc, dc) = TAP_LINES[rt], TAP_LINES[ct]
            blocks[pr * 2 + pc, shift_index(-dr, -dc)] = mats[rt * 4 + ct]
    zero = jnp.zeros((CH, CH), F32)
    for phase in range(4):
        row = [blocks.get((phase, s), zero) for s in range(9)]
        wf_ref[phase * CH : (phase + 1) * CH, :] = jnp.concatenate(row, axis=1).astype(BF16)
    give, keep = halves(wd_ref[branch].astype(F32), branch)
    mats = tap_matrices(jnp.concatenate([give, keep], axis=0), 9, wscr)[::-1]
    half = CH // 2
    wt_ref[...] = jnp.concatenate(
        [mat[:, h * half : (h + 1) * half] for h in range(2) for mat in mats], axis=1
    ).astype(BF16)
    slopes = []
    for pre_ref in pre_refs:
        pre = pre_ref[...]
        gate = 1.0 / (1.0 + jnp.exp(-pre))
        slopes.append(gate * (1.0 + pre * (1.0 - gate)))
    for copy in copies:
        copy.wait()
    total = pairing_ref.shape[0]
    matches = []
    for p in range(2):
        position = tile * 2 + p
        matched, inverse = pairing_ref[position, pair], jnp.int32(0)
        for i in range(total):
            inverse = inverse + jnp.where(pairing_ref[i, pair] == position, i, 0)
        matched = jnp.where(branch == 0, matched, inverse)
        matches.append(jnp.where(matched // 2 == tile, 0, 2) + matched % 2)
    swapped = matches[0] == 3
    slope_first[...] = jnp.where(swapped, slopes[1], slopes[0])
    slope_second[...] = jnp.where(swapped, slopes[0], slopes[1])
    for first, second, pairs in ((act_first, act_second, act_refs), (ph_first, ph_second, ph_refs)):
        first[...] = jnp.where(swapped, pairs[1][...], pairs[0][...])
        second[...] = jnp.where(swapped, pairs[0][...], pairs[1][...])
    rows = send_refs[0].shape[0] - 16
    cots = [ref[rows:, :].astype(F32) for ref in send_refs]
    cot_ref[0:16, :] = jnp.where(swapped, cots[1], cots[0])
    cot_ref[16:32, :] = jnp.where(swapped, cots[0], cots[1])
    row = lax.broadcasted_iota(jnp.int32, select_ref.shape, 0)
    select = jnp.zeros(select_ref.shape, F32)
    for p in range(2):
        position = jnp.where(swapped, 1 - p, p)
        live = jnp.where(tile * 2 + p < valid_ref[pair], 8 + position, -1)
        select = jnp.where((row == position * 4 + matches[p]) | (row == live), 1.0, select)
    select_ref[...] = jnp.where(row == jnp.where(swapped, 10, -1), 1.0, select)
    row = lax.broadcasted_iota(jnp.int32, place_ref.shape, 0)
    here = scene // 2 % 4
    place = jnp.zeros(place_ref.shape, F32)
    for k, source in enumerate((scene, scene ^ 1)):
        owner = owner_ref[source]
        target = owner // (2 * bias_rows)
        half = jnp.where(target // 8 == branch, 0, 1)
        wanted = k * 64 + ((target // 2 % 4) ^ here) * 16 + half * 8 + owner % (2 * bias_rows)
        place = jnp.where(row == jnp.where(target % 2 == branch, wanted, -1), 1.0, place)
    place_ref[...] = place


HALF = 9 * CH // 2


def shift_rows(pieces, reach, side, target):
    masks = shifted_masks(side, reach)
    rows = CH // 2
    for h, piece in enumerate(pieces):
        for s, (dr, dc) in enumerate(SHIFTS):
            at = h * HALF + s * rows
            target[at : at + rows, :] = shifted(piece, dr, dc, side, reach, masks)


def pick(position, candidates, select_ref, first=0):
    partner = None
    for k, payload in enumerate(candidates, first):
        term = payload * select_ref[position * 4 + k : position * 4 + k + 1, :].astype(BF16)
        partner = term if partner is None else partner + term
    return partner


def backward_patch(position, partner, select_ref, cot_ref, wt_ref, slope_ref, shift_scr):
    side = math.isqrt(slope_ref.shape[1])
    lanes = side * side // 128
    core = lax.axis_index("scene") % 2
    live = select_ref[8 + position : 9 + position, :]
    signal = (cot_ref[position * 16 : position * 16 + 16, :] + partner[lanes * CH :, :].astype(F32)) * live
    out_grad = jnp.concatenate(
        [signal[j : j + 1, :] * partner[j * CH : (j + 1) * CH, :].astype(F32) for j in range(lanes)], axis=1
    )
    shift_rows([piece.astype(BF16) for piece in halves(out_grad, core)], 2, side, shift_scr)
    return dot(wt_ref[...], shift_scr[...]) * slope_ref[...]


def backward_first_kernel(
    far0_ref, near_ref, select_ref, cot_ref, wt_ref, act_ref, slope_ref, ph_ref,
    pick_ref, pre_b_ref, bias_ref, dilated_ref, strided_ref, shift_scr,
):
    side = math.isqrt(slope_ref.shape[1])
    core = lax.axis_index("scene") % 2
    candidates = (near_ref[0], near_ref[1], far0_ref[...])
    pick_ref[...] = pick(1, candidates, select_ref)
    pre_grad = backward_patch(0, pick(0, candidates, select_ref), select_ref, cot_ref, wt_ref, slope_ref, shift_scr)
    act = act_ref[...]
    dilated_ref[...] = dot_nt(shift_scr[...], jnp.concatenate([act, act], axis=0))
    bias_ref[...] = jnp.broadcast_to(jnp.sum(pre_grad, axis=1, keepdims=True), bias_ref.shape)
    pre_b_ref[...] = pre_grad.astype(BF16)
    shift_rows([piece.astype(BF16) for piece in halves(pre_grad, core)], 1, side, shift_scr)
    strided_ref[...] = dot_nt(shift_scr[...], ph_ref[...])


def tap_blocks(strided, dilated):
    rows = CH // 2
    lower = lax.broadcasted_iota(jnp.int32, (rows, 2 * CH), 1) < CH

    def strided_piece(pr, shift):
        return strided[shift * rows : (shift + 1) * rows, pr * 2 * CH : (pr + 1) * 2 * CH]

    blocks = []
    for rt in range(4):
        pr, dr = TAP_LINES[rt]
        blocks.append(strided_piece(pr, shift_index(-dr, 0)))
        blocks.append(
            jnp.where(lower, strided_piece(pr, shift_index(-dr, -1)), strided_piece(pr, shift_index(-dr, 1)))
        )
    for j in range(5):
        low = dilated[(8 - 2 * j) * rows : (9 - 2 * j) * rows, :]
        high = dilated[(7 - 2 * j) * rows : (8 - 2 * j) * rows, :] if j < 4 else jnp.zeros_like(low)
        blocks.append(jnp.where(lower, low, high))
    return blocks


def write_blocks(blocks, bias_wide, ref, chunked):
    if not chunked:
        for i, block in enumerate(blocks):
            ref[i] = block
        return
    here = lax.axis_index("scene") // 2 % 4
    for m in range(4):
        pieces = [block[8 * m : 8 * m + 8] for block in blocks] + [bias_wide]
        ref[here ^ m] = jnp.concatenate(pieces, axis=0).astype(BF16)


def backward_second_kernel(
    far1_ref, pick_ref, select_ref, cot_ref, wt_ref, act_ref, slope_ref, ph_ref,
    other_bias_ref, other_dilated_ref, other_strided_ref,
    pre_b_ref, bias_ref, give_ref, out_shifts_ref, shift_scr, *, chunked,
):
    side = math.isqrt(slope_ref.shape[1])
    core = lax.axis_index("scene") % 2
    partner = pick_ref[...] + pick(1, (far1_ref[...],), select_ref, 3)
    pre_grad = backward_patch(1, partner, select_ref, cot_ref, wt_ref, slope_ref, out_shifts_ref)
    act = act_ref[...]
    dilated = dot_nt(out_shifts_ref[0:HALF, :], jnp.concatenate([act, act], axis=0))
    give, _ = halves(pre_grad, core)
    shift_rows([give.astype(BF16)], 1, side, shift_scr)
    strided = dot_nt(shift_scr[...], ph_ref[...])
    pre_b_ref[...] = pre_grad.astype(BF16)
    bias_wide = (jnp.sum(pre_grad, axis=1, keepdims=True) + other_bias_ref[...]).T[0:8, :]
    bias_wide = jnp.concatenate([bias_wide, jnp.zeros_like(bias_wide)], axis=1)
    bias_ref[...] = bias_wide
    blocks = tap_blocks(strided + other_strided_ref[0:HALF, :], dilated + other_dilated_ref[0:HALF, :])
    write_blocks(blocks, bias_wide, give_ref, chunked)


def backward_kept_kernel(
    select_ref, out_shifts_ref, pre_b_ref, other_ref, act_ref, ph_ref, other_dilated_ref, other_strided_ref,
    keep_ref, pre_b0_ref, pre_b1_ref, shift_scr, *, chunked,
):
    side = math.isqrt(act_ref.shape[1])
    act = act_ref[...]
    dilated = dot_nt(out_shifts_ref[HALF:, :], jnp.concatenate([act, act], axis=0))
    pre_b, other = pre_b_ref[...], other_ref[...]
    _, keep = halves(pre_b.astype(F32), lax.axis_index("scene") % 2)
    shift_rows([keep.astype(BF16)], 1, side, shift_scr)
    strided = dot_nt(shift_scr[...], ph_ref[...])
    blocks = tap_blocks(strided + other_strided_ref[HALF:, :], dilated + other_dilated_ref[HALF:, :])
    write_blocks(blocks, jnp.zeros((8, 2 * CH), F32), keep_ref, chunked)
    swapped = select_ref[10:11, 0:1].astype(BF16)
    straight = 1.0 - swapped
    pre_b0_ref[...] = other * straight + pre_b * swapped
    pre_b1_ref[...] = other * swapped + pre_b * straight


def spread_kernel(place_ref, bias_ref, keep_ref, got_ref, *out_refs):
    rows = keep_ref.shape[1]
    top = lax.broadcasted_iota(jnp.int32, (16, 128), 0) < 8
    mine = bias_ref[0:1, :]
    theirs = got_ref[0, rows - 16 :, :].astype(F32)[8:9, :]
    for d, out_ref in enumerate(out_refs):
        for half, ref in enumerate((keep_ref, got_ref)):
            at = d * 16 + half * 8
            bias = place_ref[at : at + 8, :] * mine + place_ref[64 + at : 72 + at, :] * theirs
            last = ref[d, rows - 16 :, :].astype(F32)
            last = jnp.where(top, last, jnp.concatenate([bias, bias], axis=0))
            out_ref[half * rows : (half + 1) * rows - 16, :] = ref[d, : rows - 16, :]
            out_ref[(half + 1) * rows - 16 : (half + 1) * rows, :] = last.astype(BF16)


def join_kernel(own_ref, a_ref, b_ref, c_ref, keep_ref, stay_ref, cross_ref):
    scene = lax.axis_index("scene")
    rows = keep_ref.shape[0]
    total = (own_ref[...].astype(F32) + a_ref[...].astype(F32)) + (
        b_ref[...].astype(F32) + c_ref[...].astype(F32)
    )
    mine, theirs = total[:rows, :], total[rows:, :]
    first = scene // 8 == scene % 2
    kept = jnp.where(first, mine, theirs)
    keep_ref[...] = kept
    stay_ref[...] = kept.astype(BF16)
    cross_ref[...] = jnp.where(first, theirs, mine).astype(BF16)


def finish_kernel(
    own_ref, a_ref, b_ref, c_ref, weights_hbm, bias_hbm,
    weights_ref, bias_ref, tap_scr, turn_scr, dilated_scr, sems, *, weight_scale, bias_scale,
):
    tile = lax.axis_index("tile")
    total = (own_ref[...] + a_ref[...].astype(F32)) + (b_ref[...].astype(F32) + c_ref[...].astype(F32))
    bias = total[(BLOCKS - 1) * 8 :, :] * bias_scale
    index = lax.broadcasted_iota(jnp.int32, bias.shape, 0)
    bias_ref[...] = jnp.sum(jnp.where(index == tile, bias, 0.0), axis=0, keepdims=True)[:, 0:CH]
    bias_out = pltpu.make_async_copy(bias_ref, bias_hbm, sems.at[0])
    bias_out.start()
    total = total * weight_scale
    other = pltpu.roll(total, CH, 1)
    for block in range(8):
        for half, source in enumerate((total, other)):
            tap = block // 2 * 4 + ((1, 2), (3, 0))[block % 2][half]
            tap_scr[pl.ds(tap, 8, stride=16), :] = source[block * 8 : block * 8 + 8, :]
    lines = tap_scr[0:128, :].T[0:CH, :].reshape(8, 8, 128)
    sub = lax.broadcasted_iota(jnp.int32, lines.shape, 1)
    chunk = lax.broadcasted_iota(jnp.int32, lines.shape, 2) // 16
    for step in (1, 2, 4):
        up = pltpu.roll(pltpu.roll(lines, 8 - step, 1), 16 * step, 2)
        down = pltpu.roll(pltpu.roll(lines, step, 1), 128 - 16 * step, 2)
        high, wide = sub // step % 2, chunk // step % 2
        lines = jnp.where(high == wide, lines, jnp.where(high == 0, up, down))
    for block in range(8):
        weights_ref[:, block * 128 : (block + 1) * 128] = lines[block]
    strided_part, dilated_part = pl.ds(0, 16 * CH), pl.ds(16 * CH, DIL_TAPS * CH)
    strided_out = pltpu.make_async_copy(weights_ref.at[:, strided_part], weights_hbm.at[:, strided_part], sems.at[1])
    strided_out.start()
    turn_scr[0:40, :] = total[64:104, :]
    turned = turn_scr[...].T
    for tap in range(DIL_TAPS):
        half = tap % 2
        dilated_scr[pl.ds(tap, CH, stride=DIL_TAPS), :] = turned[half * CH : (half + 1) * CH, :]
    spread = dilated_scr[0 : DIL_TAPS * CH, :].T
    tap = lax.broadcasted_iota(jnp.int32, (8, DIL_TAPS * CH), 1) % DIL_TAPS
    result = spread[0:8, :]
    for j in range(1, 5):
        result = jnp.where(tap // 2 == j, spread[8 * j : 8 * j + 8, :], result)
    weights_ref[:, 16 * CH :] = result
    dilated_out = pltpu.make_async_copy(weights_ref.at[:, dilated_part], weights_hbm.at[:, dilated_part], sems.at[2])
    dilated_out.start()
    for copy in (bias_out, strided_out, dilated_out):
        copy.wait()


def feature_patch(pre_b_ref, wf_ref, out_ref, shift_scr):
    side = math.isqrt(pre_b_ref.shape[1])
    near = shifted_masks(side, 1)
    merge = merge_matrix(side)
    run, wide = 16 * side, 4 * side
    pre_b = pre_b_ref[...]
    for s, (dr, dc) in enumerate(SHIFTS):
        shift_scr[s * CH : (s + 1) * CH, :] = shifted(pre_b, dr, dc, side, 1, near)
    phases = dot(wf_ref[...], shift_scr[...]).astype(BF16)
    runs = out_ref.shape[1] // run
    stacked = jnp.concatenate(
        [
            jnp.concatenate(
                [phases[k * CH : (k + 1) * CH, q * wide : (q + 1) * wide] for k in range(4)], axis=1
            )
            for q in range(runs)
        ],
        axis=0,
    )
    merged = dot(stacked, merge).astype(BF16)
    for q in range(runs):
        out_ref[:, q * run : (q + 1) * run] = merged[q * CH : (q + 1) * CH, :]


def feature_kernel(pre_b0_ref, pre_b1_ref, wf_ref, out_ref, shift_scr):
    for p, pre_b_ref in enumerate((pre_b0_ref, pre_b1_ref)):
        feature_patch(pre_b_ref, wf_ref, out_ref.at[p], shift_scr)


def store_kernel(features_ref, out_hbm, sem):
    copy = pltpu.make_async_copy(features_ref, out_hbm, sem)
    copy.start()
    copy.wait()


SPACES = {"s": pltpu.SMEM, "v": pltpu.VMEM, "h": pltpu.HBM, "a": pl.ANY}


def call(kernel, outs, ins, scratch, *args, flops=0, out_spaces="", aliases=None):
    args = [
        pltpu.with_memory_space_constraint(arg, pltpu.HBM) if space == "h" else arg
        for space, arg in zip(ins, args)
    ]
    return pl.pallas_call(
        kernel,
        out_shape=[jax.ShapeDtypeStruct(shape, kind) for shape, kind in outs],
        in_specs=[pl.BlockSpec(memory_space=SPACES[space]) for space in ins],
        out_specs=[pl.BlockSpec(memory_space=SPACES[space]) for space in out_spaces or "v" * len(outs)],
        scratch_shapes=[pltpu.VMEM(*item) if isinstance(item, tuple) else item for item in scratch],
        input_output_aliases=aliases or {},
        compiler_params=pltpu.CompilerParams(vmem_limit_bytes=VMEM_LIMIT),
        cost_estimate=pl.CostEstimate(flops=flops, bytes_accessed=1 << 20, transcendentals=0),
    )(*args)


def device_pairs(x, pairs):
    tiles = lax.axis_size("tile")
    flat = [(source[0] * tiles + source[1], target[0] * tiles + target[1]) for source, target in pairs]
    return lax.ppermute(x, ("scene", "tile"), flat)


def scene_xor(x, distance):
    return lax.ppermute(x, "scene", [(i, i ^ distance) for i in range(lax.axis_size("scene"))])


def device_xor(x, scene_distance, tile_distance):
    scenes, tiles = range(lax.axis_size("scene")), range(lax.axis_size("tile"))
    return device_pairs(
        x, [((s, t), (s ^ scene_distance, t ^ tile_distance)) for s in scenes for t in tiles]
    )


def join_halves(give, keep):
    parts = [half.reshape(BLOCKS - 1, -1, 8, half.shape[-1]) for half in (give, keep)]
    first = lax.axis_index("scene") % 2 == 0
    pair = jnp.stack([jnp.where(first, parts[1], parts[0]), jnp.where(first, parts[0], parts[1])], axis=2)
    return pair.reshape(BLOCKS - 1, -1, pair.shape[-1])


def reduce_anywhere(blocks, bias_row, tile_owner, bias_rows, weight_scale, bias_scale):
    channels = blocks.shape[1]
    scene = lax.axis_index("scene")
    scenes, tiles = lax.axis_size("scene"), lax.axis_size("tile")
    halves = blocks.reshape(BLOCKS - 1, channels, 2, channels)
    strided, dilated = [None] * 16, []
    for block in range(8):
        for half in range(2):
            strided[block // 2 * 4 + ((1, 2), (3, 0))[block % 2][half]] = halves[block, :, half]
    for tap in range(DIL_TAPS):
        dilated.append(halves[8 + tap // 2, :, tap % 2])
    row = jnp.concatenate(
        [
            jnp.stack(strided, axis=-1).reshape(channels, 16 * channels),
            jnp.stack(dilated, axis=-1).reshape(channels, DIL_TAPS * channels),
        ],
        axis=1,
    )
    hit = jnp.arange(2, dtype=jnp.int32)[:, None, None] == scene % 2
    term = jnp.where(hit, row[None] * weight_scale, 0.0).reshape(2 * channels, 25 * channels)
    weights = lax.psum(lax.psum_scatter(term, "scene", scatter_dimension=0, tiled=True), "tile")
    tile_id = lax.dynamic_index_in_dim(tile_owner, scene, 0, keepdims=False)
    owned = jnp.arange(scenes * tiles * bias_rows, dtype=jnp.int32) == tile_id
    bias = jnp.where(owned[:, None], bias_row[None, :channels] * bias_scale, 0.0)
    return weights, lax.psum_scatter(bias, ("scene", "tile"), scatter_dimension=0, tiled=True)


def local(
    features_in,
    strided_weights,
    dilated_weights,
    tile_bias,
    cost_cotangent,
    footprint_pairing,
    valid_counts,
    tile_owner,
):
    features, own_cot = features_in[0], cost_cotangent[0]
    patches, channels, cells_in = features.shape
    cells = own_cot.shape[1]
    scenes, tiles = lax.axis_size("scene"), lax.axis_size("tile")
    weight_scale = 1.0 / math.sqrt(scenes * patches * tiles * cells)
    bias_scale = 1.0 / math.sqrt(patches * tiles * cells)
    bias_rows = tile_bias.shape[0] // (scenes * tiles)
    grid = (channels, cells)
    payload = (cells * channels // 128 + 16, 128)
    chunked = scenes == 16 and tiles == 2 and patches == 2 and bias_rows == 1
    wscr = ((16 * channels + 16, 2 * channels), F32)
    im_scr = ((8 * channels, cells), BF16)
    patch_outs = [((4 * channels, cells), BF16), (grid, F32), (grid, BF16), (payload, BF16)]
    first_outs = patch_outs + [
        ((4 * channels, 4 * channels), BF16),
        ((3 * channels, 3 * channels), BF16),
        ((channels, 128), F32),
        (own_cot.shape, BF16),
        ((channels, cells_in), BF16),
    ]
    *part, w_strided, w_dilated, bias_col, cot, later = call(
        first_kernel,
        first_outs,
        "hhhhhh",
        [
            ((channels, cells_in), BF16),
            (strided_weights.shape[1:], BF16),
            (dilated_weights.shape[1:], BF16),
            (tile_bias.shape, F32),
            pltpu.SMEM(tile_owner.shape, jnp.int32),
            wscr,
            im_scr,
            pltpu.SemaphoreType.DMA((7,)),
        ],
        tile_owner, features, strided_weights, dilated_weights, tile_bias, own_cot,
        flops=10**9,
    )
    far = [device_xor(part[3], 1, 1)]
    *late, both = call(
        later_kernel,
        patch_outs + [((2,) + payload, BF16)],
        "vvvvvv",
        [im_scr],
        later, cot, w_strided, w_dilated, bias_col, part[3],
        flops=10**10,
    )
    far.append(device_xor(late[3], 1, 1))
    near = scene_xor(both, 1)
    phases, pre, act, send = zip(part, late)
    ordered = [(grid, F32)] * 2 + [(grid, BF16)] * 2 + [((4 * channels, cells), BF16)] * 2
    *both, w_feature, w_act, select, place, cots = call(
        functools.partial(prepare_kernel, bias_rows=bias_rows),
        ordered
        + [
            ((4 * channels, 9 * channels), BF16),
            ((channels, 9 * channels), BF16),
            ((16, 128), F32),
            ((128, 128), F32),
            ((32, 128), F32),
        ],
        "hhhvvvvvvvvvv",
        [
            pltpu.SMEM(footprint_pairing.shape[::-1], jnp.int32),
            pltpu.SMEM(valid_counts.shape, jnp.int32),
            pltpu.SMEM(tile_owner.shape, jnp.int32),
            wscr,
            pltpu.SemaphoreType.DMA((3,)),
        ],
        footprint_pairing.T, valid_counts, tile_owner, strided_weights, dilated_weights,
        *pre, *act, *phases, *send,
        flops=10**10,
    )
    slope, act, phases = both[0:2], both[2:4], both[4:6]
    shift_scr = ((9 * channels, cells), BF16)
    sums = [((9 * channels, 128), F32), ((9 * channels, 4 * channels), F32)]
    picked, *first = call(
        backward_first_kernel,
        [(payload, BF16), (grid, BF16), ((channels, 128), F32)] + sums,
        "v" * 8,
        [shift_scr],
        far[0], near, select, cots, w_act, act[0], slope[0], phases[0],
        flops=10**9,
    )
    half_shift = ((9 * channels // 2, cells), BF16)
    grads_shape = ((4, BLOCKS * 8, 128), BF16) if chunked else ((BLOCKS - 1, channels // 2, 128), F32)
    last, bias, give, out_shifts = call(
        functools.partial(backward_second_kernel, chunked=chunked),
        [(grid, BF16), ((8, 128), F32), grads_shape, shift_scr],
        "v" * 11,
        [half_shift],
        far[1], picked, select, cots, w_act, act[1], slope[1], phases[1], *first[1:],
        flops=10**9,
    )
    if chunked:
        got = scene_xor(give, 1)
    keep, *pre_b = call(
        functools.partial(backward_kept_kernel, chunked=chunked),
        [grads_shape] + [(grid, BF16)] * 2,
        "v" * 8,
        [half_shift],
        select, out_shifts, last, first[0], act[1], phases[1], *first[2:],
        flops=10**9,
    )
    wide_scr = ((9 * channels, cells), BF16)
    if chunked:
        stage = ((2 * BLOCKS * 8, 128), BF16)
        own, by_y, by_z, by_zy = call(spread_kernel, [stage] * 4, "vvvv", [], place, bias, keep, got)
        by_zy, by_z, by_y = scene_xor(by_zy, 6), scene_xor(by_z, 4), scene_xor(by_y, 2)
    (feature_grads,) = call(
        feature_kernel, [(features.shape, BF16)], "vvv", [wide_scr], *pre_b, w_feature, flops=10**9
    )
    chunk = (BLOCKS * 8, 128)
    if chunked:
        feature_grads, own = lax.optimization_barrier((feature_grads, own))
        kept, stay, cross = call(
            join_kernel, [(chunk, F32), (chunk, BF16), (chunk, BF16)], "vvvv", [], own, by_zy, by_z, by_y
        )
        by_zx, by_z, by_x = device_xor(cross, 8, 1), device_xor(cross, 8, 0), device_xor(stay, 0, 1)
    (feature_grads,) = call(
        store_kernel,
        [(features.shape, BF16)],
        "v",
        [pltpu.SemaphoreType.DMA],
        feature_grads,
        flops=10**9,
        out_spaces="h",
    )
    if not chunked:
        grad_weights, grad_bias = reduce_anywhere(
            join_halves(give, keep), bias[0], tile_owner, bias_rows, weight_scale, bias_scale
        )
        return (feature_grads[None], grad_weights, grad_bias)
    feature_grads, kept = lax.optimization_barrier((feature_grads, kept))
    grad_weights, grad_bias = call(
        functools.partial(finish_kernel, weight_scale=weight_scale, bias_scale=bias_scale),
        [((8, 25 * channels), F32), ((1, channels), F32)],
        "vvvv",
        [
            ((8, 25 * channels), F32),
            ((1, channels), F32),
            ((144, 128), F32),
            ((128, 128), F32),
            ((9 * channels + 16, 128), F32),
            pltpu.SemaphoreType.DMA((3,)),
        ],
        kept, by_zx, by_z, by_x,
        out_spaces="hh",
    )
    return (feature_grads[None], grad_weights, grad_bias)


def solution(mesh):
    return jax.shard_map(
        local,
        mesh=mesh,
        in_specs=(
            P("scene", "tile", None, None),
            P(),
            P(),
            P(),
            P("scene", "tile", None),
            P(),
            P(),
            P(),
        ),
        out_specs=(P("scene", "tile", None, None), P("scene", None), P(("scene", "tile"), None)),
        check_vma=False,
    )
```
